32 devices in a mesh: grp: 2 (over x), seq: 8 (over z, y), head: 2 (over core).
Axes of the slice: x: 2, y: 2, z: 4, core: 2. Of those that a mesh axis runs over, the one named last changes fastest.
Arguments:
- q_feat: bfloat16 [8192, 256], P(('grp', 'seq'), 'head'), parts along dimension 0, may hold values from -5 to 5
- k_feat: bfloat16 [8192, 256], P(('grp', 'seq'), 'head'), parts along dimension 0, may hold values from -5 to 5
- values: bfloat16 [8192, 2048], P(('grp', 'seq'), 'head'), parts along dimension 0, may hold values from -8 to 8
- win_query: bfloat16 [8192, 2048], P(('grp', 'seq'), 'head'), parts along dimension 0, may hold values from -20 to 20
- win_key: bfloat16 [8192, 2048], P(('grp', 'seq'), 'head'), parts along dimension 0, may hold values from -5 to 5
- log_gates: float32 [8192, 16], P(('grp', 'seq'), 'head'), parts along dimension 0, may hold values from -2.2 to 0
- conv_weight: float32 [3, 2048], P(None, 'head'), may hold values from -2.5 to 2.5
Outputs:
- mixed: bfloat16 [8192, 2048], P(('grp', 'seq'), 'head'), parts along dimension 0
The draws below stay inside these ranges and needn't reach their ends.
There are 2 independent parts, one for each index of `grp`. The reference program is written for one: setup_inputs(seed, part) draws one part's arguments, and reference() takes and returns one part's arrays. A program takes and returns all parts, laid end to end along the dimension named above; an argument that names none is the same for every part. Nothing has to cross between parts.
All inputs are finite; a program needn't handle non-finite values.
Results may differ from the reference program's by a relative error of at most 0.011.
Values may be sent and summed in bfloat16 or wider, within the bound.
No kernel may reach another device: no remote copies, remote signals or barrier semaphores. Data moves between devices by JAX's collectives and lax.ppermute only.
A program may use at most 192 MiB of HBM per device.

```python
import math
import jax
import jax.numpy as jnp
from jax import lax

HEADS = 16
HEAD_DIM = 128
FEAT_DIM = 16
FEATURES = 273
WINDOW = 64
CONV = 3
BLOCK = 512
TOK_DEV = 512
DOCUMENT_TOKENS = 4096


def draw_win_key(key, part):
    shape = (DOCUMENT_TOKENS, HEADS * HEAD_DIM)
    drawn = jnp.clip(jax.random.normal(jax.random.fold_in(key, 11), shape, jnp.float32), -5.0, 5.0)
    return drawn.astype(jnp.bfloat16)


def draw_win_query(key, part):
    shape = (DOCUMENT_TOKENS, HEADS * HEAD_DIM)
    drawn = jnp.clip(jax.random.normal(jax.random.fold_in(key, 13), shape, jnp.float32), -5.0, 5.0)
    return drawn.astype(jnp.bfloat16)


def draw_k_feat(key, part):
    shape = (DOCUMENT_TOKENS, HEADS * FEAT_DIM)
    pieces = DOCUMENT_TOKENS // TOK_DEV
    phase = jax.random.randint(jax.random.fold_in(key, 41), (HEADS,), 0, 2)
    piece_index = jnp.arange(pieces)
    loud = (piece_index[:, None] + phase[None, :]) % 2 == 0
    level = jnp.where(loud, 2.5, 0.25).astype(jnp.float32)
    level = jnp.repeat(jnp.repeat(level, FEAT_DIM, axis=1), TOK_DEV, axis=0)
    noise = jax.random.normal(jax.random.fold_in(key, 42), shape, jnp.float32)
    return jnp.clip(noise * level, -5.0, 5.0).astype(jnp.bfloat16)


def draw_values(key, part):
    shape = (DOCUMENT_TOKENS, HEADS * HEAD_DIM)
    drawn = 2.0 * jax.random.normal(jax.random.fold_in(key, 21), shape, jnp.float32)
    return jnp.clip(drawn, -8.0, 8.0).astype(jnp.bfloat16)


def head_classes(key):
    order = jax.random.permutation(jax.random.fold_in(key, 31), HEADS)
    count = max(1, HEADS // 4)
    fast = order < count
    medium = (order >= count) & (order < 2 * count)
    return (fast, medium)


def draw_log_gates(key, part):
    fast, medium = head_classes(key)
    pieces = DOCUMENT_TOKENS // TOK_DEV
    slow_rate = jnp.exp(jax.random.uniform(jax.random.fold_in(key, 32), (HEADS,), jnp.float32, math.log(0.02), math.log(0.11))) / DOCUMENT_TOKENS
    fast_rate = 1.0 / jnp.exp(jax.random.uniform(jax.random.fold_in(key, 33), (HEADS,), jnp.float32, math.log(30.0), math.log(50.0)))
    medium_total = jnp.exp(jax.random.uniform(jax.random.fold_in(key, 38), (HEADS,), jnp.float32, math.log(4.65), math.log(5.0)))
    multiplier = jnp.exp(jax.random.uniform(jax.random.fold_in(key, 34), (pieces, HEADS), jnp.float32, -0.7, 0.7))
    medium_factor = jnp.exp(jax.random.uniform(jax.random.fold_in(key, 37), (pieces, HEADS), jnp.float32, 0.0, math.log(2.0)))
    drawn_rate = jnp.where(fast, fast_rate, slow_rate)[None, :] * multiplier
    medium_rate = medium_total[None, :] * medium_factor / TOK_DEV
    piece_rate = jnp.where(medium[None, :], medium_rate, drawn_rate)
    rates = jnp.repeat(piece_rate, TOK_DEV, axis=0)
    spike_location = jax.random.randint(jax.random.fold_in(key, 35), (3,), 0, DOCUMENT_TOKENS)
    spike_retained = jax.random.uniform(jax.random.fold_in(key, 36), (3,), jnp.float32, 0.5, 0.8)
    token_positions = jnp.arange(DOCUMENT_TOKENS)[:, None]
    spikes_list = jnp.sum(jnp.where(token_positions == spike_location[None, :], jnp.log(spike_retained)[None, :], 0.0), axis=1, keepdims=True)
    return (-rates + spikes_list).astype(jnp.float32)


def block_levels(key, dims, cuts, low, high):
    def one(dim, blocks):
        steps = jax.random.uniform(jax.random.fold_in(jax.random.fold_in(key, 6), dim), (blocks,), jnp.float32, low / len(cuts), high / len(cuts))
        return jnp.repeat(jnp.exp(steps), dims[dim] // blocks).reshape((-1,) + (1,) * (len(dims) - dim - 1))

    gain = one(*cuts[0])
    for cut in cuts[1:]:
        gain = gain * one(*cut)
    return gain


def normal_values(key, shape, scale, most, cuts=(), kind=jnp.bfloat16):
    entries = jax.random.normal(key, shape, jnp.float32) * scale
    if len(cuts) > 0:
        entries = block_levels(key, shape, cuts, -0.22, 0.18) * entries
    return jnp.clip(entries, min=-most, max=most).astype(kind)


def setup_inputs(seed: int = 0, part: int = 0) -> dict:
    seeds = jax.random.split(jax.random.key(seed), 8)
    part_splits = jax.random.split(jax.random.fold_in(seeds[7], part), 8)
    return {
        "q_feat": normal_values(part_splits[0], (DOCUMENT_TOKENS, HEADS * FEAT_DIM), 2.0, 5.0, ((0, 8), (1, 2))),
        "k_feat": draw_k_feat(jax.random.fold_in(jax.random.fold_in(seeds[7], part), 71), part),
        "values": draw_values(jax.random.fold_in(jax.random.fold_in(seeds[7], part), 71), part),
        "win_query": draw_win_query(jax.random.fold_in(jax.random.fold_in(seeds[7], part), 71), part),
        "win_key": draw_win_key(jax.random.fold_in(jax.random.fold_in(seeds[7], part), 71), part),
        "log_gates": draw_log_gates(jax.random.fold_in(jax.random.fold_in(seeds[7], part), 71), part),
        "conv_weight": normal_values(seeds[6], (CONV, HEADS * HEAD_DIM), 0.6, 2.5, ((1, 2),), jnp.float32),
    }


def taylor_map(features, heads):
    tok_rows = features.shape[0]
    width = features.shape[1] // heads
    spread = features.astype(jnp.float32).reshape(tok_rows, heads, width)
    linear = spread * width ** -0.25
    square = (spread[:, :, :, None] * spread[:, :, None, :]).reshape(tok_rows, heads, width * width) * (2.0 * width) ** -0.5
    ones = jnp.ones((tok_rows, heads, 1), jnp.float32)
    return jnp.concatenate([ones, linear, square], axis=2).astype(jnp.bfloat16)


def reference(q_feat, k_feat, values, win_query, win_key, log_gates, conv_weight):
    maximum_level = lax.Precision.HIGHEST
    count = DOCUMENT_TOKENS // BLOCK
    channels = HEADS * HEAD_DIM

    def split(array):
        return array.reshape((count, BLOCK) + array.shape[1:])

    block_inputs = (split(q_feat), split(k_feat), split(values), split(win_query), split(win_key), split(log_gates), jnp.arange(count, dtype=jnp.int32))
    start_carry = (jnp.zeros((HEADS, FEATURES, HEAD_DIM), jnp.float32), jnp.zeros((HEADS, FEATURES), jnp.float32),
                   jnp.zeros((WINDOW, channels), jnp.bfloat16), jnp.zeros((WINDOW, channels), jnp.bfloat16))
    causal = jnp.arange(BLOCK)[:, None] >= jnp.arange(BLOCK)[None, :]
    query_pos = jnp.arange(BLOCK)[:, None]
    key_pos = jnp.arange(BLOCK + WINDOW)[None, :] - WINDOW

    def advance(carry, inputs):
        running_state, norm_total, prev_key, prev_value = carry
        query_block, key_block, value_block, wq_block, wk_block, gate_block, index = inputs
        value_ext = jnp.concatenate([prev_value, value_block], axis=0)
        key_ext = jnp.concatenate([prev_key, wk_block], axis=0)
        convolved = jnp.zeros((BLOCK, channels), jnp.float32)
        for tap in range(CONV):
            convolved = convolved + conv_weight[tap][None, :] * value_ext[WINDOW - tap: WINDOW - tap + BLOCK].astype(jnp.float32)
        filtered_values = convolved.astype(jnp.bfloat16).reshape(BLOCK, HEADS, HEAD_DIM).astype(jnp.float32)
        query_features = taylor_map(query_block, HEADS).astype(jnp.float32)
        key_features = taylor_map(key_block, HEADS).astype(jnp.float32)
        cumulative = jnp.cumsum(gate_block, axis=0)
        cum_heads = cumulative.T
        decay_factor = jnp.exp(jnp.where(causal[None], cum_heads[:, :, None] - cum_heads[:, None, :], -jnp.inf))
        score_matrix = jnp.einsum("sjz,djz->jsd", query_features, key_features, precision=maximum_level) * decay_factor
        denominator = jnp.sum(score_matrix, axis=2).T
        numerator = jnp.einsum("hqk,khd->qhd", score_matrix.astype(jnp.bfloat16).astype(jnp.float32), filtered_values, precision=maximum_level)
        entering = jnp.exp(cumulative)
        numerator = numerator + entering[:, :, None] * jnp.einsum("qhf,hfd->qhd", query_features, running_state, precision=maximum_level)
        denominator = denominator + entering * jnp.einsum("qhf,hf->qh", query_features, norm_total, precision=maximum_level)
        linear = numerator / denominator[:, :, None]
        block_finish = cumulative[-1]
        retention = jnp.exp(block_finish[None, :] - cumulative)
        key_expanded = key_features * retention[:, :, None]
        running_state = jnp.exp(block_finish)[:, None, None] * running_state + jnp.einsum("mwv,mwr->wvr", key_expanded, filtered_values, precision=maximum_level)
        norm_total = jnp.exp(block_finish)[:, None] * norm_total + jnp.sum(key_expanded, axis=0)
        win_keys = key_ext.reshape(BLOCK + WINDOW, HEADS, HEAD_DIM).astype(jnp.float32)
        win_values = value_ext.reshape(BLOCK + WINDOW, HEADS, HEAD_DIM).astype(jnp.float32)
        win_queries = wq_block.reshape(BLOCK, HEADS, HEAD_DIM).astype(jnp.float32)
        win_scores = jnp.einsum("qhd,khd->hqk", win_queries, win_keys, precision=maximum_level) * HEAD_DIM ** -0.5
        valid = (key_pos <= query_pos) & (key_pos > query_pos - WINDOW) & (index * BLOCK + key_pos >= 0)
        win_scores = jnp.where(valid[None], win_scores, -jnp.inf)
        top = jnp.max(win_scores, axis=2, keepdims=True)
        weights = jnp.exp(win_scores - top)
        total = jnp.sum(weights, axis=2, keepdims=True)
        probs = (weights / total).astype(jnp.bfloat16).astype(jnp.float32)
        window_out = jnp.einsum("hqk,khd->qhd", probs, win_values, precision=maximum_level)
        mixed = (linear + window_out).astype(jnp.bfloat16).reshape(BLOCK, channels)
        return (running_state, norm_total, wk_block[BLOCK - WINDOW:], value_block[BLOCK - WINDOW:]), mixed

    final_carry, outputs = lax.scan(advance, start_carry, block_inputs)
    return outputs.reshape(DOCUMENT_TOKENS, channels)
```

```python
import numpy as np
import jax
import jax.numpy as jnp
from jax import lax
from jax.experimental import pallas as pl
from jax.experimental.pallas import tpu as pltpu
from jax.sharding import PartitionSpec as P

WINDOW = 64
ROWS = 160
MISC = 157
LOG2E = float(np.log2(np.e))
F32 = jnp.float32
BF16 = jnp.bfloat16
VMEM_LIMIT = 48 * 1024 * 1024


def feature_tables(width):
    first = -np.ones(ROWS, np.int32)
    second = -np.ones(ROWS, np.int32)
    scale = np.zeros(ROWS, np.float32)
    twice = np.ones(ROWS, np.float32)
    scale[0] = 1.0
    at = 1
    for i in range(width):
        first[at], scale[at] = i, width ** (-0.25)
        at += 1
    for i in range(width):
        for j in range(i, width):
            first[at], second[at], scale[at] = i, j, (2.0 * width) ** (-0.5)
            twice[at] = 1.0 if i == j else 2.0
            at += 1
    one_a = ((first < 0) & (scale > 0)).astype(np.float32)
    one_b = ((second < 0) & (scale > 0)).astype(np.float32)
    return first, second, one_a, one_b, scale, twice


def key_tables(width):
    first, second, one_a, one_b, scale, _ = feature_tables(width)
    lanes = lambda column: np.repeat(column[:, None], 128, axis=1)
    index = np.stack([lanes(np.where(first < 0, -1000, first)), lanes(np.where(second < 0, -1000, second))])
    real = np.stack([lanes(one_a), lanes(one_b), lanes(scale)])
    return jnp.asarray(index, jnp.int32), jnp.asarray(real, F32)


def query_tables(width):
    first, second, one_a, one_b, scale, twice = feature_tables(width)

    def row(values, fill):
        wide = np.full((1, 256), fill, np.float32)
        wide[0, :ROWS] = values
        return wide

    index = np.concatenate(
        [row(np.where(first < 0, -1000, first), -1000), row(np.where(second < 0, -1000, second), -1000)]
        + [np.full((6, 256), -1000, np.float32)]
    )
    real = np.concatenate([row(one_a, 0), row(one_b, 0), row(scale * twice, 0), np.zeros((5, 256), np.float32)])
    return jnp.asarray(index, jnp.int32), jnp.asarray(real, F32)


def nt(a, b):
    return lax.dot_general(a, b, (((1,), (1,)), ((), ())), preferred_element_type=F32)


def nn(a, b):
    return lax.dot_general(a, b, (((1,), (0,)), ((), ())), preferred_element_type=F32)


def tn(a, b):
    return lax.dot_general(a, b, (((0,), (0,)), ((), ())), preferred_element_type=F32)


def parts(wide):
    upper = wide.astype(BF16)
    rest = wide - upper.astype(F32)
    middle = rest.astype(BF16)
    lower = (rest - middle.astype(F32)).astype(BF16)
    return upper, middle, lower


def iota(shape, dim):
    return lax.broadcasted_iota(jnp.int32, shape, dim)


def cumulative_rows(gates):
    rows = gates.shape[0]
    upto = (iota((rows, rows), 0) <= iota((rows, rows), 1)).astype(BF16)
    return sum(tn(piece, upto) for piece in parts(gates))


def cumulative_columns(gates):
    rows = gates.shape[0]
    upto = (iota((rows, rows), 1) <= iota((rows, rows), 0)).astype(BF16)
    return sum(nn(upto, piece) for piece in parts(gates))


def tile4(table, count):
    return jnp.concatenate([table] * count, axis=1)


def shifted(x, by):
    return jnp.where(iota(x.shape, 0) < by, 0.0, pltpu.roll(x, by, 0))


def state_kernel(order, quarter_heads, group_ref, k_ref, v_ref, g_ref, w_ref, index_ref, real_ref, *refs):
    outs, (cum_ref, norm_ref) = refs[: len(order)], refs[len(order) :]
    rows, wide = k_ref.shape
    heads = g_ref.shape[1]
    width = wide // heads
    k = k_ref[...]
    cum_ref[...] = cumulative_rows(g_ref[...])
    norm_ref[...] = jnp.zeros(norm_ref.shape, F32)
    lane = iota((ROWS, wide), 1)
    lane1 = iota((1, 128), 1)
    sub = iota((8, 128), 0)
    one_a, one_b, scale = (tile4(real_ref[i], rows // 128) for i in range(3))
    keys8 = k[0:16].astype(F32)[0:8]
    for out_ref, distance in zip(outs, order):
        quarter = group_ref[0] ^ distance
        for j in range(quarter_heads):
            head = quarter * quarter_heads + j
            at = pl.ds(pl.multiple_of(head * 128, 128), 128)
            pick_a = (lane == index_ref[0] + head * width).astype(BF16)
            pick_b = (lane == index_ref[1] + head * width).astype(BF16)
            cum = cum_ref[pl.ds(head, 1), :]
            last = cum[:, rows - 1 :]
            keep = jnp.exp(last - cum)
            phi = (((nt(pick_a, k) + one_a) * (nt(pick_b, k) + one_b) * scale) * keep).astype(BF16)
            v = v_ref[:, at].astype(F32)
            w = w_ref[:, at]
            conv = (w[0:1] * v + w[1:2] * shifted(v, 1) + w[2:3] * shifted(v, 2)).astype(BF16)
            state = nn(phi, conv)
            norm_ref[:, 0:ROWS] = nt(jnp.ones((8, rows), BF16), phi)
            norm = norm_ref[0:1, :]
            high = norm.astype(BF16).astype(F32)
            low = norm - high
            turned = pltpu.roll(keys8, (wide - head * width) % wide, 1)
            turned2 = pltpu.roll(keys8, (wide - head * width + width) % wide, 1)
            misc = jnp.where(lane1 < width, turned[0:1], 0.0)
            misc = jnp.where((lane1 >= width) & (lane1 < 2 * width), turned2[1:2], misc)
            place = 2 * width
            for value in (keep[:, 0:1], keep[:, 1:2], jnp.exp(last)):
                for piece in parts(value):
                    misc = jnp.where(lane1 == place, piece.astype(F32), misc)
                    place += 1
            tail = state[ROWS - 8 :]
            for row, line in enumerate((high[:, :128], high[:, 128:], low[:, :128], low[:, 128:], misc)):
                tail = jnp.where(sub == row + 1, line, tail)
            tail = jnp.where(sub >= 6, v[rows - 8 :], tail)
            out_ref[j, 0 : ROWS - 16, :] = state[: ROWS - 16].astype(BF16)
            out_ref[j, ROWS - 16 :, :] = jnp.concatenate([state[ROWS - 16 : ROWS - 8], tail]).astype(BF16)


class Element:
    def __init__(self, tile, width):
        self.tile = tile
        self.width = width
        tail = tile[ROWS - 8 :]
        misc = tail[5:6]
        lane1 = iota((1, 128), 1)
        place = 2 * width

        def value(i):
            here = (lane1 >= place + 3 * i) & (lane1 < place + 3 * i + 3)
            return jnp.sum(jnp.where(here, misc, 0.0), axis=1, keepdims=True)

        self.misc = misc
        self.enter = (value(0), value(1))
        self.decay = value(2)
        self.last = (tail[6:7], tail[7:8])


def first_keys(miscs, index_ref, real_ref, width):
    lane = iota((ROWS, 128), 1)
    rows = jnp.concatenate(miscs + [jnp.zeros((8 - len(miscs), 128), F32)] if len(miscs) < 8 else miscs).astype(BF16)
    one_a, one_b, scale = (real_ref[i][:, 0:8] for i in range(3))
    found = []
    for token in range(2):
        pick_a = (lane == index_ref[0] + token * width).astype(BF16)
        pick_b = (lane == index_ref[1] + token * width).astype(BF16)
        found.append((nt(pick_a, rows) + one_a) * (nt(pick_b, rows) + one_b) * scale)
    return found


def merge(left, right, columns, w):
    before, last = left.last
    carry0 = w[1:2] * last + w[2:3] * before
    carry1 = w[2:3] * last
    enter0, enter1 = right.enter
    joined = right.decay * left.tile + right.tile
    joined = joined + columns[0] * (enter0 * carry0) + columns[1] * (enter1 * carry1)
    sub = iota((8, 128), 0)
    lane1 = iota((1, 128), 1)
    misc = jnp.where(lane1 < 2 * left.width, left.misc, left.misc * right.decay)
    tail = jnp.where(sub == 5, misc, joined[ROWS - 8 :])
    tail = jnp.where(sub >= 6, right.tile[ROWS - 8 :], tail)
    return Element(jnp.concatenate([joined[: ROWS - 8], tail]), left.width)


def packed(tile, width):
    tail = tile[ROWS - 8 :]
    sub = iota((8, 128), 0)
    lane1 = iota((1, 128), 1)
    for row in (1, 2):
        norm = tail[row : row + 1] + tail[row + 2 : row + 3]
        high = norm.astype(BF16).astype(F32)
        tail = jnp.where(sub == row, high, jnp.where(sub == row + 2, norm - high, tail))
    misc = tail[5:6]
    place = 2 * width
    fresh = jnp.where(lane1 < place, misc, 0.0)
    for i in range(3):
        here = (lane1 >= place) & (lane1 < place + 3)
        value = jnp.sum(jnp.where(here, misc, 0.0), axis=1, keepdims=True)
        for piece in parts(value):
            fresh = jnp.where(lane1 == place, piece.astype(F32), fresh)
            place += 1
    tail = jnp.where(sub == 5, fresh, tail)
    return jnp.concatenate([tile[: ROWS - 8], tail]).astype(BF16)


def group_kernel(width, group_ref, w_ref, index_ref, real_ref, x0, x1, x2, x3, total_ref, before_ref, held):
    group = group_ref[0]
    count = x0.shape[0]
    for distance, ref in enumerate((x0, x1, x2, x3)):
        held[group ^ distance] = ref[...]
    elements = [[Element(held[p, j].astype(F32), width) for j in range(count)] for p in range(4)]
    columns = first_keys([elements[p][j].misc for p in range(4) for j in range(count)], index_ref, real_ref, width)
    for j in range(count):
        w = w_ref[:, pl.ds(pl.multiple_of((group * count + j) * 128, 128), 128)]
        so_far = elements[0][j]
        for p in range(1, 4):
            before_ref[p - 1, j] = so_far.tile
            pick = p * count + j
            so_far = merge(so_far, elements[p][j], [c[:, pick : pick + 1] for c in columns], w)
        total_ref[j] = packed(so_far.tile, width)


def pair_kernel(width, group_ref, w_ref, index_ref, real_ref, left_ref, right_ref, out_ref):
    count = left_ref.shape[0]
    group = group_ref[0]
    rights = [Element(right_ref[j].astype(F32), width) for j in range(count)]
    columns = first_keys([right.misc for right in rights], index_ref, real_ref, width)
    for j in range(count):
        w = w_ref[:, pl.ds(pl.multiple_of((group * count + j) * 128, 128), 128)]
        left = Element(left_ref[j].astype(F32), width)
        out_ref[j] = packed(merge(left, rights[j], [c[:, j : j + 1] for c in columns], w).tile, width)


def spread_kernel(width, group_ref, w_ref, index_ref, real_ref, base_ref, before_ref, o0, o1, o2, o3, held):
    group = group_ref[0]
    live = group_ref[1] > 0
    count = base_ref.shape[0]
    for j in range(count):
        w = w_ref[:, pl.ds(pl.multiple_of((group * count + j) * 128, 128), 128)]
        base = Element(jnp.where(live, base_ref[j].astype(F32), 0.0), width)
        held[0, j] = base.tile.astype(BF16)
        rights = [Element(before_ref[p, j], width) for p in range(3)]
        columns = first_keys([right.misc for right in rights], index_ref, real_ref, width)
        for p in range(3):
            held[p + 1, j] = packed(merge(base, rights[p], [c[:, p : p + 1] for c in columns], w).tile, width)
    for distance, ref in enumerate((o0, o1, o2, o3)):
        ref[...] = held[group ^ distance]


def block_kernel(edge_ref, q_ref, k_ref, v_ref, wq_ref, wk_ref, g_ref, w_ref, pk_ref, pv_ref, num_ref, den_ref, win_ref):
    rows, wide = q_ref.shape
    heads = g_ref.shape[1]
    width = wide // heads
    q = q_ref[...]
    k = k_ref[...]
    gates = g_ref[...]
    cum_row = cumulative_rows(gates) * LOG2E
    cum_col = cumulative_columns(gates) * LOG2E
    lane = iota(k.shape, 1)
    step = 128
    ones = jnp.ones((rows, 128), BF16)
    causal = iota((step, step), 0) >= iota((step, step), 1)
    half = WINDOW
    seen = iota((half, 2 * half), 1)
    mine = iota((half, 2 * half), 0)
    valid = (seen > mine) & (seen <= mine + half)
    first_valid = valid & ((seen >= half) | (edge_ref[0] > 0))
    for h in range(heads):
        at = slice(128 * h, 128 * h + 128)
        k_here = jnp.where((lane >= h * width) & (lane < (h + 1) * width), k, jnp.zeros_like(k)) * BF16(0.25)
        v = v_ref[:, at]
        prev = pv_ref[:, at]
        v32 = v.astype(F32)
        ahead = jnp.concatenate([prev[WINDOW - 16 :].astype(F32)[8:], v32])
        w = w_ref[:, at]
        conv = w[0:1] * v32 + w[1:2] * pltpu.roll(ahead, 1, 0)[8:] + w[2:3] * pltpu.roll(ahead, 2, 0)[8:]
        right = jnp.concatenate([conv.astype(BF16), ones], axis=1)
        for i in range(rows // step):
            here = slice(i * step, (i + 1) * step)
            upto = (i + 1) * step
            x = nt(q[here], k_here[:upto])
            diff = cum_col[here, h : h + 1] - cum_row[h : h + 1, :upto]
            if i:
                masked = jnp.where(causal, diff[:, i * step :], -jnp.inf)
                diff = jnp.concatenate([diff[:, : i * step], masked], axis=1)
            else:
                diff = jnp.where(causal, diff, -jnp.inf)
            score = ((0.5 * x + 1.0) * x + 1.0) * jnp.exp2(diff)
            both = nn(score.astype(BF16), right[:upto])
            num_ref[here, at] = both[:, :128]
            den_ref[here, at] = both[:, 128:]
        keys = jnp.concatenate([pk_ref[:, at], wk_ref[:, at]])
        vals = jnp.concatenate([jnp.concatenate([prev, v]), jnp.ones((rows + WINDOW, 128), BF16)], axis=1)
        for i in range(rows // half):
            here = slice(i * half, (i + 1) * half)
            span = slice(i * half, (i + 2) * half)
            s = nt(wq_ref[here, at], keys[span]) * (128 ** (-0.5) * LOG2E)
            s = jnp.where(first_valid if i == 0 else valid, s, -jnp.inf)
            p = jnp.exp2(s - jnp.max(s, axis=1, keepdims=True)).astype(BF16)
            both = nn(p, vals[span])
            win_ref[here, at] = both[:, :128] / both[:, 128:]


def finish_kernel(group_ref, q_ref, g_ref, index_ref, real_ref, x0, x1, x2, x3, num_ref, den_ref, win_ref, out_ref, held):
    group = group_ref[0]
    rows, wide = q_ref.shape
    heads = g_ref.shape[1]
    width = wide // heads
    count = x0.shape[0]
    for distance, ref in enumerate((x0, x1, x2, x3)):
        held[group ^ distance] = ref[...]
    q = q_ref[...]
    enter = jnp.exp(cumulative_columns(g_ref[...]))
    row = iota((wide, 256), 0)
    one_a, one_b, scale = (real_ref[i : i + 1] for i in range(3))
    for h in range(heads):
        at = slice(128 * h, 128 * h + 128)
        pick_a = (row == index_ref[0:1] + h * width).astype(BF16)
        pick_b = (row == index_ref[1:2] + h * width).astype(BF16)
        phi = ((nn(q, pick_a) + one_a) * (nn(q, pick_b) + one_b) * scale).astype(BF16)
        tile = held[h // count, h % count]
        tail = tile[ROWS - 16 :].astype(F32)[8:]
        high = jnp.concatenate([tail[1:2], tail[2:3]], axis=1)
        low = jnp.concatenate([tail[3:4], tail[4:5]], axis=1)
        norm = nt(phi, jnp.broadcast_to(high, (128, 256)).astype(BF16)) + nt(
            phi, jnp.broadcast_to(low, (128, 256)).astype(BF16)
        )
        add = nn(phi[:, :ROWS], tile)
        e = enter[:, h : h + 1]
        num = num_ref[:, at] + e * add
        den = den_ref[:, at] + e * norm
        out_ref[:, at] = (num / den + win_ref[:, at]).astype(BF16)


def call(kernel, inputs, outs, scratch=(), smem=(0,)):
    where = [pl.BlockSpec(memory_space=pltpu.SMEM if i in smem else pltpu.VMEM) for i in range(len(inputs))]
    return pl.pallas_call(
        kernel,
        out_shape=outs,
        in_specs=where,
        out_specs=jax.tree.map(lambda _: pl.BlockSpec(memory_space=pltpu.VMEM), outs),
        scratch_shapes=scratch,
        compiler_params=pltpu.CompilerParams(vmem_limit_bytes=VMEM_LIMIT),
    )(*inputs)


def local(count, q_feat, k_feat, values, win_query, win_key, log_gates, conv_weight):
    rows = values.shape[0]
    heads = log_gates.shape[1]
    width = q_feat.shape[1] // heads
    quarter = heads // 4
    position = lax.axis_index("seq")
    group = (position % 4).astype(jnp.int32)
    one = lambda *numbers: jnp.stack([jnp.asarray(n, jnp.int32) for n in numbers])
    k_index, k_real = key_tables(width)
    q_index, q_real = query_tables(width)

    def swap(x, distance):
        return lax.ppermute(x, "seq", [(i, i ^ distance) for i in range(count)])

    def states(order):
        shape = jax.ShapeDtypeStruct((quarter, ROWS, 128), BF16)
        return call(
            lambda *refs: state_kernel(order, quarter, *refs),
            (one(group), k_feat, values, log_gates, conv_weight, k_index, k_real),
            [shape] * len(order),
            [pltpu.VMEM((heads, rows), F32), pltpu.VMEM((8, 256), F32)],
        )

    sent = states((1, 2, 3))
    (own,) = states((0,))
    others = [swap(x, d) for d, x in zip((1, 2, 3), sent)]
    shape = jax.ShapeDtypeStruct((quarter, ROWS, 128), BF16)
    total, before = call(
        lambda *refs: group_kernel(width, *refs),
        (one(group), conv_weight, k_index, k_real, own, *others),
        [shape, jax.ShapeDtypeStruct((3, quarter, ROWS, 128), F32)],
        [pltpu.VMEM((4, quarter, ROWS, 128), BF16)],
    )
    base = jnp.zeros_like(total)
    live = position < 0
    distance = 4
    while distance < count:
        got = swap(total, distance)
        upper = (position & distance) > 0
        if distance == 4:
            base = got
            live = upper
        else:
            pair = lambda left, right: call(
                lambda *refs: pair_kernel(width, *refs), (one(group), conv_weight, k_index, k_real, left, right), shape
            )
            base = jnp.where(upper, jnp.where(live, pair(got, base), got), base)
            live = live | upper
        if 2 * distance < count:
            lower_half = jnp.where(upper, got, total)
            upper_half = jnp.where(upper, total, got)
            total = call(
                lambda *refs: pair_kernel(width, *refs),
                (one(group), conv_weight, k_index, k_real, lower_half, upper_half),
                shape,
            )
        distance *= 2
    here, *sent = call(
        lambda *refs: spread_kernel(width, *refs),
        (one(group, live), conv_weight, k_index, k_real, base, before),
        [shape] * 4,
        [pltpu.VMEM((4, quarter, ROWS, 128), BF16)],
    )
    prefixes = [here] + [swap(x, d) for d, x in zip((1, 2, 3), sent)]

    shift = [(i, i + 1) for i in range(count - 1)]
    prev_key, prev_value = lax.ppermute((win_key[rows - WINDOW :], values[rows - WINDOW :]), "seq", shift)
    flat = jax.ShapeDtypeStruct(values.shape, F32)
    num, den, win = call(
        block_kernel,
        (one(position > 0), q_feat, k_feat, values, win_query, win_key, log_gates, conv_weight, prev_key, prev_value),
        [flat, flat, flat],
    )
    return call(
        finish_kernel,
        (one(group), q_feat, log_gates, q_index, q_real, *prefixes, num, den, win),
        jax.ShapeDtypeStruct(values.shape, BF16),
        [pltpu.VMEM((4, quarter, ROWS, 128), BF16)],
    )


def solution(mesh):
    rows = P(("grp", "seq"), "head")
    count = mesh.shape["seq"]
    return jax.shard_map(
        lambda *args: local(count, *args),
        mesh=mesh,
        in_specs=(rows,) * 6 + (P(None, "head"),),
        out_specs=rows,
        check_vma=False,
    )
```

```python
import numpy as np
import jax
import jax.numpy as jnp
from jax import lax
from jax.experimental import pallas as pl
from jax.experimental.pallas import tpu as pltpu
from jax.sharding import PartitionSpec as P

WINDOW = 64
ROWS = 160
MISC = 157
LOG2E = float(np.log2(np.e))
F32 = jnp.float32
BF16 = jnp.bfloat16
VMEM_LIMIT = 24 * 1024 * 1024


def feature_tables(width):
    first = -np.ones(ROWS, np.int32)
    second = -np.ones(ROWS, np.int32)
    scale = np.zeros(ROWS, np.float32)
    twice = np.ones(ROWS, np.float32)
    scale[0] = 1.0
    at = 1
    for i in range(width):
        first[at], scale[at] = i, width ** (-0.25)
        at += 1
    for i in range(width):
        for j in range(i, width):
            first[at], second[at], scale[at] = i, j, (2.0 * width) ** (-0.5)
            twice[at] = 1.0 if i == j else 2.0
            at += 1
    one_a = ((first < 0) & (scale > 0)).astype(np.float32)
    one_b = ((second < 0) & (scale > 0)).astype(np.float32)
    return first, second, one_a, one_b, scale, twice


def key_table(width):
    first, second, one_a, one_b, scale, _ = feature_tables(width)
    table = np.zeros((ROWS, 128), np.float32)
    table[:, :5] = np.stack([first, second, one_a, one_b, scale], axis=1)
    return jnp.asarray(np.where(table < 0, -1000, table), F32)


def query_table(width):
    first, second, one_a, one_b, scale, twice = feature_tables(width)
    table = np.zeros((8, 256), np.float32)
    table[:2] = -1000
    for row, line in enumerate((first, second, one_a, one_b, scale * twice)):
        table[row, :ROWS] = np.where(line < 0, -1000, line)
    return jnp.asarray(table, F32)


def nt(a, b):
    return lax.dot_general(a, b, (((1,), (1,)), ((), ())), preferred_element_type=F32)


def nn(a, b):
    return lax.dot_general(a, b, (((1,), (0,)), ((), ())), preferred_element_type=F32)


def tn(a, b):
    return lax.dot_general(a, b, (((0,), (0,)), ((), ())), preferred_element_type=F32)


def parts(wide):
    upper = wide.astype(BF16)
    rest = wide - upper.astype(F32)
    middle = rest.astype(BF16)
    lower = (rest - middle.astype(F32)).astype(BF16)
    return upper, middle, lower


def iota(shape, dim):
    return lax.broadcasted_iota(jnp.int32, shape, dim)


def cumulative_rows(gates):
    heads, rows = gates.shape
    upto = (iota((128, 128), 0) <= iota((128, 128), 1)).astype(BF16)
    blocks = [gates[:, i : i + 128] for i in range(0, rows, 128)]
    stacked = jnp.concatenate([piece for block in blocks for piece in parts(block)], axis=0)
    inside = nn(stacked, upto)
    done, before = [], 0.0
    for i in range(len(blocks)):
        three = [inside[(3 * i + p) * heads : (3 * i + p + 1) * heads] for p in range(3)]
        done.append(three[0] + three[1] + three[2] + before)
        before = done[-1][:, 127:]
    return jnp.concatenate(done, axis=1)


def columns_of(table_ref):
    return [jnp.broadcast_to(table_ref[:, i : i + 1], (ROWS, 128)) for i in range(5)]


def shifted(x, by):
    return jnp.where(iota(x.shape, 0) < by, 0.0, pltpu.roll(x, by, 0))


def edge_kernel(k_ref, v_ref, out_ref, sems):
    rows = k_ref.shape[0]
    copies = [
        pltpu.make_async_copy(
            ref.at[pl.ds(rows - WINDOW, WINDOW)], out_ref.at[pl.ds(i * WINDOW, WINDOW)], sems.at[i]
        )
        for i, ref in enumerate((k_ref, v_ref))
    ]
    for copy in copies:
        copy.start()
    for copy in copies:
        copy.wait()


def one_state(head, out_ref, j, k, v_ref, w_ref, cum_ref, norm_ref, table):
    rows, wide = k.shape
    heads = cum_ref.shape[0]
    width = wide // heads
    first, second, one_a, one_b, scale = table
    lane = iota((ROWS, wide), 1).astype(F32)
    lane1 = iota((1, 128), 1)
    sub = iota((8, 128), 0)
    at = pl.ds(pl.multiple_of(head * 128, 128), 128)
    shift = (head * width).astype(F32)
    pick_a = (lane == first + shift).astype(BF16)
    pick_b = (lane == second + shift).astype(BF16)
    cum = cum_ref[pl.ds(head, 1), :]
    last = cum[:, rows - 1 :]
    keep = jnp.exp(last - cum)
    wide4 = lambda x: jnp.concatenate([x] * (rows // 128), axis=1)
    phi = (((nt(pick_a, k) + wide4(one_a)) * (nt(pick_b, k) + wide4(one_b)) * wide4(scale)) * keep).astype(BF16)
    v = v_ref[:, at].astype(F32)
    w = w_ref[:, at]
    conv = (w[0:1] * v + w[1:2] * shifted(v, 1) + w[2:3] * shifted(v, 2)).astype(BF16)
    state = nn(phi, conv)
    norm_ref[j, :, 0:ROWS] = nt(jnp.ones((8, rows), BF16), phi)
    norm = norm_ref[j, 0:1, :]
    high = norm.astype(BF16).astype(F32)
    low = norm - high
    keys8 = k[0:16].astype(F32)[0:8]
    turned = pltpu.roll(keys8, (wide - head * width) % wide, 1)
    turned2 = pltpu.roll(keys8, (wide - head * width + width) % wide, 1)
    misc = jnp.where(lane1 < width, turned[0:1], 0.0)
    misc = jnp.where((lane1 >= width) & (lane1 < 2 * width), turned2[1:2], misc)
    place = 2 * width
    for value in (keep[:, 0:1], keep[:, 1:2], jnp.exp(last)):
        for piece in parts(value):
            misc = jnp.where(lane1 == place, piece.astype(F32), misc)
            place += 1
    tail = state[ROWS - 8 :]
    for row, line in enumerate((high[:, :128], high[:, 128:], low[:, :128], low[:, 128:], misc)):
        tail = jnp.where(sub == row + 1, line, tail)
    tail = jnp.where(sub >= 6, v[rows - 8 :], tail)
    out_ref[j, 0 : ROWS - 16, :] = state[: ROWS - 16].astype(BF16)
    out_ref[j, ROWS - 16 :, :] = jnp.concatenate([state[ROWS - 16 : ROWS - 8], tail]).astype(BF16)


def state_kernel(order, group_ref, k_ref, v_ref, g_ref, w_ref, table_ref, *refs):
    outs, cum_ref, norm_ref = refs[: len(order)], refs[len(order)], refs[-1]
    cum_ref[...] = cumulative_rows(g_ref[...])
    norm_ref[...] = jnp.zeros(norm_ref.shape, F32)
    table = columns_of(table_ref)
    k = k_ref[...]
    for i, (out_ref, distance) in enumerate(zip(outs, order)):
        count = out_ref.shape[0]
        for j in range(count):
            head = (group_ref[0] ^ distance) * count + j
            one_state(head, out_ref, j, k, v_ref, w_ref, cum_ref, norm_ref.at[i], table)


def own_kernel(group_ref, k_ref, v_ref, cum_ref, w_ref, table_ref, after_ref, out_ref, column_ref, norm_ref):
    norm_ref[...] = jnp.zeros(norm_ref.shape, F32)
    table = columns_of(table_ref)
    k = k_ref[...]
    count = out_ref.shape[0]
    for j in range(count):
        one_state(group_ref[0] * count + j, out_ref, j, k, v_ref, w_ref, cum_ref, norm_ref, table)
    column_ref[...] = cum_ref[...].T


def tail_of(tile):
    return tile[ROWS - 8 :]


def value_of(tile, i, width):
    lane1 = iota((1, 128), 1)
    place = 2 * width + 3 * i
    here = (lane1 >= place) & (lane1 < place + 3)
    return jnp.sum(jnp.where(here, tail_of(tile)[5:6], 0.0), axis=1, keepdims=True)


def first_keys(tiles, table, width):
    lane = iota((ROWS, 128), 1).astype(F32)
    lines = [tail_of(tile)[5:6] for tile in tiles]
    rows = jnp.concatenate(lines + [jnp.zeros((8 - len(lines), 128), F32)] if len(lines) < 8 else lines).astype(BF16)
    first, second, one_a, one_b, scale = table
    found = []
    for token in range(2):
        pick_a = (lane == first + token * width).astype(BF16)
        pick_b = (lane == second + token * width).astype(BF16)
        found.append((nt(pick_a, rows) + one_a[:, 0:8]) * (nt(pick_b, rows) + one_b[:, 0:8]) * scale[:, 0:8])
    return found


def carried(tile, w):
    tail = tail_of(tile)
    return w[1:2] * tail[7:8] + w[2:3] * tail[6:7], w[2:3] * tail[7:8]


def seam(left, columns, enter, w):
    carry0, carry1 = carried(left, w)
    return columns[0] * (enter[0] * carry0) + columns[1] * (enter[1] * carry1)


def merge(left, right, columns, w, width):
    decay = value_of(right, 2, width)
    joined = decay * left + right + seam(left, columns, (value_of(right, 0, width), value_of(right, 1, width)), w)
    sub = iota((8, 128), 0)
    lane1 = iota((1, 128), 1)
    misc = tail_of(left)[5:6]
    misc = jnp.where(lane1 < 2 * width, misc, misc * decay)
    tail = jnp.where(sub == 5, misc, tail_of(joined))
    tail = jnp.where(sub >= 6, tail_of(right), tail)
    return jnp.concatenate([joined[: ROWS - 8], tail])


def packed(tile, width):
    tail = tail_of(tile)
    sub = iota((8, 128), 0)
    lane1 = iota((1, 128), 1)
    misc = tail[5:6]
    fresh = jnp.where(lane1 < 2 * width, misc, 0.0)
    place = 2 * width
    for i in range(3):
        for piece in parts(value_of(tile, i, width)):
            fresh = jnp.where(lane1 == place, piece.astype(F32), fresh)
            place += 1
    tail = jnp.where(sub == 5, fresh, norm_parts(tail))
    return jnp.concatenate([tile[: ROWS - 8], tail]).astype(BF16)


def norm_parts(tail):
    sub = iota((8, 128), 0)
    for row in (1, 2):
        norm = tail[row : row + 1] + tail[row + 2 : row + 3]
        high = norm.astype(BF16).astype(F32)
        tail = jnp.where(sub == row, high, jnp.where(sub == row + 2, norm - high, tail))
    return tail


def head_taps(w_ref, head):
    return w_ref[:, pl.ds(pl.multiple_of(head * 128, 128), 128)]


def group_kernel(width, group_ref, w_ref, table_ref, x0, x1, x2, x3, after_ref, total_ref, before_ref, keys_ref, small_ref, held):
    group = group_ref[0]
    count = x0.shape[0]
    for distance, ref in enumerate((x0, x1, x2, x3)):
        held[group ^ distance] = ref[...]
    tiles = [[held[p, j].astype(F32) for j in range(count)] for p in range(4)]
    columns = first_keys([tiles[p][j] for p in range(4) for j in range(count)], columns_of(table_ref), width)
    sub = iota((8, 128), 0)
    for j in range(count):
        w = head_taps(w_ref, group * count + j)
        so_far = tiles[0][j]
        for p in range(1, 4):
            before_ref[p - 1, j] = so_far
            pick = p * count + j
            so_far = merge(so_far, tiles[p][j], [c[:, pick : pick + 1] for c in columns], w, width)
        total_ref[j] = packed(so_far, width)
        for token in range(2):
            keys_ref[token, j] = jnp.broadcast_to(columns[token][:, j : j + 1], (ROWS, 128))
        decays = [value_of(tiles[p][j], 2, width) for p in range(3)]
        small = jnp.zeros((8, 128), F32)
        lines = decays[0], value_of(tiles[0][j], 0, width), value_of(tiles[0][j], 1, width), decays[1], decays[1] * decays[2]
        for row, value in enumerate(lines):
            small = jnp.where(sub == row, value, small)
        small_ref[j] = small


def pair_kernel(width, group_ref, w_ref, table_ref, left_ref, right_ref, out_ref):
    count = left_ref.shape[0]
    rights = [right_ref[j].astype(F32) for j in range(count)]
    columns = first_keys(rights, columns_of(table_ref), width)
    for j in range(count):
        w = head_taps(w_ref, group_ref[0] * count + j)
        left = left_ref[j].astype(F32)
        out_ref[j] = packed(merge(left, rights[j], [c[:, j : j + 1] for c in columns], w, width), width)


def spread_kernel(group_ref, live_ref, w_ref, base_ref, before_ref, keys_ref, small_ref, after_ref, o0, o1, o2, o3, held):
    group = group_ref[0]
    live = live_ref[0] > 0
    count = base_ref.shape[0]
    for j in range(count):
        w = head_taps(w_ref, group * count + j)
        base = jnp.where(live, base_ref[j].astype(F32), 0.0)
        held[0, j] = base.astype(BF16)
        small = small_ref[j]
        through = small[0:1] * base + seam(base, (keys_ref[0, j], keys_ref[1, j]), (small[1:2], small[2:3]), w)
        for p in range(3):
            tile = before_ref[p, j] + (through if p == 0 else small[2 + p : 3 + p] * through)
            held[p + 1, j] = jnp.concatenate([tile[: ROWS - 8], norm_parts(tail_of(tile))]).astype(BF16)
    for distance, ref in enumerate((o0, o1, o2, o3)):
        ref[...] = held[group ^ distance]


def window_kernel(edge_ref, wq_ref, wk_ref, v_ref, halo_ref, after_ref, win_ref):
    rows = wq_ref.shape[0]
    half = WINDOW
    seen = iota((half, 2 * half), 1)
    mine = iota((half, 2 * half), 0)
    valid = (seen > mine) & (seen <= mine + half)
    start = valid & ((seen >= half) | (edge_ref[0] > 0))
    steps = rows // half
    ones = jnp.ones((rows + half, 128), BF16)
    heads = wq_ref.shape[1] // 128
    for pair in range(0, heads, 2):
        scores, right = [], []
        for h in range(pair, pair + 2):
            at = slice(128 * h, 128 * h + 128)
            keys = jnp.concatenate([halo_ref[:half, at], wk_ref[:, at]])
            right.append(jnp.concatenate([jnp.concatenate([halo_ref[half:, at], v_ref[:, at]]), ones], axis=1))
            scores.append([nt(wq_ref[i * half : (i + 1) * half, at], keys[i * half : (i + 2) * half]) for i in range(steps)])
        probs = []
        for group in scores:
            group = [jnp.where(start if i == 0 else valid, s * (128 ** (-0.5) * LOG2E), -jnp.inf) for i, s in enumerate(group)]
            s = jnp.concatenate(group)
            probs.append(jnp.exp2(s - jnp.max(s, axis=1, keepdims=True)).astype(BF16))
        for h, p, r in zip(range(pair, pair + 2), probs, right):
            both = jnp.concatenate([nn(p[i * half : (i + 1) * half], r[i * half : (i + 2) * half]) for i in range(steps)])
            win_ref[:, 128 * h : 128 * h + 128] = both[:, :128] / both[:, 128:]


def block_kernel(q_ref, k_ref, v_ref, w_ref, cum_ref, column_ref, halo_ref, after_ref, num_ref, den_ref):
    rows, wide = q_ref.shape
    heads = cum_ref.shape[0]
    width = wide // heads
    q = q_ref[...]
    k = k_ref[...]
    cum_row = cum_ref[...] * LOG2E
    cum_col = column_ref[...] * LOG2E
    lane = iota(k.shape, 1)
    step, piece = 256, 128
    ones = jnp.ones((rows, 128), BF16)
    causal = iota((piece, piece), 0) >= iota((piece, piece), 1)
    for h in range(heads):
        at = slice(128 * h, 128 * h + 128)
        k_here = jnp.where((lane >= h * width) & (lane < (h + 1) * width), k, jnp.zeros_like(k)) * BF16(width ** (-0.5))
        v = v_ref[:, at].astype(F32)
        ahead = jnp.concatenate([halo_ref[2 * WINDOW - 16 :, at].astype(F32)[8:], v])
        w = w_ref[:, at]
        conv = w[0:1] * v + w[1:2] * pltpu.roll(ahead, 1, 0)[8:] + w[2:3] * pltpu.roll(ahead, 2, 0)[8:]
        right = jnp.concatenate([conv.astype(BF16), ones], axis=1)
        column = jnp.broadcast_to(cum_col[:, h : h + 1], (rows, piece))
        total = None
        for low in range(0, rows, step):
            x = nt(q[low:], k_here[low : low + step])
            lines = []
            for i in range(low, rows, piece):
                line = []
                for j in range(low, low + step, piece):
                    if j > i:
                        line.append(jnp.zeros((piece, piece), BF16))
                        continue
                    here = x[i - low : i - low + piece, j - low : j - low + piece]
                    gap = column[i : i + piece] - cum_row[h : h + 1, j : j + piece]
                    if i == j:
                        gap = jnp.where(causal, gap, -jnp.inf)
                    line.append((((0.5 * here + 1.0) * here + 1.0) * jnp.exp2(gap)).astype(BF16))
                lines.append(jnp.concatenate(line, axis=1))
            both = nn(jnp.concatenate(lines), right[low : low + step])
            total = both if total is None else jnp.concatenate([total[:low], total[low:] + both])
        num_ref[:, at] = total[:, :128]
        den_ref[:, at] = total[:, 128:]


def query_kernel(q_ref, column_ref, table_ref, after_ref, out_ref):
    rows, wide = q_ref.shape
    heads = column_ref.shape[1]
    width = wide // heads
    q = q_ref[...]
    enter = jnp.exp(column_ref[...])
    row = iota((wide, 256), 0).astype(F32)
    first, second, one_a, one_b, scale = (table_ref[i : i + 1] for i in range(5))
    for h in range(heads):
        pick_a = (row == first + h * width).astype(BF16)
        pick_b = (row == second + h * width).astype(BF16)
        phi = (nn(q, pick_a) + one_a) * (nn(q, pick_b) + one_b) * scale
        out_ref[h] = (phi * enter[:, h : h + 1]).astype(BF16)


def finish_kernel(group_ref, phi_ref, x0, x1, x2, x3, num_ref, den_ref, win_ref, out_ref, held):
    group = group_ref[0]
    heads = phi_ref.shape[0]
    count = x0.shape[0]
    for distance, ref in enumerate((x0, x1, x2, x3)):
        held[group ^ distance] = ref[...]
    tiles = [held[h // count, h % count] for h in range(heads)]
    lines = []
    for tile in tiles:
        tail = tile[ROWS - 16 :].astype(F32)[8:]
        lines.append(jnp.concatenate([tail[1:2] + tail[3:4], tail[2:3] + tail[4:5]], axis=1))
    norms = jnp.concatenate(lines).T
    for h in range(heads):
        at = slice(128 * h, 128 * h + 128)
        norm = jnp.broadcast_to(norms[:ROWS, h : h + 1], (ROWS, 128)).astype(BF16)
        both = nn(phi_ref[h][:, :ROWS], jnp.concatenate([tiles[h], norm], axis=1))
        out = (num_ref[:, at] + both[:, :128]) / (den_ref[:, at] + both[:, 128:]) + win_ref[:, at]
        out_ref[:, at] = out.astype(BF16)


def call(kernel, inputs, outs, scratch=(), smem=(), free=(), far=(), name=None):
    def space(i):
        return pltpu.SMEM if i in smem else pl.ANY if i in free else pltpu.HBM if i in far else pltpu.VMEM

    return pl.pallas_call(
        kernel,
        out_shape=outs,
        in_specs=[pl.BlockSpec(memory_space=space(i)) for i in range(len(inputs))],
        out_specs=jax.tree.map(lambda _: pl.BlockSpec(memory_space=pltpu.VMEM), outs),
        scratch_shapes=scratch,
        compiler_params=pltpu.CompilerParams(vmem_limit_bytes=VMEM_LIMIT),
        name=name,
    )(*inputs)


def local(count, q_feat, k_feat, values, win_query, win_key, log_gates, conv_weight):
    rows = values.shape[0]
    heads = log_gates.shape[1]
    width = q_feat.shape[1] // heads
    quarter = heads // 4
    position = lax.axis_index("seq")
    one = lambda number: jnp.reshape(number, (1,)).astype(jnp.int32)
    group = one(position & 3)
    table = key_table(width)
    shape = jax.ShapeDtypeStruct((quarter, ROWS, 128), BF16)
    wide = lambda *dims: jax.ShapeDtypeStruct(dims, F32)
    norm_scratch = pltpu.VMEM((quarter, 8, 256), F32)
    held = pltpu.VMEM((4, quarter, ROWS, 128), BF16)

    def swap(x, distance):
        return lax.ppermute(x, "seq", [(i, i ^ distance) for i in range(count)])

    edge = call(
        edge_kernel,
        (win_key, values),
        jax.ShapeDtypeStruct((2 * WINDOW, values.shape[1]), BF16),
        [pltpu.SemaphoreType.DMA((2,))],
        far=(0, 1),
        name="edge",
    )
    halo = lax.ppermute(edge, "seq", [(i, i + 1) for i in range(count - 1)])

    *sent, cum = call(
        lambda *refs: state_kernel((1, 2, 3), *refs),
        (group, k_feat, values, log_gates.T, conv_weight, table),
        [shape] * 3 + [wide(heads, rows)],
        [pltpu.VMEM((3, quarter, 8, 256), F32)],
        smem=(0,),
        name="states",
    )
    others = [swap(x, d) for d, x in zip((1, 2, 3), sent)]
    own, column = call(
        own_kernel,
        (group, k_feat, values, cum, conv_weight, table, sent[0]),
        [shape, wide(rows, heads)],
        [norm_scratch],
        smem=(0,),
        free=(6,),
        name="own_states",
    )
    win = call(
        window_kernel,
        (one(position > 0), win_query, win_key, values, halo, own),
        wide(*values.shape),
        smem=(0,),
        free=(5,),
        name="window",
    )
    total, before, keys, small = call(
        lambda *refs: group_kernel(width, *refs),
        (group, conv_weight, table, own, *others, win),
        [shape, wide(3, quarter, ROWS, 128), wide(2, quarter, ROWS, 128), wide(quarter, 8, 128)],
        [held],
        smem=(0,),
        free=(7,),
        name="merge_group",
    )
    base = jnp.zeros_like(total)
    live = position < 0
    distance = 4
    last = total
    while distance < count:
        got = swap(total, distance)
        upper = (position & distance) > 0

        def pair(left, right):
            return call(
                lambda *refs: pair_kernel(width, *refs),
                (group, conv_weight, table, left, right),
                shape,
                smem=(0,),
                name="merge_pair",
            )

        if distance == 4:
            base = got
        else:
            base = jnp.where(upper, jnp.where(live, pair(got, base), got), base)
        live = live | upper
        if 2 * distance < count:
            total = pair(jnp.where(upper, got, total), jnp.where(upper, total, got))
        distance *= 2
    num, den = call(
        block_kernel,
        (q_feat, k_feat, values, conv_weight, cum, column, halo, last),
        [wide(*values.shape)] * 2,
        free=(7,),
        name="block",
    )
    here, *sent = call(
        spread_kernel,
        (group, one(live), conv_weight, base, before, keys, small, num),
        [shape] * 4,
        [held],
        smem=(0, 1),
        free=(7,),
        name="spread",
    )
    prefixes = [here] + [swap(x, d) for d, x in zip((1, 2, 3), sent)]
    phi = call(
        query_kernel,
        (q_feat, column, query_table(width), here),
        jax.ShapeDtypeStruct((heads, rows, 256), BF16),
        free=(3,),
        name="query_features",
    )
    return call(
        finish_kernel,
        (group, phi, *prefixes, num, den, win),
        jax.ShapeDtypeStruct(values.shape, BF16),
        [held],
        smem=(0,),
        name="finish",
    )


def solution(mesh):
    rows = P(("grp", "seq"), "head")
    count = mesh.shape["seq"]
    return jax.shard_map(
        lambda *args: local(count, *args),
        mesh=mesh,
        in_specs=(rows,) * 6 + (P(None, "head"),),
        out_specs=rows,
        check_vma=False,
    )
```

```python
import numpy as np
import jax
import jax.numpy as jnp
from jax import lax
from jax.experimental import pallas as pl
from jax.experimental.pallas import tpu as pltpu
from jax.sharding import PartitionSpec as P

WINDOW = 64
ROWS = 160
EDGE = 158
LOG2E = float(np.log2(np.e))
F32 = jnp.float32
BF16 = jnp.bfloat16
VMEM_LIMIT = 24 * 1024 * 1024


def feature_tables(width):
    first = -np.ones(ROWS, np.int32)
    second = -np.ones(ROWS, np.int32)
    scale = np.zeros(ROWS, np.float32)
    twice = np.ones(ROWS, np.float32)
    scale[0] = 1.0
    at = 1
    for i in range(width):
        first[at], scale[at] = i, width ** (-0.25)
        at += 1
    for i in range(width):
        for j in range(i, width):
            first[at], second[at], scale[at] = i, j, (2.0 * width) ** (-0.5)
            twice[at] = 1.0 if i == j else 2.0
            at += 1
    one_a = ((first < 0) & (scale > 0)).astype(np.float32)
    one_b = ((second < 0) & (scale > 0)).astype(np.float32)
    return first, second, one_a, one_b, scale, twice


def key_table(width):
    first, second, one_a, one_b, scale, _ = feature_tables(width)
    table = np.zeros((ROWS, 128), np.float32)
    table[:, :5] = np.stack([first, second, one_a, one_b, scale], axis=1)
    return jnp.asarray(np.where(table < 0, -1000, table), F32)


def query_table(width):
    first, second, one_a, one_b, scale, twice = feature_tables(width)
    table = np.zeros((8, 256), np.float32)
    table[:2] = -1000
    for row, line in enumerate((first, second, one_a, one_b, scale * twice)):
        table[row, :ROWS] = np.where(line < 0, -1000, line)
    table[2:4, EDGE : EDGE + 2] = 1.0
    table[4:6, EDGE : EDGE + 2] = 0.5
    return jnp.asarray(table, F32)


def nt(a, b):
    return lax.dot_general(a, b, (((1,), (1,)), ((), ())), preferred_element_type=F32)


def nn(a, b):
    return lax.dot_general(a, b, (((1,), (0,)), ((), ())), preferred_element_type=F32)


def tn(a, b):
    return lax.dot_general(a, b, (((0,), (0,)), ((), ())), preferred_element_type=F32)


def parts(wide):
    upper = wide.astype(BF16)
    rest = wide - upper.astype(F32)
    middle = rest.astype(BF16)
    lower = (rest - middle.astype(F32)).astype(BF16)
    return upper, middle, lower


def iota(shape, dim):
    return lax.broadcasted_iota(jnp.int32, shape, dim)


def cumulative_rows(gates):
    heads, rows = gates.shape
    upto = (iota((128, 128), 0) <= iota((128, 128), 1)).astype(BF16)
    blocks = [gates[:, i : i + 128] for i in range(0, rows, 128)]
    stacked = jnp.concatenate([piece for block in blocks for piece in parts(block)], axis=0)
    inside = nn(stacked, upto)
    done, before = [], 0.0
    for i in range(len(blocks)):
        three = [inside[(3 * i + p) * heads : (3 * i + p + 1) * heads] for p in range(3)]
        done.append(three[0] + three[1] + three[2] + before)
        before = done[-1][:, 127:]
    return jnp.concatenate(done, axis=1)


def columns_of(table_ref):
    return [jnp.broadcast_to(table_ref[:, i : i + 1], (ROWS, 128)) for i in range(5)]


def shifted(x, by):
    return jnp.where(iota(x.shape, 0) < by, 0.0, pltpu.roll(x, by, 0))


def edge_kernel(k_ref, v_ref, after_ref, out_ref, sems):
    rows = k_ref.shape[0]
    copies = [
        pltpu.make_async_copy(
            ref.at[pl.ds(rows - WINDOW, WINDOW)], out_ref.at[pl.ds(i * WINDOW, WINDOW)], sems.at[i]
        )
        for i, ref in enumerate((k_ref, v_ref))
    ]
    for copy in copies:
        copy.start()
    for copy in copies:
        copy.wait()


def one_state(head, out_ref, j, k, v_ref, w_ref, cum_ref, norm_ref, table):
    rows, wide = k.shape
    heads = cum_ref.shape[0]
    width = wide // heads
    first, second, one_a, one_b, scale = table
    lane = iota((ROWS, wide), 1).astype(F32)
    lane1 = iota((1, 128), 1)
    sub = iota((8, 128), 0)
    at = pl.ds(pl.multiple_of(head * 128, 128), 128)
    shift = (head * width).astype(F32)
    pick_a = (lane == first + shift).astype(BF16)
    pick_b = (lane == second + shift).astype(BF16)
    cum = cum_ref[pl.ds(head, 1), :]
    last = cum[:, rows - 1 :]
    keep = jnp.exp(last - cum)
    wide4 = lambda x: jnp.concatenate([x] * (rows // 128), axis=1)
    phi = (((nt(pick_a, k) + wide4(one_a)) * (nt(pick_b, k) + wide4(one_b)) * wide4(scale)) * keep).astype(BF16)
    v = v_ref[:, at].astype(F32)
    w = w_ref[:, at]
    conv = (w[0:1] * v + w[1:2] * shifted(v, 1) + w[2:3] * shifted(v, 2)).astype(BF16)
    state = nn(phi, conv)
    norm_ref[j, :, 0:ROWS] = nt(jnp.ones((8, rows), BF16), phi)
    norm = norm_ref[j, 0:1, :]
    high = norm.astype(BF16).astype(F32)
    low = norm - high
    keys8 = k[0:16].astype(F32)[0:8]
    turned = pltpu.roll(keys8, (wide - head * width) % wide, 1)
    turned2 = pltpu.roll(keys8, (wide - head * width + width) % wide, 1)
    misc = jnp.where(lane1 < width, turned[0:1], 0.0)
    misc = jnp.where((lane1 >= width) & (lane1 < 2 * width), turned2[1:2], misc)
    place = 2 * width
    for value in (keep[:, 0:1], keep[:, 1:2], jnp.exp(last)):
        for piece in parts(value):
            misc = jnp.where(lane1 == place, piece.astype(F32), misc)
            place += 1
    tail = state[ROWS - 8 :]
    for row, line in enumerate((high[:, :128], high[:, 128:], low[:, :128], low[:, 128:], misc)):
        tail = jnp.where(sub == row + 1, line, tail)
    tail = jnp.where(sub >= 6, v[rows - 8 :], tail)
    out_ref[j, 0 : ROWS - 16, :] = state[: ROWS - 16].astype(BF16)
    out_ref[j, ROWS - 16 :, :] = jnp.concatenate([state[ROWS - 16 : ROWS - 8], tail]).astype(BF16)


def gate_kernel(place_ref, g_ref, cum_ref):
    cum_ref[...] = cumulative_rows(g_ref[...])


def state_kernel(order, place_ref, k_ref, v_ref, cum_ref, w_ref, table_ref, after_ref, *refs):
    outs, norm_ref = refs[:-1], refs[-1]
    norm_ref[...] = jnp.zeros(norm_ref.shape, F32)
    table = columns_of(table_ref)
    k = k_ref[...]
    for i, (out_ref, distance) in enumerate(zip(outs, order)):
        count = out_ref.shape[0]
        for j in range(count):
            head = ((place_ref[0] & 3) ^ distance) * count + j
            one_state(head, out_ref, j, k, v_ref, w_ref, cum_ref, norm_ref.at[i], table)


def tail_of(tile):
    return tile[ROWS - 8 :]


def value_of(tile, i, width):
    lane1 = iota((1, 128), 1)
    place = 2 * width + 3 * i
    here = (lane1 >= place) & (lane1 < place + 3)
    return jnp.sum(jnp.where(here, tail_of(tile)[5:6], 0.0), axis=1, keepdims=True)


def first_keys(tiles, table, width):
    lane = iota((ROWS, 128), 1).astype(F32)
    lines = [tail_of(tile)[5:6] for tile in tiles]
    rows = jnp.concatenate(lines + [jnp.zeros((8 - len(lines), 128), F32)] if len(lines) < 8 else lines).astype(BF16)
    first, second, one_a, one_b, scale = table
    found = []
    for token in range(2):
        pick_a = (lane == first + token * width).astype(BF16)
        pick_b = (lane == second + token * width).astype(BF16)
        found.append((nt(pick_a, rows) + one_a[:, 0:8]) * (nt(pick_b, rows) + one_b[:, 0:8]) * scale[:, 0:8])
    return found


def carried(tile, w):
    tail = tail_of(tile)
    return w[1:2] * tail[7:8] + w[2:3] * tail[6:7], w[2:3] * tail[7:8]


def seam(left, columns, enter, w):
    carry0, carry1 = carried(left, w)
    return columns[0] * (enter[0] * carry0) + columns[1] * (enter[1] * carry1)


def merge(left, right, columns, w, width):
    decay = value_of(right, 2, width)
    joined = decay * left + right + seam(left, columns, (value_of(right, 0, width), value_of(right, 1, width)), w)
    sub = iota((8, 128), 0)
    lane1 = iota((1, 128), 1)
    misc = tail_of(left)[5:6]
    misc = jnp.where(lane1 < 2 * width, misc, misc * decay)
    tail = jnp.where(sub == 5, misc, tail_of(joined))
    tail = jnp.where(sub >= 6, tail_of(right), tail)
    return jnp.concatenate([joined[: ROWS - 8], tail])


def packed(tile, width):
    tail = tail_of(tile)
    sub = iota((8, 128), 0)
    lane1 = iota((1, 128), 1)
    misc = tail[5:6]
    fresh = jnp.where(lane1 < 2 * width, misc, 0.0)
    place = 2 * width
    for i in range(3):
        for piece in parts(value_of(tile, i, width)):
            fresh = jnp.where(lane1 == place, piece.astype(F32), fresh)
            place += 1
    tail = jnp.where(sub == 5, fresh, norm_parts(tail))
    return jnp.concatenate([tile[: ROWS - 8], tail]).astype(BF16)


def norm_parts(tail):
    sub = iota((8, 128), 0)
    for row in (1, 2):
        norm = tail[row : row + 1] + tail[row + 2 : row + 3]
        high = norm.astype(BF16).astype(F32)
        tail = jnp.where(sub == row, high, jnp.where(sub == row + 2, norm - high, tail))
    return tail


def head_taps(w_ref, head):
    return w_ref[:, pl.ds(pl.multiple_of(head * 128, 128), 128)]


def group_kernel(width, place_ref, w_ref, table_ref, x0, x1, x2, x3, after_ref, total_ref, before_ref, keys_ref, small_ref, held):
    group = (place_ref[0] & 3)
    count = x0.shape[0]
    for distance, ref in enumerate((x0, x1, x2, x3)):
        held[group ^ distance] = ref[...]
    tiles = [[held[p, j].astype(F32) for j in range(count)] for p in range(4)]
    columns = first_keys([tiles[p][j] for p in range(4) for j in range(count)], columns_of(table_ref), width)
    sub = iota((8, 128), 0)
    for j in range(count):
        w = head_taps(w_ref, group * count + j)
        so_far = tiles[0][j]
        for p in range(1, 4):
            before_ref[p - 1, j] = so_far
            pick = p * count + j
            so_far = merge(so_far, tiles[p][j], [c[:, pick : pick + 1] for c in columns], w, width)
        total_ref[j] = packed(so_far, width)
        for token in range(2):
            keys_ref[token, j] = jnp.broadcast_to(columns[token][:, j : j + 1], (ROWS, 128))
        decays = [value_of(tiles[p][j], 2, width) for p in range(3)]
        small = jnp.zeros((8, 128), F32)
        lines = decays[0], value_of(tiles[0][j], 0, width), value_of(tiles[0][j], 1, width), decays[1], decays[1] * decays[2]
        for row, value in enumerate(lines):
            small = jnp.where(sub == row, value, small)
        small_ref[j] = small


def pair_kernel(width, place_ref, w_ref, table_ref, left_ref, right_ref, out_ref):
    count = left_ref.shape[0]
    rights = [right_ref[j].astype(F32) for j in range(count)]
    columns = first_keys(rights, columns_of(table_ref), width)
    for j in range(count):
        w = head_taps(w_ref, (place_ref[0] & 3) * count + j)
        left = left_ref[j].astype(F32)
        out_ref[j] = packed(merge(left, rights[j], [c[:, j : j + 1] for c in columns], w, width), width)


def with_edge(tile, source, w):
    carry0, carry1 = carried(source, w)
    sub = iota((8, 128), 0)
    tail = norm_parts(tail_of(tile))
    tail = jnp.where(sub == 6, carry0, jnp.where(sub == 7, carry1, tail))
    return jnp.concatenate([tile[: ROWS - 8], tail]).astype(BF16)


def spread_kernel(place_ref, w_ref, base_ref, before_ref, keys_ref, small_ref, after_ref, o0, o1, o2, o3, held):
    group = (place_ref[0] & 3)
    live = place_ref[0] > 3
    count = base_ref.shape[0]
    for j in range(count):
        w = head_taps(w_ref, group * count + j)
        base = jnp.where(live, base_ref[j].astype(F32), 0.0)
        held[0, j] = with_edge(base, base, w)
        small = small_ref[j]
        through = small[0:1] * base + seam(base, (keys_ref[0, j], keys_ref[1, j]), (small[1:2], small[2:3]), w)
        for p in range(3):
            tile = before_ref[p, j] + (through if p == 0 else small[2 + p : 3 + p] * through)
            held[p + 1, j] = with_edge(tile, before_ref[p, j], w)
    for distance, ref in enumerate((o0, o1, o2, o3)):
        ref[...] = held[group ^ distance]


def window_kernel(place_ref, wq_ref, wk_ref, v_ref, halo_ref, after_ref, win_ref):
    rows = wq_ref.shape[0]
    half = WINDOW
    seen = iota((half, 2 * half), 1)
    mine = iota((half, 2 * half), 0)
    valid = (seen > mine) & (seen <= mine + half)
    start = valid & ((seen >= half) | (place_ref[0] > 0))
    steps = rows // half
    ones = jnp.ones((rows + half, 128), BF16)
    heads = wq_ref.shape[1] // 128
    for pair in range(0, heads, 2):
        scores, right = [], []
        for h in range(pair, pair + 2):
            at = slice(128 * h, 128 * h + 128)
            keys = jnp.concatenate([halo_ref[:half, at], wk_ref[:, at]])
            right.append(jnp.concatenate([jnp.concatenate([halo_ref[half:, at], v_ref[:, at]]), ones], axis=1))
            scores.append([nt(wq_ref[i * half : (i + 1) * half, at], keys[i * half : (i + 2) * half]) for i in range(steps)])
        probs = []
        for group in scores:
            group = [jnp.where(start if i == 0 else valid, s * (128 ** (-0.5) * LOG2E), -jnp.inf) for i, s in enumerate(group)]
            s = jnp.concatenate(group)
            probs.append(jnp.exp2(s - jnp.max(s, axis=1, keepdims=True)).astype(BF16))
        for h, p, r in zip(range(pair, pair + 2), probs, right):
            both = jnp.concatenate([nn(p[i * half : (i + 1) * half], r[i * half : (i + 2) * half]) for i in range(steps)])
            win_ref[:, 128 * h : 128 * h + 128] = both[:, :128] / both[:, 128:]


def block_kernel(q_ref, k_ref, v_ref, w_ref, cum_ref, after_ref, num_ref, den_ref, token_ref):
    rows, wide = q_ref.shape
    heads = cum_ref.shape[0]
    width = wide // heads
    q = q_ref[...]
    k = k_ref[...]
    cum_row = cum_ref[...] * LOG2E
    cum_col = cum_row.T
    token_ref[...] = jnp.zeros(token_ref.shape, F32)
    lane = iota(k.shape, 1)
    step, piece = 256, 128
    ones = jnp.ones((rows, 128), BF16)
    causal = iota((piece, piece), 0) >= iota((piece, piece), 1)
    for h in range(heads):
        at = slice(128 * h, 128 * h + 128)
        k_here = jnp.where((lane >= h * width) & (lane < (h + 1) * width), k, jnp.zeros_like(k)) * BF16(width ** (-0.5))
        v = v_ref[:, at].astype(F32)
        w = w_ref[:, at]
        conv = w[0:1] * v + w[1:2] * shifted(v, 1) + w[2:3] * shifted(v, 2)
        right = jnp.concatenate([conv.astype(BF16), ones], axis=1)
        column = jnp.broadcast_to(cum_col[:, h : h + 1], (rows, piece))
        total = None
        for low in range(0, rows, step):
            x = nt(q[low:], k_here[low : low + step])
            lines = []
            for i in range(low, rows, piece):
                line = []
                for j in range(low, low + step, piece):
                    if j > i:
                        line.append(jnp.zeros((piece, piece), BF16))
                        continue
                    here = x[i - low : i - low + piece, j - low : j - low + piece]
                    gap = column[i : i + piece] - cum_row[h : h + 1, j : j + piece]
                    if i == j:
                        gap = jnp.where(causal, gap, -jnp.inf)
                    line.append((((0.5 * here + 1.0) * here + 1.0) * jnp.exp2(gap)).astype(BF16))
                lines.append(jnp.concatenate(line, axis=1))
            both = nn(jnp.concatenate(lines), right[low : low + step])
            total = both if total is None else jnp.concatenate([total[:low], total[low:] + both])
        num_ref[:, at] = total[:, :128]
        den_ref[:, at] = total[:, 128:]


def query_kernel(q_ref, k_ref, cum_ref, table_ref, after_ref, out_ref, token_ref):
    rows, wide = q_ref.shape
    heads = cum_ref.shape[0]
    width = wide // heads
    q = q_ref[...]
    column = cum_ref[...].T
    token_ref[...] = jnp.zeros(token_ref.shape, F32)
    row = iota((wide, 256), 0)
    lane = iota((wide, 256), 1)
    keys = k_ref[0:16].astype(F32)[0:8].T * width ** (-0.5)
    keys = jnp.where(lane == EDGE, keys[:, 0:1], jnp.where(lane == EDGE + 1, keys[:, 1:2], 0.0))
    first, second, one_a, one_b, scale, plus = (table_ref[i : i + 1] for i in range(6))
    side = iota((1, 128), 1) + 128
    early = (iota((rows, 128), 0) == 0) & (iota((rows, 128), 1) == EDGE + 1 - 128)
    for h in range(heads):
        here = (row >= h * width) & (row < (h + 1) * width)
        keys_here = jnp.where(here, keys, 0.0)
        pick_a = jnp.where(row.astype(F32) == first + h * width, 1.0, keys_here).astype(BF16)
        pick_b = jnp.where(row.astype(F32) == second + h * width, 1.0, keys_here).astype(BF16)
        phi = (nn(q, pick_a) + one_a) * (nn(q, pick_b) + one_b) * scale + plus
        since = column[:, h : h + 1]
        offset = jnp.where(side == EDGE, since[0:1], jnp.where(side == EDGE + 1, since[1:2], 0.0))
        enter = jnp.where(early, 0.0, jnp.exp(since - offset))
        out_ref[h, :, :128] = (phi[:, :128] * jnp.exp(since)).astype(BF16)
        out_ref[h, :, 128:] = (phi[:, 128:] * enter).astype(BF16)


def finish_kernel(place_ref, phi_ref, x0, x1, x2, x3, num_ref, den_ref, win_ref, out_ref, held):
    group = (place_ref[0] & 3)
    heads = phi_ref.shape[0]
    count = x0.shape[0]
    for distance, ref in enumerate((x0, x1, x2, x3)):
        held[group ^ distance] = ref[...]
    tiles = [held[h // count, h % count] for h in range(heads)]
    lines = []
    for tile in tiles:
        tail = tile[ROWS - 16 :].astype(F32)[8:]
        lines.append(jnp.concatenate([tail[1:2] + tail[3:4], tail[2:3] + tail[4:5]], axis=1))
    norms = jnp.concatenate(lines).T
    for h in range(heads):
        at = slice(128 * h, 128 * h + 128)
        norm = jnp.broadcast_to(norms[:ROWS, h : h + 1], (ROWS, 128)).astype(BF16)
        both = nn(phi_ref[h][:, :ROWS], jnp.concatenate([tiles[h], norm], axis=1))
        out = (num_ref[:, at] + both[:, :128]) / (den_ref[:, at] + both[:, 128:]) + win_ref[:, at]
        out_ref[:, at] = out.astype(BF16)


def call(kernel, inputs, outs, scratch=(), smem=(), free=(), far=(), name=None, us=1.0):
    def space(i):
        return pltpu.SMEM if i in smem else pl.ANY if i in free else pltpu.HBM if i in far else pltpu.VMEM

    return pl.pallas_call(
        kernel,
        out_shape=outs,
        in_specs=[pl.BlockSpec(memory_space=space(i)) for i in range(len(inputs))],
        out_specs=jax.tree.map(lambda _: pl.BlockSpec(memory_space=pltpu.VMEM), outs),
        scratch_shapes=scratch,
        compiler_params=pltpu.CompilerParams(vmem_limit_bytes=VMEM_LIMIT),
        name=name,
        cost_estimate=pl.CostEstimate(flops=int(us * 3e9), bytes_accessed=int(us * 9e6), transcendentals=0),
    )(*inputs)


def local(count, q_feat, k_feat, values, win_query, win_key, log_gates, conv_weight):
    rows = values.shape[0]
    heads = log_gates.shape[1]
    width = q_feat.shape[1] // heads
    quarter = heads // 4
    position = lax.axis_index("seq")
    one = lambda number: jnp.reshape(number, (1,)).astype(jnp.int32)
    place = one(position)
    table = key_table(width)
    shape = jax.ShapeDtypeStruct((quarter, ROWS, 128), BF16)
    wide = lambda *dims: jax.ShapeDtypeStruct(dims, F32)
    held = pltpu.VMEM((4, quarter, ROWS, 128), BF16)

    def swap(x, distance):
        return lax.ppermute(x, "seq", [(i, i ^ distance) for i in range(count)])

    cum = call(gate_kernel, (place, log_gates.T), wide(heads, rows), smem=(0,), name="gates", us=6.0)

    def states(order, after, name, us):
        return call(
            lambda *refs: state_kernel(order, *refs),
            (place, k_feat, values, cum, conv_weight, table, after),
            [shape] * len(order),
            [pltpu.VMEM((len(order), quarter, 8, 256), F32)],
            smem=(0,),
            free=(6,),
            name=name,
            us=us,
        )

    sent = states((1, 2, 3), cum, "states", 2.0)
    others = [swap(x, d) for d, x in zip((1, 2, 3), sent)]
    (own,) = states((0,), sent[0], "own_states", 0.8)
    edge = call(
        edge_kernel,
        (win_key, values, own),
        jax.ShapeDtypeStruct((2 * WINDOW, values.shape[1]), BF16),
        [pltpu.SemaphoreType.DMA((2,))],
        far=(0, 1),
        free=(2,),
        name="edge",
        us=0.4,
    )
    halo = lax.ppermute(edge, "seq", [(i, i + 1) for i in range(count - 1)])

    phi, token = call(
        query_kernel,
        (q_feat, k_feat, cum, query_table(width), edge),
        [jax.ShapeDtypeStruct((heads, rows, 256), BF16), wide(8, 128)],
        free=(4,),
        name="query_features",
        us=1.5,
    )
    total, before, keys, small = call(
        lambda *refs: group_kernel(width, *refs),
        (place, conv_weight, table, own, *others, token),
        [shape, wide(3, quarter, ROWS, 128), wide(2, quarter, ROWS, 128), wide(quarter, 8, 128)],
        [held],
        smem=(0,),
        free=(7,),
        name="merge_group",
        us=2.0,
    )
    base = jnp.zeros_like(total)
    live = position < 0
    distance = 4
    last = total
    while distance < count:
        got = swap(total, distance)
        upper = (position & distance) > 0

        def pair(left, right):
            return call(
                lambda *refs: pair_kernel(width, *refs),
                (place, conv_weight, table, left, right),
                shape,
                smem=(0,),
                name="merge_pair",
            )

        if distance == 4:
            base = got
        else:
            base = jnp.where(upper, jnp.where(live, pair(got, base), got), base)
        live = live | upper
        if 2 * distance < count:
            total = pair(jnp.where(upper, got, total), jnp.where(upper, total, got))
        distance *= 2
    num, den, token = call(
        block_kernel,
        (q_feat, k_feat, values, conv_weight, cum, last),
        [wide(*values.shape)] * 2 + [wide(8, 128)],
        free=(5,),
        name="block",
        us=2.7,
    )
    here, *sent = call(
        spread_kernel,
        (place, conv_weight, base, before, keys, small, token),
        [shape] * 4,
        [held],
        smem=(0,),
        free=(6,),
        name="spread",
        us=1.0,
    )
    prefixes = [here] + [swap(x, d) for d, x in zip((1, 2, 3), sent)]
    win = call(
        window_kernel,
        (place, win_query, win_key, values, halo, here),
        wide(*values.shape),
        smem=(0,),
        free=(5,),
        name="window",
        us=2.6,
    )
    return call(
        finish_kernel,
        (place, phi, *prefixes, num, den, win),
        jax.ShapeDtypeStruct(values.shape, BF16),
        [held],
        smem=(0,),
        name="finish",
        us=2.1,
    )


def solution(mesh):
    rows = P(("grp", "seq"), "head")
    count = mesh.shape["seq"]
    return jax.shard_map(
        lambda *args: local(count, *args),
        mesh=mesh,
        in_specs=(rows,) * 6 + (P(None, "head"),),
        out_specs=rows,
        check_vma=False,
    )
```

```python
import numpy as np
import jax
import jax.numpy as jnp
from jax import lax
from jax.experimental import pallas as pl
from jax.experimental.pallas import tpu as pltpu
from jax.sharding import PartitionSpec as P

WINDOW = 64
ROWS = 160
EDGE = 158
LOG2E = float(np.log2(np.e))
F32 = jnp.float32
BF16 = jnp.bfloat16
VMEM_LIMIT = 24 * 1024 * 1024


def feature_tables(width):
    first = -np.ones(ROWS, np.int32)
    second = -np.ones(ROWS, np.int32)
    scale = np.zeros(ROWS, np.float32)
    twice = np.ones(ROWS, np.float32)
    scale[0] = 1.0
    at = 1
    for i in range(width):
        first[at], scale[at] = i, width ** (-0.25)
        at += 1
    for i in range(width):
        for j in range(i, width):
            first[at], second[at], scale[at] = i, j, (2.0 * width) ** (-0.5)
            twice[at] = 1.0 if i == j else 2.0
            at += 1
    one_a = ((first < 0) & (scale > 0)).astype(np.float32)
    one_b = ((second < 0) & (scale > 0)).astype(np.float32)
    return first, second, one_a, one_b, scale, twice


def key_table(width):
    first, second, one_a, one_b, scale, _ = feature_tables(width)
    table = np.zeros((ROWS, 128), np.float32)
    table[:, :5] = np.stack([first, second, one_a, one_b, scale], axis=1)
    return jnp.asarray(np.where(table < 0, -1000, table), F32)


def wide_rows(width):
    half = width // 2
    pair = lambda i, j: i * width + j if i < half else half * width + (i - half) * half + j - half
    linear = half * width + half * half
    return pair, linear, linear + width


def picks(width):
    first, second, _, _, _, twice = feature_tables(width)
    pair, linear, constant = wide_rows(width)
    keys = np.zeros((ROWS, constant + 16), np.float32)
    keys[0, constant] = 1.0
    for row in range(1, ROWS):
        if second[row] >= 0:
            keys[row, pair(first[row], second[row])] = 1.0
        elif first[row] >= 0:
            keys[row, linear + first[row]] = 1.0
    queries = keys * twice[:, None]
    queries[EDGE, constant + 1] = 1.0
    queries[EDGE + 1, constant + 2] = 1.0
    return jnp.asarray(keys, BF16), jnp.asarray(queries, BF16)


def products(x, factor):
    width = x.shape[0]
    half = width // 2
    scaled = x * (factor * (2.0 * width) ** (-0.5))
    blocks = [x * scaled[i : i + 1] for i in range(half)]
    blocks += [x[half:] * scaled[i : i + 1] for i in range(half, width)]
    return blocks + [x * (factor * width ** (-0.25))]


def nt(a, b):
    return lax.dot_general(a, b, (((1,), (1,)), ((), ())), preferred_element_type=F32)


def nn(a, b):
    return lax.dot_general(a, b, (((1,), (0,)), ((), ())), preferred_element_type=F32)


def tn(a, b):
    return lax.dot_general(a, b, (((0,), (0,)), ((), ())), preferred_element_type=F32)


def parts(wide):
    upper = wide.astype(BF16)
    rest = wide - upper.astype(F32)
    middle = rest.astype(BF16)
    lower = (rest - middle.astype(F32)).astype(BF16)
    return upper, middle, lower


def iota(shape, dim):
    return lax.broadcasted_iota(jnp.int32, shape, dim)


def cumulative_rows(gates):
    heads, rows = gates.shape
    upto = (iota((128, 128), 0) <= iota((128, 128), 1)).astype(BF16)
    blocks = [gates[:, i : i + 128] for i in range(0, rows, 128)]
    stacked = jnp.concatenate([piece for block in blocks for piece in parts(block)], axis=0)
    inside = nn(stacked, upto)
    done, before = [], 0.0
    for i in range(len(blocks)):
        three = [inside[(3 * i + p) * heads : (3 * i + p + 1) * heads] for p in range(3)]
        done.append(three[0] + three[1] + three[2] + before)
        before = done[-1][:, 127:]
    return jnp.concatenate(done, axis=1)


def columns_of(table_ref):
    return [jnp.broadcast_to(table_ref[:, i : i + 1], (ROWS, 128)) for i in range(5)]


def shifted(x, by):
    return jnp.where(iota(x.shape, 0) < by, 0.0, pltpu.roll(x, by, 0))


def one_state(head, out_ref, j, k_ref, turned_ref, v_ref, w_ref, cum_ref, norm_ref, pick):
    rows, wide = k_ref.shape
    heads = cum_ref.shape[0]
    width = wide // heads
    lane1 = iota((1, 128), 1)
    sub = iota((8, 128), 0)
    at = pl.ds(pl.multiple_of(head * 128, 128), 128)
    cum = cum_ref[pl.ds(head, 1), :]
    last = cum[:, rows - 1 :]
    keep = jnp.exp(last - cum)
    k = turned_ref[pl.ds(pl.multiple_of(head * width, width), width), :]
    constant = jnp.where(iota((16, rows), 0) == 0, keep, 0.0)
    phi = jnp.concatenate(products(k, keep) + [constant]).astype(BF16)
    v = v_ref[:, at].astype(F32)
    w = w_ref[:, at]
    conv = (w[0:1] * v + w[1:2] * shifted(v, 1) + w[2:3] * shifted(v, 2)).astype(BF16)
    state = nn(pick, nn(phi, conv).astype(BF16))
    norm = nt(jnp.ones((8, rows), BF16), phi)
    high = norm.astype(BF16).astype(F32)
    norm = jnp.where(iota(norm.shape, 0) == 0, high, norm - high).astype(BF16)
    norm_ref[j, :, 0:ROWS] = nt(norm, pick)
    high, low = norm_ref[j, 0:1, :], norm_ref[j, 1:2, :]
    keys8 = k_ref[0:16].astype(F32)[0:8]
    turned = pltpu.roll(keys8, (wide - head * width) % wide, 1)
    turned2 = pltpu.roll(keys8, (wide - head * width + width) % wide, 1)
    misc = jnp.where(lane1 < width, turned[0:1], 0.0)
    misc = jnp.where((lane1 >= width) & (lane1 < 2 * width), turned2[1:2], misc)
    place = 2 * width
    for value in (keep[:, 0:1], keep[:, 1:2], jnp.exp(last)):
        for piece in parts(value):
            misc = jnp.where(lane1 == place, piece.astype(F32), misc)
            place += 1
    tail = state[ROWS - 8 :]
    for row, line in enumerate((high[:, :128], high[:, 128:], low[:, :128], low[:, 128:], misc)):
        tail = jnp.where(sub == row + 1, line, tail)
    tail = jnp.where(sub >= 6, v[rows - 8 :], tail)
    out_ref[j, 0 : ROWS - 16, :] = state[: ROWS - 16].astype(BF16)
    out_ref[j, ROWS - 16 :, :] = jnp.concatenate([state[ROWS - 16 : ROWS - 8], tail]).astype(BF16)


def open_kernel(place_ref, token_ref):
    token_ref[...] = jnp.zeros(token_ref.shape, F32)


def gate_kernel(g_ref, k_ref, after_ref, cum_ref, turned_ref):
    cum_ref[...] = cumulative_rows(g_ref[...])
    turned_ref[...] = k_ref[...].astype(F32).T


def state_kernel(order, place_ref, k_ref, turned_ref, v_ref, cum_ref, w_ref, pick_ref, after_ref, *refs):
    outs, norm_ref = refs[:-1], refs[-1]
    norm_ref[...] = jnp.zeros(norm_ref.shape, F32)
    pick = pick_ref[...]
    for i, (out_ref, distance) in enumerate(zip(outs, order)):
        count = out_ref.shape[0]
        for j in range(count):
            head = ((place_ref[0] & 3) ^ distance) * count + j
            one_state(head, out_ref, j, k_ref, turned_ref, v_ref, w_ref, cum_ref, norm_ref.at[i], pick)


def own_kernel(place_ref, k_ref, turned_ref, v_ref, cum_ref, w_ref, pick_ref, after_ref, win_key_ref, out_ref, edge_ref, norm_ref):
    edge_ref[:WINDOW] = win_key_ref[win_key_ref.shape[0] - WINDOW :]
    edge_ref[WINDOW:] = v_ref[v_ref.shape[0] - WINDOW :]
    state_kernel((0,), place_ref, k_ref, turned_ref, v_ref, cum_ref, w_ref, pick_ref, after_ref, out_ref, norm_ref)


def tail_of(tile):
    return tile[ROWS - 8 :]


def value_of(tile, i, width):
    lane1 = iota((1, 128), 1)
    place = 2 * width + 3 * i
    here = (lane1 >= place) & (lane1 < place + 3)
    return jnp.sum(jnp.where(here, tail_of(tile)[5:6], 0.0), axis=1, keepdims=True)


def first_keys(tiles, table, width):
    lane = iota((ROWS, 128), 1).astype(F32)
    lines = [tail_of(tile)[5:6] for tile in tiles]
    rows = jnp.concatenate(lines + [jnp.zeros((8 - len(lines), 128), F32)] if len(lines) < 8 else lines).astype(BF16)
    first, second, one_a, one_b, scale = table
    found = []
    for token in range(2):
        pick_a = (lane == first + token * width).astype(BF16)
        pick_b = (lane == second + token * width).astype(BF16)
        found.append((nt(pick_a, rows) + one_a[:, 0:8]) * (nt(pick_b, rows) + one_b[:, 0:8]) * scale[:, 0:8])
    return found


def carried(tile, w):
    tail = tail_of(tile)
    return w[1:2] * tail[7:8] + w[2:3] * tail[6:7], w[2:3] * tail[7:8]


def seam(left, columns, enter, w):
    carry0, carry1 = carried(left, w)
    return columns[0] * (enter[0] * carry0) + columns[1] * (enter[1] * carry1)


def merge(left, right, columns, w, width):
    decay = value_of(right, 2, width)
    joined = decay * left + right + seam(left, columns, (value_of(right, 0, width), value_of(right, 1, width)), w)
    sub = iota((8, 128), 0)
    lane1 = iota((1, 128), 1)
    misc = tail_of(left)[5:6]
    misc = jnp.where(lane1 < 2 * width, misc, misc * decay)
    tail = jnp.where(sub == 5, misc, tail_of(joined))
    tail = jnp.where(sub >= 6, tail_of(right), tail)
    return jnp.concatenate([joined[: ROWS - 8], tail])


def packed(tile, width):
    tail = tail_of(tile)
    sub = iota((8, 128), 0)
    lane1 = iota((1, 128), 1)
    misc = tail[5:6]
    fresh = jnp.where(lane1 < 2 * width, misc, 0.0)
    place = 2 * width
    for i in range(3):
        for piece in parts(value_of(tile, i, width)):
            fresh = jnp.where(lane1 == place, piece.astype(F32), fresh)
            place += 1
    tail = jnp.where(sub == 5, fresh, norm_parts(tail))
    return jnp.concatenate([tile[: ROWS - 8], tail]).astype(BF16)


def norm_parts(tail):
    sub = iota((8, 128), 0)
    for row in (1, 2):
        norm = tail[row : row + 1] + tail[row + 2 : row + 3]
        high = norm.astype(BF16).astype(F32)
        tail = jnp.where(sub == row, high, jnp.where(sub == row + 2, norm - high, tail))
    return tail


def head_taps(w_ref, head):
    return w_ref[:, pl.ds(pl.multiple_of(head * 128, 128), 128)]


def group_kernel(width, place_ref, w_ref, table_ref, x0, x1, x2, x3, after_ref, total_ref, before_ref, keys_ref, small_ref, held):
    group = (place_ref[0] & 3)
    count = x0.shape[0]
    for distance, ref in enumerate((x0, x1, x2, x3)):
        held[group ^ distance] = ref[...]
    tiles = [[held[p, j].astype(F32) for j in range(count)] for p in range(4)]
    columns = first_keys([tiles[p][j] for p in range(4) for j in range(count)], columns_of(table_ref), width)
    sub = iota((8, 128), 0)
    for j in range(count):
        w = head_taps(w_ref, group * count + j)
        so_far = tiles[0][j]
        for p in range(1, 4):
            before_ref[p - 1, j] = so_far
            pick = p * count + j
            so_far = merge(so_far, tiles[p][j], [c[:, pick : pick + 1] for c in columns], w, width)
        total_ref[j] = packed(so_far, width)
        for token in range(2):
            keys_ref[token, j] = jnp.broadcast_to(columns[token][:, j : j + 1], (ROWS, 128))
        decays = [value_of(tiles[p][j], 2, width) for p in range(3)]
        small = jnp.zeros((8, 128), F32)
        lines = decays[0], value_of(tiles[0][j], 0, width), value_of(tiles[0][j], 1, width), decays[1], decays[1] * decays[2]
        for row, value in enumerate(lines):
            small = jnp.where(sub == row, value, small)
        small_ref[j] = small


def pair_kernel(width, place_ref, w_ref, table_ref, left_ref, right_ref, out_ref):
    count = left_ref.shape[0]
    rights = [right_ref[j].astype(F32) for j in range(count)]
    columns = first_keys(rights, columns_of(table_ref), width)
    for j in range(count):
        w = head_taps(w_ref, (place_ref[0] & 3) * count + j)
        left = left_ref[j].astype(F32)
        out_ref[j] = packed(merge(left, rights[j], [c[:, j : j + 1] for c in columns], w, width), width)


def with_edge(tile, source, w):
    carry0, carry1 = carried(source, w)
    sub = iota((8, 128), 0)
    tail = norm_parts(tail_of(tile))
    tail = jnp.where(sub == 6, carry0, jnp.where(sub == 7, carry1, tail))
    return jnp.concatenate([tile[: ROWS - 8], tail]).astype(BF16)


def spread_kernel(place_ref, w_ref, base_ref, before_ref, keys_ref, small_ref, after_ref, o0, o1, o2, o3, held):
    group = (place_ref[0] & 3)
    live = place_ref[0] > 3
    count = base_ref.shape[0]
    for j in range(count):
        w = head_taps(w_ref, group * count + j)
        base = jnp.where(live, base_ref[j].astype(F32), 0.0)
        held[0, j] = with_edge(base, base, w)
        small = small_ref[j]
        through = small[0:1] * base + seam(base, (keys_ref[0, j], keys_ref[1, j]), (small[1:2], small[2:3]), w)
        for p in range(3):
            tile = before_ref[p, j] + (through if p == 0 else small[2 + p : 3 + p] * through)
            held[p + 1, j] = with_edge(tile, before_ref[p, j], w)
    for distance, ref in enumerate((o0, o1, o2, o3)):
        ref[...] = held[group ^ distance]


def window_kernel(place_ref, wq_ref, wk_ref, v_ref, halo_ref, after_ref, win_ref):
    rows = wq_ref.shape[0]
    half = WINDOW
    seen = iota((half, 2 * half), 1)
    mine = iota((half, 2 * half), 0)
    valid = (seen > mine) & (seen <= mine + half)
    start = valid & ((seen >= half) | (place_ref[0] > 0))
    steps = rows // half
    ones = jnp.ones((rows + half, 128), BF16)
    zeros = jnp.zeros((rows + half, 128), BF16)
    heads = wq_ref.shape[1] // 128
    spans = [slice(i * half, (i + 2) * half) for i in range(steps)]
    for four in range(0, heads, 4):
        scores = []
        for h in range(four, four + 4, 2):
            one, two = slice(128 * h, 128 * h + 128), slice(128 * h + 128, 128 * h + 256)
            upper = jnp.concatenate([jnp.concatenate([halo_ref[:half, one], wk_ref[:, one]]), zeros], axis=1)
            lower = jnp.concatenate([zeros, jnp.concatenate([halo_ref[:half, two], wk_ref[:, two]])], axis=1)
            queries = wq_ref[:, 128 * h : 128 * h + 256]
            s = [nt(queries[i * half : (i + 1) * half], jnp.concatenate([upper[span], lower[span]])) for i, span in enumerate(spans)]
            scores += [[x[:, :128] for x in s], [x[:, 128:] for x in s]]
        probs = []
        for s in scores:
            s = jnp.concatenate([jnp.where(valid if i else start, x * (128 ** (-0.5) * LOG2E), -jnp.inf) for i, x in enumerate(s)])
            probs.append(jnp.exp2(s - jnp.max(s, axis=1, keepdims=True)).astype(BF16))
        for h, p in zip(range(four, four + 4), probs):
            at = slice(128 * h, 128 * h + 128)
            right = jnp.concatenate([jnp.concatenate([halo_ref[half:, at], v_ref[:, at]]), ones], axis=1)
            both = jnp.concatenate([nn(p[i * half : (i + 1) * half], right[span]) for i, span in enumerate(spans)])
            win_ref[:, at] = both[:, :128] / both[:, 128:]


def block_kernel(q_ref, turned_ref, v_ref, w_ref, cum_ref, after_ref, num_ref, den_ref, token_ref):
    rows, wide = q_ref.shape
    heads = cum_ref.shape[0]
    width = wide // heads
    q = q_ref[...]
    cum_row = cum_ref[...] * LOG2E
    cum_col = cum_row.T
    token_ref[...] = jnp.zeros(token_ref.shape, F32)
    level = iota(turned_ref.shape, 0)
    step, piece = 256, 128
    ones = jnp.ones((rows, 128), BF16)
    causal = iota((piece, piece), 0) >= iota((piece, piece), 1)
    for h in range(heads):
        at = slice(128 * h, 128 * h + 128)
        here = (level >= h * width) & (level < (h + 1) * width)
        k_here = jnp.where(here, turned_ref[...] * width ** (-0.5), 0.0).astype(BF16)
        v = v_ref[:, at].astype(F32)
        w = w_ref[:, at]
        conv = w[0:1] * v + w[1:2] * shifted(v, 1) + w[2:3] * shifted(v, 2)
        right = jnp.concatenate([conv.astype(BF16), ones], axis=1)
        column = jnp.broadcast_to(cum_col[:, h : h + 1], (rows, piece))
        total = None
        for low in range(0, rows, step):
            x = nn(q[low:], k_here[:, low : low + step])
            lines = []
            for i in range(low, rows, piece):
                line = []
                for j in range(low, low + step, piece):
                    if j > i:
                        line.append(jnp.zeros((piece, piece), BF16))
                        continue
                    here = x[i - low : i - low + piece, j - low : j - low + piece]
                    gap = column[i : i + piece] - cum_row[h : h + 1, j : j + piece]
                    if i == j:
                        gap = jnp.where(causal, gap, -jnp.inf)
                    line.append((((0.5 * here + 1.0) * here + 1.0) * jnp.exp2(gap)).astype(BF16))
                lines.append(jnp.concatenate(line, axis=1))
            both = nn(jnp.concatenate(lines), right[low : low + step])
            total = both if total is None else jnp.concatenate([total[:low], total[low:] + both])
        num_ref[:, at] = total[:, :128]
        den_ref[:, at] = total[:, 128:]


def query_kernel(q_ref, k_ref, cum_ref, pick_ref, after_ref, out_ref):
    rows, wide = q_ref.shape
    heads = cum_ref.shape[0]
    width = wide // heads
    q = q_ref[...]
    turned = q.astype(F32).T
    pick = pick_ref[...]
    keys = k_ref[0:16].astype(F32)[0:8] * width ** (-0.5)
    line = iota((2 * heads, wide), 0)
    lane = iota((2 * heads, wide), 1)
    keys = jnp.where(line < heads, keys[0:1], keys[1:2])
    low = jnp.where(line < heads, line, line - heads) * width
    x = nt(jnp.where((lane >= low) & (lane < low + width), keys, 0.0).astype(BF16), q)
    x = (0.5 * x + 1.0) * x + 1.0
    sub = iota((16, rows), 0)
    at = iota((1, rows), 1)
    for h in range(heads):
        cum = cum_ref[h : h + 1, :]
        enter = jnp.exp(cum)
        score0 = x[h : h + 1] * jnp.exp(cum - cum[:, 0:1])
        score1 = x[heads + h : heads + h + 1] * jnp.exp(jnp.where(at < 1, -jnp.inf, cum - cum[:, 1:2]))
        rest = jnp.where(sub == 0, enter, jnp.where(sub == 1, score0, jnp.where(sub == 2, score1, 0.0)))
        phi = jnp.concatenate(products(turned[h * width : (h + 1) * width], enter) + [rest]).astype(BF16)
        out_ref[h, :, 0:ROWS] = nn(pick, phi).astype(BF16).T


def finish_kernel(place_ref, phi_ref, x0, x1, x2, x3, num_ref, den_ref, win_ref, out_far, held, out_ref, sems):
    group = (place_ref[0] & 3)
    heads = phi_ref.shape[0]
    count = x0.shape[0]
    for distance, ref in enumerate((x0, x1, x2, x3)):
        held[group ^ distance] = ref[...]
    tiles = [held[h // count, h % count] for h in range(heads)]
    lines = []
    for tile in tiles:
        tail = tile[ROWS - 16 :].astype(F32)[8:]
        lines.append(jnp.concatenate([tail[1:2] + tail[3:4], tail[2:3] + tail[4:5]], axis=1))
    norms = jnp.concatenate(lines).T
    copies = []
    for h in range(heads):
        at = slice(128 * h, 128 * h + 128)
        norm = jnp.broadcast_to(norms[:ROWS, h : h + 1], (ROWS, 128)).astype(BF16)
        both = nn(phi_ref[h][:, :ROWS], jnp.concatenate([tiles[h], norm], axis=1))
        out = (num_ref[:, at] + both[:, :128]) / (den_ref[:, at] + both[:, 128:]) + win_ref[:, at]
        out_ref[h] = out.astype(BF16)
        copies.append(pltpu.make_async_copy(out_ref.at[h], out_far.at[:, pl.ds(128 * h, 128)], sems.at[h]))
        copies[-1].start()
    for copy in copies:
        copy.wait()


def call(kernel, inputs, outs, scratch=(), smem=(), free=(), far=(), name=None, us=1.0, out_space=pltpu.VMEM):
    def space(i):
        return pltpu.SMEM if i in smem else pl.ANY if i in free else pltpu.HBM if i in far else pltpu.VMEM

    return pl.pallas_call(
        kernel,
        out_shape=outs,
        in_specs=[pl.BlockSpec(memory_space=space(i)) for i in range(len(inputs))],
        out_specs=jax.tree.map(lambda _: pl.BlockSpec(memory_space=out_space), outs),
        scratch_shapes=scratch,
        compiler_params=pltpu.CompilerParams(vmem_limit_bytes=VMEM_LIMIT),
        name=name,
        cost_estimate=pl.CostEstimate(flops=int(us * 3e9), bytes_accessed=int(us * 9e6), transcendentals=0),
    )(*inputs)


def local(count, q_feat, k_feat, values, win_query, win_key, log_gates, conv_weight):
    rows = values.shape[0]
    heads = log_gates.shape[1]
    width = q_feat.shape[1] // heads
    quarter = heads // 4
    position = lax.axis_index("seq")
    one = lambda number: jnp.reshape(number, (1,)).astype(jnp.int32)
    place = one(position)
    table = key_table(width)
    pick_keys, pick_queries = picks(width)
    shape = jax.ShapeDtypeStruct((quarter, ROWS, 128), BF16)
    wide = lambda *dims: jax.ShapeDtypeStruct(dims, F32)
    held = pltpu.VMEM((4, quarter, ROWS, 128), BF16)

    def swap(x, distance):
        return lax.ppermute(x, "seq", [(i, i ^ distance) for i in range(count)])

    token = call(open_kernel, (place,), wide(8, 128), smem=(0,), name="open", us=6.0)
    cum, turned = call(
        gate_kernel,
        (log_gates.T, k_feat, token),
        [wide(heads, rows), wide(k_feat.shape[1], rows)],
        free=(2,),
        name="gates",
        us=0.01,
    )

    sent = call(
        lambda *refs: state_kernel((1, 2, 3), *refs),
        (place, k_feat, turned, values, cum, conv_weight, pick_keys, cum),
        [shape] * 3,
        [pltpu.VMEM((3, quarter, 8, 256), F32)],
        smem=(0,),
        free=(7,),
        name="states",
        us=2.0,
    )
    others = [swap(x, d) for d, x in zip((1, 2, 3), sent)]
    own, edge = call(
        own_kernel,
        (place, k_feat, turned, values, cum, conv_weight, pick_keys, sent[0], win_key),
        [shape, jax.ShapeDtypeStruct((2 * WINDOW, values.shape[1]), BF16)],
        [pltpu.VMEM((1, quarter, 8, 256), F32)],
        smem=(0,),
        free=(7,),
        name="own_states",
        us=0.8,
    )
    halo = lax.ppermute(edge, "seq", [(i, i + 1) for i in range(count - 1)])

    total, before, keys, small = call(
        lambda *refs: group_kernel(width, *refs),
        (place, conv_weight, table, own, *others, edge),
        [shape, wide(3, quarter, ROWS, 128), wide(2, quarter, ROWS, 128), wide(quarter, 8, 128)],
        [held],
        smem=(0,),
        free=(7,),
        name="merge_group",
        us=2.0,
    )
    base = jnp.zeros_like(total)
    live = position < 0
    distance = 4
    last = total
    while distance < count:
        got = swap(total, distance)
        upper = (position & distance) > 0

        def pair(left, right):
            return call(
                lambda *refs: pair_kernel(width, *refs),
                (place, conv_weight, table, left, right),
                shape,
                smem=(0,),
                name="merge_pair",
            )

        if distance == 4:
            base = got
        else:
            base = jnp.where(upper, jnp.where(live, pair(got, base), got), base)
        live = live | upper
        if 2 * distance < count:
            total = pair(jnp.where(upper, got, total), jnp.where(upper, total, got))
        distance *= 2
    num, den, token = call(
        block_kernel,
        (q_feat, turned, values, conv_weight, cum, last),
        [wide(*values.shape)] * 2 + [wide(8, 128)],
        free=(5,),
        name="block",
        us=2.7,
    )
    here, *sent = call(
        spread_kernel,
        (place, conv_weight, base, before, keys, small, token),
        [shape] * 4,
        [held],
        smem=(0,),
        free=(6,),
        name="spread",
        us=1.0,
    )
    prefixes = [here] + [swap(x, d) for d, x in zip((1, 2, 3), sent)]
    phi = call(
        query_kernel,
        (q_feat, k_feat, cum, pick_queries, here),
        jax.ShapeDtypeStruct((heads, rows, 256), BF16),
        free=(4,),
        name="query_features",
        us=1.5,
    )
    win = call(
        window_kernel,
        (place, win_query, win_key, values, halo, phi),
        wide(*values.shape),
        smem=(0,),
        free=(5,),
        name="window",
        us=2.6,
    )
    return call(
        finish_kernel,
        (place, phi, *prefixes, num, den, win),
        jax.ShapeDtypeStruct(values.shape, BF16),
        [held, pltpu.VMEM((heads, rows, 128), BF16), pltpu.SemaphoreType.DMA((heads,))],
        smem=(0,),
        out_space=pltpu.HBM,
        name="finish",
        us=2.1,
    )


def solution(mesh):
    rows = P(("grp", "seq"), "head")
    count = mesh.shape["seq"]
    return jax.shard_map(
        lambda *args: local(count, *args),
        mesh=mesh,
        in_specs=(rows,) * 6 + (P(None, "head"),),
        out_specs=rows,
        check_vma=False,
    )
```

```python
import numpy as np
import jax
import jax.numpy as jnp
from jax import lax
from jax.experimental import pallas as pl
from jax.experimental.pallas import tpu as pltpu
from jax.sharding import PartitionSpec as P

WINDOW = 64
ROWS = 160
EDGE = 158
LOG2E = float(np.log2(np.e))
F32 = jnp.float32
BF16 = jnp.bfloat16
VMEM_LIMIT = 24 * 1024 * 1024


def feature_tables(width):
    first = -np.ones(ROWS, np.int32)
    second = -np.ones(ROWS, np.int32)
    scale = np.zeros(ROWS, np.float32)
    twice = np.ones(ROWS, np.float32)
    scale[0] = 1.0
    at = 1
    for i in range(width):
        first[at], scale[at] = i, width ** (-0.25)
        at += 1
    for i in range(width):
        for j in range(i, width):
            first[at], second[at], scale[at] = i, j, (2.0 * width) ** (-0.5)
            twice[at] = 1.0 if i == j else 2.0
            at += 1
    one_a = ((first < 0) & (scale > 0)).astype(np.float32)
    one_b = ((second < 0) & (scale > 0)).astype(np.float32)
    return first, second, one_a, one_b, scale, twice


def key_tables(width):
    first, second, one_a, one_b, scale, _ = feature_tables(width)
    pick = np.zeros((2, 2, ROWS, 128), np.float32)
    for token in range(2):
        for factor, index in enumerate((first, second)):
            for row in range(ROWS):
                if index[row] >= 0:
                    pick[token, factor, row, token * width + index[row]] = 1.0
    real = np.stack([np.repeat(x[:, None], 8, axis=1) for x in (one_a, one_b, scale)])
    return jnp.asarray(pick.reshape(4 * ROWS, 128), BF16), jnp.asarray(real, F32)


def wide_rows(width):
    half = width // 2
    pair = lambda i, j: i * width + j if i < half else half * width + (i - half) * half + j - half
    linear = half * width + half * half
    return pair, linear, linear + width


def picks(width):
    first, second, _, _, _, twice = feature_tables(width)
    pair, linear, constant = wide_rows(width)
    keys = np.zeros((ROWS, constant + 16), np.float32)
    keys[0, constant] = 1.0
    for row in range(1, ROWS):
        if second[row] >= 0:
            keys[row, pair(first[row], second[row])] = 1.0
        elif first[row] >= 0:
            keys[row, linear + first[row]] = 1.0
    queries = keys * twice[:, None]
    queries[EDGE, constant + 1] = 1.0
    queries[EDGE + 1, constant + 2] = 1.0
    return jnp.asarray(keys, BF16), jnp.asarray(queries, BF16)


def products(x, factor):
    width = x.shape[0]
    half = width // 2
    scaled = x * (factor * (2.0 * width) ** (-0.5))
    blocks = [x * scaled[i : i + 1] for i in range(half)]
    blocks += [x[half:] * scaled[i : i + 1] for i in range(half, width)]
    return blocks + [x * (factor * width ** (-0.25))]


def nt(a, b):
    return lax.dot_general(a, b, (((1,), (1,)), ((), ())), preferred_element_type=F32)


def nn(a, b):
    return lax.dot_general(a, b, (((1,), (0,)), ((), ())), preferred_element_type=F32)


def tn(a, b):
    return lax.dot_general(a, b, (((0,), (0,)), ((), ())), preferred_element_type=F32)


def parts(wide):
    upper = wide.astype(BF16)
    rest = wide - upper.astype(F32)
    middle = rest.astype(BF16)
    lower = (rest - middle.astype(F32)).astype(BF16)
    return upper, middle, lower


def iota(shape, dim):
    return lax.broadcasted_iota(jnp.int32, shape, dim)


def cumulative_rows(gates):
    heads, rows = gates.shape
    upto = (iota((128, 128), 0) <= iota((128, 128), 1)).astype(BF16)
    blocks = [gates[:, i : i + 128] for i in range(0, rows, 128)]
    stacked = jnp.concatenate([piece for block in blocks for piece in parts(block)], axis=0)
    inside = nn(stacked, upto)
    done, before = [], 0.0
    for i in range(len(blocks)):
        three = [inside[(3 * i + p) * heads : (3 * i + p + 1) * heads] for p in range(3)]
        done.append(three[0] + three[1] + three[2] + before)
        before = done[-1][:, 127:]
    return jnp.concatenate(done, axis=1)


def shifted(x, by):
    return jnp.where(iota(x.shape, 0) < by, 0.0, pltpu.roll(x, by, 0))


def quarter_states(quarter, out_ref, k_ref, turned_ref, v_ref, w_ref, cum_ref, norm_ref, pick):
    rows, wide = k_ref.shape
    heads = cum_ref.shape[0]
    width = wide // heads
    count = out_ref.shape[0]
    lane1 = iota((1, 128), 1)
    sub = iota((8, 128), 0)
    keys8 = k_ref[0:16].astype(F32)[0:8]
    wides, norms, values, keeps, lasts = [], [], [], [], []
    for j in range(count):
        head = quarter * count + j
        at = pl.ds(pl.multiple_of(head * 128, 128), 128)
        cum = cum_ref[pl.ds(head, 1), :]
        last = cum[:, rows - 1 :]
        keep = jnp.exp(last - cum)
        k = turned_ref[pl.ds(pl.multiple_of(head * width, width), width), :]
        constant = jnp.where(iota((16, rows), 0) == 0, keep, 0.0)
        phi = jnp.concatenate(products(k, keep) + [constant]).astype(BF16)
        v = v_ref[:, at].astype(F32)
        w = w_ref[:, at]
        conv = (w[0:1] * v + w[1:2] * shifted(v, 1) + w[2:3] * shifted(v, 2)).astype(BF16)
        wides.append(nn(phi, conv).astype(BF16))
        norms.append(nt(jnp.ones((8, rows), BF16), phi))
        values.append(v)
        keeps.append(keep)
        lasts.append(last)
    states = nn(pick, jnp.concatenate(wides, axis=1))
    line = iota(norms[0].shape, 0)
    mixed = jnp.zeros(norms[0].shape, F32)
    for j, norm in enumerate(norms):
        high = norm.astype(BF16).astype(F32)
        mixed = jnp.where(line == 2 * j, high, jnp.where(line == 2 * j + 1, norm - high, mixed))
    norm_ref[:, 0:ROWS] = nt(mixed.astype(BF16), pick)
    for j in range(count):
        head = quarter * count + j
        high, low = norm_ref[2 * j : 2 * j + 1, :], norm_ref[2 * j + 1 : 2 * j + 2, :]
        turned = pltpu.roll(keys8, (wide - head * width) % wide, 1)
        turned2 = pltpu.roll(keys8, (wide - head * width + width) % wide, 1)
        misc = jnp.where(lane1 < width, turned[0:1], 0.0)
        misc = jnp.where((lane1 >= width) & (lane1 < 2 * width), turned2[1:2], misc)
        place = 2 * width
        for value in (keeps[j][:, 0:1], keeps[j][:, 1:2], jnp.exp(lasts[j])):
            for piece in parts(value):
                misc = jnp.where(lane1 == place, piece.astype(F32), misc)
                place += 1
        state = states[:, 128 * j : 128 * j + 128]
        tail = state[ROWS - 8 :]
        for row, text in enumerate((high[:, :128], high[:, 128:], low[:, :128], low[:, 128:], misc)):
            tail = jnp.where(sub == row + 1, text, tail)
        tail = jnp.where(sub >= 6, values[j][rows - 8 :], tail)
        out_ref[j, 0 : ROWS - 16, :] = state[: ROWS - 16].astype(BF16)
        out_ref[j, ROWS - 16 :, :] = jnp.concatenate([state[ROWS - 16 : ROWS - 8], tail]).astype(BF16)


def open_kernel(place_ref, token_ref):
    token_ref[...] = jnp.zeros(token_ref.shape, F32)


def gate_kernel(g_ref, k_ref, after_ref, cum_ref, turned_ref):
    cum_ref[...] = cumulative_rows(g_ref[...])
    turned_ref[...] = k_ref[...].astype(F32).T


def state_kernel(order, place_ref, k_ref, turned_ref, v_ref, cum_ref, w_ref, pick_ref, after_ref, *refs):
    outs, norm_ref = refs[:-1], refs[-1]
    norm_ref[...] = jnp.zeros(norm_ref.shape, F32)
    pick = pick_ref[...]
    for i, (out_ref, distance) in enumerate(zip(outs, order)):
        quarter = (place_ref[0] & 3) ^ distance
        quarter_states(quarter, out_ref, k_ref, turned_ref, v_ref, w_ref, cum_ref, norm_ref.at[i], pick)


def edge_kernel(win_key_ref, v_ref, after_ref, edge_ref):
    edge_ref[:WINDOW] = win_key_ref[win_key_ref.shape[0] - WINDOW :]
    edge_ref[WINDOW:] = v_ref[v_ref.shape[0] - WINDOW :]


def tail_of(tile):
    return tile[ROWS - 8 :]


def value_of(tile, i, width):
    lane1 = iota((1, 128), 1)
    place = 2 * width + 3 * i
    here = (lane1 >= place) & (lane1 < place + 3)
    return jnp.sum(jnp.where(here, tail_of(tile)[5:6], 0.0), axis=1, keepdims=True)


def first_keys(tiles, pick_ref, real_ref):
    lines = [tail_of(tile)[5:6] for tile in tiles]
    rows = jnp.concatenate(lines + [jnp.zeros((8 - len(lines), 128), F32)] if len(lines) < 8 else lines).astype(BF16)
    found = nt(pick_ref[...], rows)
    factors = [found[i * ROWS : (i + 1) * ROWS] for i in range(4)]
    one_a, one_b, scale = (real_ref[i] for i in range(3))
    return [(factors[2 * t] + one_a) * (factors[2 * t + 1] + one_b) * scale for t in range(2)]


def carried(tile, w):
    tail = tail_of(tile)
    return w[1:2] * tail[7:8] + w[2:3] * tail[6:7], w[2:3] * tail[7:8]


def seam(left, columns, enter, w):
    carry0, carry1 = carried(left, w)
    return columns[0] * (enter[0] * carry0) + columns[1] * (enter[1] * carry1)


def merge(left, right, columns, w, width):
    decay = value_of(right, 2, width)
    joined = decay * left + right + seam(left, columns, (value_of(right, 0, width), value_of(right, 1, width)), w)
    sub = iota((8, 128), 0)
    lane1 = iota((1, 128), 1)
    misc = tail_of(left)[5:6]
    misc = jnp.where(lane1 < 2 * width, misc, misc * decay)
    tail = jnp.where(sub == 5, misc, tail_of(joined))
    tail = jnp.where(sub >= 6, tail_of(right), tail)
    return jnp.concatenate([joined[: ROWS - 8], tail])


def packed(tile, width):
    tail = tail_of(tile)
    sub = iota((8, 128), 0)
    lane1 = iota((1, 128), 1)
    misc = tail[5:6]
    fresh = jnp.where(lane1 < 2 * width, misc, 0.0)
    place = 2 * width
    for i in range(3):
        for piece in parts(value_of(tile, i, width)):
            fresh = jnp.where(lane1 == place, piece.astype(F32), fresh)
            place += 1
    tail = jnp.where(sub == 5, fresh, norm_parts(tail))
    return jnp.concatenate([tile[: ROWS - 8], tail]).astype(BF16)


def norm_parts(tail):
    sub = iota((8, 128), 0)
    for row in (1, 2):
        norm = tail[row : row + 1] + tail[row + 2 : row + 3]
        high = norm.astype(BF16).astype(F32)
        tail = jnp.where(sub == row, high, jnp.where(sub == row + 2, norm - high, tail))
    return tail


def head_taps(w_ref, head):
    return w_ref[:, pl.ds(pl.multiple_of(head * 128, 128), 128)]


def group_kernel(width, place_ref, w_ref, pick_ref, real_ref, x0, x1, x2, x3, after_ref, total_ref, before_ref, keys_ref, small_ref, held):
    group = (place_ref[0] & 3)
    count = x0.shape[0]
    for distance, ref in enumerate((x0, x1, x2, x3)):
        held[group ^ distance] = ref[...]
    tiles = [[held[p, j].astype(F32) for j in range(count)] for p in range(4)]
    columns = first_keys([tiles[p][j] for p in range(4) for j in range(count)], pick_ref, real_ref)
    sub = iota((8, 128), 0)
    for j in range(count):
        w = head_taps(w_ref, group * count + j)
        so_far = tiles[0][j]
        for p in range(1, 4):
            before_ref[p - 1, j] = so_far
            pick = p * count + j
            so_far = merge(so_far, tiles[p][j], [c[:, pick : pick + 1] for c in columns], w, width)
        total_ref[j] = packed(so_far, width)
        for token in range(2):
            keys_ref[token, j] = jnp.broadcast_to(columns[token][:, j : j + 1], (ROWS, 128))
        decays = [value_of(tiles[p][j], 2, width) for p in range(3)]
        small = jnp.zeros((8, 128), F32)
        lines = decays[0], value_of(tiles[0][j], 0, width), value_of(tiles[0][j], 1, width), decays[1], decays[1] * decays[2]
        for row, value in enumerate(lines):
            small = jnp.where(sub == row, value, small)
        small_ref[j] = small


def pair_kernel(width, place_ref, w_ref, pick_ref, real_ref, left_ref, right_ref, out_ref):
    count = left_ref.shape[0]
    rights = [right_ref[j].astype(F32) for j in range(count)]
    columns = first_keys(rights, pick_ref, real_ref)
    for j in range(count):
        w = head_taps(w_ref, (place_ref[0] & 3) * count + j)
        left = left_ref[j].astype(F32)
        out_ref[j] = packed(merge(left, rights[j], [c[:, j : j + 1] for c in columns], w, width), width)


def with_edge(tile, source, w):
    carry0, carry1 = carried(source, w)
    sub = iota((8, 128), 0)
    tail = norm_parts(tail_of(tile))
    tail = jnp.where(sub == 6, carry0, jnp.where(sub == 7, carry1, tail))
    return jnp.concatenate([tile[: ROWS - 8], tail]).astype(BF16)


def spread_kernel(place_ref, w_ref, base_ref, before_ref, keys_ref, small_ref, after_ref, o0, o1, o2, o3, held):
    group = (place_ref[0] & 3)
    live = place_ref[0] > 3
    count = base_ref.shape[0]
    for j in range(count):
        w = head_taps(w_ref, group * count + j)
        base = jnp.where(live, base_ref[j].astype(F32), 0.0)
        held[0, j] = with_edge(base, base, w)
        small = small_ref[j]
        through = small[0:1] * base + seam(base, (keys_ref[0, j], keys_ref[1, j]), (small[1:2], small[2:3]), w)
        for p in range(3):
            tile = before_ref[p, j] + (through if p == 0 else small[2 + p : 3 + p] * through)
            held[p + 1, j] = with_edge(tile, before_ref[p, j], w)
    for distance, ref in enumerate((o0, o1, o2, o3)):
        ref[...] = held[group ^ distance]


def windowed(wq_ref, keys, values, valid, out_ref):
    half = WINDOW
    rows = wq_ref.shape[0]
    steps = rows // half
    ones = jnp.ones((rows + half, 128), BF16)
    zeros = jnp.zeros((rows + half, 128), BF16)
    heads = wq_ref.shape[1] // 128
    spans = [slice(i * half, (i + 2) * half) for i in range(steps)]
    for four in range(0, heads, 4):
        scores = []
        for h in range(four, four + 4, 2):
            one, two = slice(128 * h, 128 * h + 128), slice(128 * h + 128, 128 * h + 256)
            upper = jnp.concatenate([keys(one), zeros], axis=1)
            lower = jnp.concatenate([zeros, keys(two)], axis=1)
            queries = wq_ref[:, 128 * h : 128 * h + 256]
            s = [nt(queries[i * half : (i + 1) * half], jnp.concatenate([upper[span], lower[span]])) for i, span in enumerate(spans)]
            scores += [[x[:, :128] for x in s], [x[:, 128:] for x in s]]
        probs = []
        for s in scores:
            s = jnp.concatenate([jnp.where(valid, x * (128 ** (-0.5) * LOG2E), -jnp.inf) for x in s])
            probs.append(jnp.exp2(s - jnp.max(s, axis=1, keepdims=True)).astype(BF16))
        for h, p in zip(range(four, four + 4), probs):
            at = slice(128 * h, 128 * h + 128)
            right = jnp.concatenate([values(at), ones], axis=1)
            both = jnp.concatenate([nn(p[i * half : (i + 1) * half], right[span]) for i, span in enumerate(spans)])
            out_ref[:, at] = both[:, :128] / both[:, 128:]


def window_masks():
    seen = iota((WINDOW, 2 * WINDOW), 1)
    mine = iota((WINDOW, 2 * WINDOW), 0)
    return (seen > mine) & (seen <= mine + WINDOW), seen >= WINDOW


def window_kernel(wq_ref, wk_ref, v_ref, after_ref, win_ref):
    valid, _ = window_masks()
    windowed(wq_ref.at[pl.ds(WINDOW, win_ref.shape[0])], lambda at: wk_ref[:, at], lambda at: v_ref[:, at], valid, win_ref)


def early_kernel(place_ref, wq_ref, wk_ref, v_ref, halo_ref, after_ref, win_ref):
    valid, own = window_masks()
    valid = valid & (own | ((place_ref[0]) > 0))
    keys = lambda at: jnp.concatenate([halo_ref[:WINDOW, at], wk_ref[:WINDOW, at]])
    values = lambda at: jnp.concatenate([halo_ref[WINDOW:, at], v_ref[:WINDOW, at]])
    windowed(wq_ref.at[pl.ds(0, WINDOW)], keys, values, valid, win_ref)


def block_kernel(q_ref, turned_ref, v_ref, w_ref, cum_ref, after_ref, num_ref, den_ref, token_ref):
    rows, wide = q_ref.shape
    heads = cum_ref.shape[0]
    width = wide // heads
    q = q_ref[...]
    cum_row = cum_ref[...] * LOG2E
    cum_col = cum_row.T
    token_ref[...] = jnp.zeros(token_ref.shape, F32)
    level = iota(turned_ref.shape, 0)
    step, piece = 256, 128
    ones = jnp.ones((rows, 128), BF16)
    causal = iota((piece, piece), 0) >= iota((piece, piece), 1)
    for h in range(heads):
        at = slice(128 * h, 128 * h + 128)
        here = (level >= h * width) & (level < (h + 1) * width)
        k_here = jnp.where(here, turned_ref[...] * width ** (-0.5), 0.0).astype(BF16)
        v = v_ref[:, at].astype(F32)
        w = w_ref[:, at]
        conv = w[0:1] * v + w[1:2] * shifted(v, 1) + w[2:3] * shifted(v, 2)
        right = jnp.concatenate([conv.astype(BF16), ones], axis=1)
        column = jnp.broadcast_to(cum_col[:, h : h + 1], (rows, piece))
        total = None
        for low in range(0, rows, step):
            x = nn(q[low:], k_here[:, low : low + step])
            lines = []
            for i in range(low, rows, piece):
                line = []
                for j in range(low, low + step, piece):
                    if j > i:
                        line.append(jnp.zeros((piece, piece), BF16))
                        continue
                    here = x[i - low : i - low + piece, j - low : j - low + piece]
                    gap = column[i : i + piece] - cum_row[h : h + 1, j : j + piece]
                    if i == j:
                        gap = jnp.where(causal, gap, -jnp.inf)
                    line.append((((0.5 * here + 1.0) * here + 1.0) * jnp.exp2(gap)).astype(BF16))
                lines.append(jnp.concatenate(line, axis=1))
            both = nn(jnp.concatenate(lines), right[low : low + step])
            total = both if total is None else jnp.concatenate([total[:low], total[low:] + both])
        num_ref[:, at] = total[:, :128]
        den_ref[:, at] = total[:, 128:]


def query_kernel(q_ref, k_ref, cum_ref, pick_ref, after_ref, out_ref, token_ref):
    rows, wide = q_ref.shape
    heads = cum_ref.shape[0]
    width = wide // heads
    q = q_ref[...]
    turned = q.astype(F32).T
    token_ref[...] = jnp.zeros(token_ref.shape, F32)
    pick = pick_ref[...]
    keys = k_ref[0:16].astype(F32)[0:8] * width ** (-0.5)
    line = iota((2 * heads, wide), 0)
    lane = iota((2 * heads, wide), 1)
    keys = jnp.where(line < heads, keys[0:1], keys[1:2])
    low = jnp.where(line < heads, line, line - heads) * width
    x = nt(jnp.where((lane >= low) & (lane < low + width), keys, 0.0).astype(BF16), q)
    x = (0.5 * x + 1.0) * x + 1.0
    sub = iota((16, rows), 0)
    at = iota((1, rows), 1)
    for h in range(heads):
        cum = cum_ref[h : h + 1, :]
        enter = jnp.exp(cum)
        score0 = x[h : h + 1] * jnp.exp(cum - cum[:, 0:1])
        score1 = x[heads + h : heads + h + 1] * jnp.exp(jnp.where(at < 1, -jnp.inf, cum - cum[:, 1:2]))
        rest = jnp.where(sub == 0, enter, jnp.where(sub == 1, score0, jnp.where(sub == 2, score1, 0.0)))
        phi = jnp.concatenate(products(turned[h * width : (h + 1) * width], enter) + [rest]).astype(BF16)
        out_ref[h, :, 0:ROWS] = nn(pick, phi).astype(BF16).T


def finish_kernel(place_ref, phi_ref, x0, x1, x2, x3, num_ref, den_ref, win_ref, early_ref, out_far, held, out_ref, sems):
    group = (place_ref[0] & 3)
    heads = phi_ref.shape[0]
    count = x0.shape[0]
    for distance, ref in enumerate((x0, x1, x2, x3)):
        held[group ^ distance] = ref[...]
    tiles = [held[h // count, h % count] for h in range(heads)]
    lines = []
    for tile in tiles:
        tail = tile[ROWS - 16 :].astype(F32)[8:]
        lines.append(jnp.concatenate([tail[1:2] + tail[3:4], tail[2:3] + tail[4:5]], axis=1))
    norms = jnp.concatenate(lines).T
    copies = []
    for h in range(heads):
        at = slice(128 * h, 128 * h + 128)
        norm = jnp.broadcast_to(norms[:ROWS, h : h + 1], (ROWS, 128)).astype(BF16)
        both = nn(phi_ref[h][:, :ROWS], jnp.concatenate([tiles[h], norm], axis=1))
        out = (num_ref[:, at] + both[:, :128]) / (den_ref[:, at] + both[:, 128:])
        out = out + jnp.concatenate([early_ref[:, at], win_ref[:, at]])
        out_ref[h] = out.astype(BF16)
        copies.append(pltpu.make_async_copy(out_ref.at[h], out_far.at[:, pl.ds(128 * h, 128)], sems.at[h]))
        copies[-1].start()
    for copy in copies:
        copy.wait()


def call(kernel, inputs, outs, scratch=(), smem=(), free=(), far=(), name=None, us=1.0, out_space=pltpu.VMEM):
    def space(i):
        return pltpu.SMEM if i in smem else pl.ANY if i in free else pltpu.HBM if i in far else pltpu.VMEM

    return pl.pallas_call(
        kernel,
        out_shape=outs,
        in_specs=[pl.BlockSpec(memory_space=space(i)) for i in range(len(inputs))],
        out_specs=jax.tree.map(lambda _: pl.BlockSpec(memory_space=out_space), outs),
        scratch_shapes=scratch,
        compiler_params=pltpu.CompilerParams(vmem_limit_bytes=VMEM_LIMIT),
        name=name,
        cost_estimate=pl.CostEstimate(flops=int(us * 3e9), bytes_accessed=int(us * 9e6), transcendentals=0),
    )(*inputs)


def local(count, q_feat, k_feat, values, win_query, win_key, log_gates, conv_weight):
    rows = values.shape[0]
    heads = log_gates.shape[1]
    width = q_feat.shape[1] // heads
    quarter = heads // 4
    position = lax.axis_index("seq")
    one = lambda number: jnp.reshape(number, (1,)).astype(jnp.int32)
    place = one(position)
    tables = key_tables(width)
    pick_keys, pick_queries = picks(width)
    shape = jax.ShapeDtypeStruct((quarter, ROWS, 128), BF16)
    wide = lambda *dims: jax.ShapeDtypeStruct(dims, F32)
    held = pltpu.VMEM((4, quarter, ROWS, 128), BF16)

    def swap(x, distance):
        return lax.ppermute(x, "seq", [(i, i ^ distance) for i in range(count)])

    token = call(open_kernel, (place,), wide(8, 128), smem=(0,), name="open", us=6.0)
    cum, turned = call(
        gate_kernel,
        (log_gates.T, k_feat, token),
        [wide(heads, rows), wide(k_feat.shape[1], rows)],
        free=(2,),
        name="gates",
        us=0.01,
    )

    sent = call(
        lambda *refs: state_kernel((1, 2, 3), *refs),
        (place, k_feat, turned, values, cum, conv_weight, pick_keys, cum),
        [shape] * 3,
        [pltpu.VMEM((3, 8, 256), F32)],
        smem=(0,),
        free=(7,),
        name="states",
        us=2.0,
    )
    others = [swap(x, d) for d, x in zip((1, 2, 3), sent)]
    (own,) = call(
        lambda *refs: state_kernel((0,), *refs),
        (place, k_feat, turned, values, cum, conv_weight, pick_keys, sent[0]),
        [shape],
        [pltpu.VMEM((1, 8, 256), F32)],
        smem=(0,),
        free=(7,),
        name="own_states",
        us=0.8,
    )
    num, den, token = call(
        block_kernel,
        (q_feat, turned, values, conv_weight, cum, own),
        [wide(*values.shape)] * 2 + [wide(8, 128)],
        free=(5,),
        name="block",
        us=2.7,
    )
    total, before, keys, small = call(
        lambda *refs: group_kernel(width, *refs),
        (place, conv_weight, *tables, own, *others, token),
        [shape, wide(3, quarter, ROWS, 128), wide(2, quarter, ROWS, 128), wide(quarter, 8, 128)],
        [held],
        smem=(0,),
        free=(8,),
        name="merge_group",
        us=2.0,
    )
    base = jnp.zeros_like(total)
    live = position < 0
    distance = 4
    last = total
    while distance < count:
        got = swap(total, distance)
        upper = (position & distance) > 0

        def pair(left, right):
            return call(
                lambda *refs: pair_kernel(width, *refs),
                (place, conv_weight, *tables, left, right),
                shape,
                smem=(0,),
                name="merge_pair",
            )

        if distance == 4:
            base = got
        else:
            base = jnp.where(upper, jnp.where(live, pair(got, base), got), base)
        live = live | upper
        if 2 * distance < count:
            total = pair(jnp.where(upper, got, total), jnp.where(upper, total, got))
        distance *= 2
    edge = call(
        edge_kernel,
        (win_key, values, last),
        jax.ShapeDtypeStruct((2 * WINDOW, values.shape[1]), BF16),
        free=(2,),
        name="edge",
        us=0.2,
    )
    halo = lax.ppermute(edge, "seq", [(i, i + 1) for i in range(count - 1)])

    phi, token = call(
        query_kernel,
        (q_feat, k_feat, cum, pick_queries, edge),
        [jax.ShapeDtypeStruct((heads, rows, 256), BF16), wide(8, 128)],
        free=(4,),
        name="query_features",
        us=1.5,
    )
    here, *sent = call(
        spread_kernel,
        (place, conv_weight, base, before, keys, small, token),
        [shape] * 4,
        [held],
        smem=(0,),
        free=(6,),
        name="spread",
        us=1.0,
    )
    prefixes = [here] + [swap(x, d) for d, x in zip((1, 2, 3), sent)]
    win = call(
        window_kernel,
        (win_query, win_key, values, here),
        wide(rows - WINDOW, values.shape[1]),
        free=(3,),
        name="window",
        us=2.0,
    )
    early = call(
        early_kernel,
        (place, win_query, win_key, values, halo, win),
        wide(WINDOW, values.shape[1]),
        smem=(0,),
        free=(5,),
        name="window_first",
        us=0.4,
    )
    return call(
        finish_kernel,
        (place, phi, *prefixes, num, den, win, early),
        jax.ShapeDtypeStruct(values.shape, BF16),
        [held, pltpu.VMEM((heads, rows, 128), BF16), pltpu.SemaphoreType.DMA((heads,))],
        smem=(0,),
        out_space=pltpu.HBM,
        name="finish",
        us=2.1,
    )


def solution(mesh):
    rows = P(("grp", "seq"), "head")
    count = mesh.shape["seq"]
    return jax.shard_map(
        lambda *args: local(count, *args),
        mesh=mesh,
        in_specs=(rows,) * 6 + (P(None, "head"),),
        out_specs=rows,
        check_vma=False,
    )
```

```python
import numpy as np
import jax
import jax.numpy as jnp
from jax import lax
from jax.experimental import pallas as pl
from jax.experimental.pallas import tpu as pltpu
from jax.sharding import PartitionSpec as P

WINDOW = 64
ROWS = 160
EDGE = 158
LOG2E = float(np.log2(np.e))
F32 = jnp.float32
BF16 = jnp.bfloat16
VMEM_LIMIT = 24 * 1024 * 1024


def feature_tables(width):
    first = -np.ones(ROWS, np.int32)
    second = -np.ones(ROWS, np.int32)
    scale = np.zeros(ROWS, np.float32)
    twice = np.ones(ROWS, np.float32)
    scale[0] = 1.0
    at = 1
    for i in range(width):
        first[at], scale[at] = i, width ** (-0.25)
        at += 1
    for i in range(width):
        for j in range(i, width):
            first[at], second[at], scale[at] = i, j, (2.0 * width) ** (-0.5)
            twice[at] = 1.0 if i == j else 2.0
            at += 1
    one_a = ((first < 0) & (scale > 0)).astype(np.float32)
    one_b = ((second < 0) & (scale > 0)).astype(np.float32)
    return first, second, one_a, one_b, scale, twice


def key_tables(width):
    first, second, one_a, one_b, scale, _ = feature_tables(width)
    pick = np.zeros((2, 2, ROWS, 128), np.float32)
    for token in range(2):
        for factor, index in enumerate((first, second)):
            for row in range(ROWS):
                if index[row] >= 0:
                    pick[token, factor, row, token * width + index[row]] = 1.0
    real = np.stack([np.repeat(x[:, None], 8, axis=1) for x in (one_a, one_b, scale)])
    return jnp.asarray(pick.reshape(4 * ROWS, 128), BF16), jnp.asarray(real, F32)


def wide_rows(width):
    half = width // 2
    pair = lambda i, j: i * width + j if i < half else half * width + (i - half) * half + j - half
    linear = half * width + half * half
    return pair, linear, linear + width


def picks(width):
    first, second, _, _, _, twice = feature_tables(width)
    pair, linear, constant = wide_rows(width)
    keys = np.zeros((ROWS, constant + 16), np.float32)
    keys[0, constant] = 1.0
    for row in range(1, ROWS):
        if second[row] >= 0:
            keys[row, pair(first[row], second[row])] = 1.0
        elif first[row] >= 0:
            keys[row, linear + first[row]] = 1.0
    queries = keys * twice[:, None]
    queries[EDGE, constant + 1] = 1.0
    queries[EDGE + 1, constant + 2] = 1.0
    keys = np.concatenate([keys, np.zeros((256 - ROWS, keys.shape[1]), np.float32)])
    return jnp.asarray(keys, BF16), jnp.asarray(queries, BF16)


def products(x, factor):
    width = x.shape[0]
    half = width // 2
    scaled = x * (factor * (2.0 * width) ** (-0.5))
    blocks = [x * scaled[i : i + 1] for i in range(half)]
    blocks += [x[half:] * scaled[i : i + 1] for i in range(half, width)]
    return blocks + [x * (factor * width ** (-0.25))]


def nt(a, b):
    return lax.dot_general(a, b, (((1,), (1,)), ((), ())), preferred_element_type=F32)


def nn(a, b):
    return lax.dot_general(a, b, (((1,), (0,)), ((), ())), preferred_element_type=F32)


def tn(a, b):
    return lax.dot_general(a, b, (((0,), (0,)), ((), ())), preferred_element_type=F32)


def parts(wide):
    upper = wide.astype(BF16)
    rest = wide - upper.astype(F32)
    middle = rest.astype(BF16)
    lower = (rest - middle.astype(F32)).astype(BF16)
    return upper, middle, lower


def iota(shape, dim):
    return lax.broadcasted_iota(jnp.int32, shape, dim)


def cumulative_rows(gates):
    heads, rows = gates.shape
    upto = (iota((128, 128), 0) <= iota((128, 128), 1)).astype(BF16)
    blocks = [gates[:, i : i + 128] for i in range(0, rows, 128)]
    stacked = jnp.concatenate([piece for block in blocks for piece in parts(block)], axis=0)
    inside = nn(stacked, upto)
    done, before = [], 0.0
    for i in range(len(blocks)):
        three = [inside[(3 * i + p) * heads : (3 * i + p + 1) * heads] for p in range(3)]
        done.append(three[0] + three[1] + three[2] + before)
        before = done[-1][:, 127:]
    return jnp.concatenate(done, axis=1)


def shifted(x, by):
    return jnp.where(iota(x.shape, 0) < by, 0.0, pltpu.roll(x, by, 0))


def quarter_states(quarter, out_ref, k_ref, turned_ref, v_ref, w_ref, cum_ref, pick):
    rows, wide = k_ref.shape
    heads = cum_ref.shape[0]
    width = wide // heads
    count = out_ref.shape[0]
    lane1 = iota((1, 128), 1)
    sub = iota((8, 128), 0)
    keys8 = k_ref[0:16].astype(F32)[0:8]
    wides, norms, values, keeps, lasts = [], [], [], [], []
    for j in range(count):
        head = quarter * count + j
        at = pl.ds(pl.multiple_of(head * 128, 128), 128)
        cum = cum_ref[pl.ds(head, 1), :]
        last = cum[:, rows - 1 :]
        keep = jnp.exp(last - cum)
        k = turned_ref[pl.ds(pl.multiple_of(head * width, width), width), :]
        constant = jnp.where(iota((16, rows), 0) == 0, keep, 0.0)
        phi = jnp.concatenate(products(k, keep) + [constant]).astype(BF16)
        v = v_ref[:, at].astype(F32)
        w = w_ref[:, at]
        conv = (w[0:1] * v + w[1:2] * shifted(v, 1) + w[2:3] * shifted(v, 2)).astype(BF16)
        wides.append(nn(phi, conv).astype(BF16))
        norms.append(nt(jnp.ones((8, rows), BF16), phi))
        values.append(v)
        keeps.append(keep)
        lasts.append(last)
    states = nn(pick[:ROWS], jnp.concatenate(wides, axis=1))
    line = iota(norms[0].shape, 0)
    mixed = jnp.zeros(norms[0].shape, F32)
    for j, norm in enumerate(norms):
        high = norm.astype(BF16).astype(F32)
        mixed = jnp.where(line == 2 * j, high, jnp.where(line == 2 * j + 1, norm - high, mixed))
    norm = nt(mixed.astype(BF16), pick)
    for j in range(count):
        head = quarter * count + j
        high, low = norm[2 * j : 2 * j + 1], norm[2 * j + 1 : 2 * j + 2]
        turned = pltpu.roll(keys8, (wide - head * width) % wide, 1)
        turned2 = pltpu.roll(keys8, (wide - head * width + width) % wide, 1)
        misc = jnp.where(lane1 < width, turned[0:1], 0.0)
        misc = jnp.where((lane1 >= width) & (lane1 < 2 * width), turned2[1:2], misc)
        place = 2 * width
        for value in (keeps[j][:, 0:1], keeps[j][:, 1:2], jnp.exp(lasts[j])):
            for piece in parts(value):
                misc = jnp.where(lane1 == place, piece.astype(F32), misc)
                place += 1
        state = states[:, 128 * j : 128 * j + 128]
        tail = state[ROWS - 8 :]
        for row, text in enumerate((high[:, :128], high[:, 128:], low[:, :128], low[:, 128:], misc)):
            tail = jnp.where(sub == row + 1, text, tail)
        tail = jnp.where(sub >= 6, values[j][rows - 8 :], tail)
        out_ref[j, 0 : ROWS - 16, :] = state[: ROWS - 16].astype(BF16)
        out_ref[j, ROWS - 16 :, :] = jnp.concatenate([state[ROWS - 16 : ROWS - 8], tail]).astype(BF16)


def open_kernel(place_ref, token_ref):
    token_ref[...] = jnp.zeros(token_ref.shape, F32)


def gate_kernel(g_ref, k_ref, after_ref, cum_ref, turned_ref):
    cum_ref[...] = cumulative_rows(g_ref[...])
    turned_ref[...] = k_ref[...].astype(F32).T


def state_kernel(order, place_ref, k_ref, turned_ref, v_ref, cum_ref, w_ref, pick_ref, after_ref, *outs):
    pick = pick_ref[...]
    for out_ref, distance in zip(outs, order):
        quarter = (place_ref[0] & 3) ^ distance
        quarter_states(quarter, out_ref, k_ref, turned_ref, v_ref, w_ref, cum_ref, pick)


def edge_kernel(win_key_ref, v_ref, after_ref, edge_ref):
    edge_ref[:WINDOW] = win_key_ref[win_key_ref.shape[0] - WINDOW :]
    edge_ref[WINDOW:] = v_ref[v_ref.shape[0] - WINDOW :]


def tail_of(tile):
    return tile[ROWS - 8 :]


def value_of(tile, i, width):
    lane1 = iota((1, 128), 1)
    place = 2 * width + 3 * i
    here = (lane1 >= place) & (lane1 < place + 3)
    return jnp.sum(jnp.where(here, tail_of(tile)[5:6], 0.0), axis=1, keepdims=True)


def first_keys(tiles, pick_ref, real_ref):
    lines = [tail_of(tile)[5:6] for tile in tiles]
    rows = jnp.concatenate(lines + [jnp.zeros((8 - len(lines), 128), F32)] if len(lines) < 8 else lines).astype(BF16)
    found = nt(pick_ref[...], rows)
    factors = [found[i * ROWS : (i + 1) * ROWS] for i in range(4)]
    one_a, one_b, scale = (real_ref[i] for i in range(3))
    return [(factors[2 * t] + one_a) * (factors[2 * t + 1] + one_b) * scale for t in range(2)]


def carried(tile, w):
    tail = tail_of(tile)
    return w[1:2] * tail[7:8] + w[2:3] * tail[6:7], w[2:3] * tail[7:8]


def seam(left, columns, enter, w):
    carry0, carry1 = carried(left, w)
    return columns[0] * (enter[0] * carry0) + columns[1] * (enter[1] * carry1)


def merge(left, right, columns, w, width):
    decay = value_of(right, 2, width)
    joined = decay * left + right + seam(left, columns, (value_of(right, 0, width), value_of(right, 1, width)), w)
    sub = iota((8, 128), 0)
    lane1 = iota((1, 128), 1)
    misc = tail_of(left)[5:6]
    misc = jnp.where(lane1 < 2 * width, misc, misc * decay)
    tail = jnp.where(sub == 5, misc, tail_of(joined))
    tail = jnp.where(sub >= 6, tail_of(right), tail)
    return jnp.concatenate([joined[: ROWS - 8], tail])


def packed(tile, width):
    tail = tail_of(tile)
    sub = iota((8, 128), 0)
    lane1 = iota((1, 128), 1)
    misc = tail[5:6]
    fresh = jnp.where(lane1 < 2 * width, misc, 0.0)
    place = 2 * width
    for i in range(3):
        for piece in parts(value_of(tile, i, width)):
            fresh = jnp.where(lane1 == place, piece.astype(F32), fresh)
            place += 1
    tail = jnp.where(sub == 5, fresh, norm_parts(tail))
    return jnp.concatenate([tile[: ROWS - 8], tail]).astype(BF16)


def norm_parts(tail):
    sub = iota((8, 128), 0)
    for row in (1, 2):
        norm = tail[row : row + 1] + tail[row + 2 : row + 3]
        high = norm.astype(BF16).astype(F32)
        tail = jnp.where(sub == row, high, jnp.where(sub == row + 2, norm - high, tail))
    return tail


def head_taps(w_ref, head):
    return w_ref[:, pl.ds(pl.multiple_of(head * 128, 128), 128)]


def group_kernel(width, place_ref, w_ref, pick_ref, real_ref, x0, x1, x2, x3, after_ref, total_ref, before_ref, keys_ref, small_ref, held):
    group = (place_ref[0] & 3)
    count = x0.shape[0]
    for distance, ref in enumerate((x0, x1, x2, x3)):
        held[group ^ distance] = ref[...]
    tiles = [[held[p, j].astype(F32) for j in range(count)] for p in range(4)]
    columns = first_keys([tiles[p][j] for p in range(4) for j in range(count)], pick_ref, real_ref)
    sub = iota((8, 128), 0)
    for j in range(count):
        w = head_taps(w_ref, group * count + j)
        so_far = tiles[0][j]
        for p in range(1, 4):
            before_ref[p - 1, j] = so_far
            pick = p * count + j
            so_far = merge(so_far, tiles[p][j], [c[:, pick : pick + 1] for c in columns], w, width)
        total_ref[j] = packed(so_far, width)
        for token in range(2):
            keys_ref[token, j] = jnp.broadcast_to(columns[token][:, j : j + 1], (ROWS, 128))
        decays = [value_of(tiles[p][j], 2, width) for p in range(3)]
        small = jnp.zeros((8, 128), F32)
        lines = decays[0], value_of(tiles[0][j], 0, width), value_of(tiles[0][j], 1, width), decays[1], decays[1] * decays[2]
        for row, value in enumerate(lines):
            small = jnp.where(sub == row, value, small)
        small_ref[j] = small


def pair_kernel(width, place_ref, w_ref, pick_ref, real_ref, left_ref, right_ref, out_ref):
    count = left_ref.shape[0]
    rights = [right_ref[j].astype(F32) for j in range(count)]
    columns = first_keys(rights, pick_ref, real_ref)
    for j in range(count):
        w = head_taps(w_ref, (place_ref[0] & 3) * count + j)
        left = left_ref[j].astype(F32)
        out_ref[j] = packed(merge(left, rights[j], [c[:, j : j + 1] for c in columns], w, width), width)


def with_edge(tile, source, w):
    carry0, carry1 = carried(source, w)
    sub = iota((8, 128), 0)
    tail = norm_parts(tail_of(tile))
    tail = jnp.where(sub == 6, carry0, jnp.where(sub == 7, carry1, tail))
    return jnp.concatenate([tile[: ROWS - 8], tail]).astype(BF16)


def spread_kernel(place_ref, w_ref, base_ref, before_ref, keys_ref, small_ref, after_ref, o0, o1, o2, o3, held):
    group = (place_ref[0] & 3)
    live = place_ref[0] > 3
    count = base_ref.shape[0]
    for j in range(count):
        w = head_taps(w_ref, group * count + j)
        base = jnp.where(live, base_ref[j].astype(F32), 0.0)
        held[0, j] = with_edge(base, base, w)
        small = small_ref[j]
        through = small[0:1] * base + seam(base, (keys_ref[0, j], keys_ref[1, j]), (small[1:2], small[2:3]), w)
        for p in range(3):
            tile = before_ref[p, j] + (through if p == 0 else small[2 + p : 3 + p] * through)
            held[p + 1, j] = with_edge(tile, before_ref[p, j], w)
    for distance, ref in enumerate((o0, o1, o2, o3)):
        ref[...] = held[group ^ distance]


def windowed(wq_ref, keys, values, valid, out_ref):
    half = WINDOW
    rows = wq_ref.shape[0]
    steps = rows // half
    ones = jnp.ones((rows + half, 128), BF16)
    zeros = jnp.zeros((rows + half, 128), BF16)
    heads = wq_ref.shape[1] // 128
    spans = [slice(i * half, (i + 2) * half) for i in range(steps)]
    for four in range(0, heads, 4):
        scores = []
        for h in range(four, four + 4, 2):
            one, two = slice(128 * h, 128 * h + 128), slice(128 * h + 128, 128 * h + 256)
            upper = jnp.concatenate([keys(one), zeros], axis=1)
            lower = jnp.concatenate([zeros, keys(two)], axis=1)
            queries = wq_ref[:, 128 * h : 128 * h + 256]
            s = [nt(queries[i * half : (i + 1) * half], jnp.concatenate([upper[span], lower[span]])) for i, span in enumerate(spans)]
            scores += [[x[:, :128] for x in s], [x[:, 128:] for x in s]]
        probs = []
        for s in scores:
            s = jnp.concatenate([jnp.where(valid, x * (128 ** (-0.5) * LOG2E), -jnp.inf) for x in s])
            probs.append(jnp.exp2(s - jnp.max(s, axis=1, keepdims=True)).astype(BF16))
        for h, p in zip(range(four, four + 4), probs):
            at = slice(128 * h, 128 * h + 128)
            right = jnp.concatenate([values(at), ones], axis=1)
            both = jnp.concatenate([nn(p[i * half : (i + 1) * half], right[span]) for i, span in enumerate(spans)])
            out_ref[:, at] = both[:, :128] / both[:, 128:]


def window_masks():
    seen = iota((WINDOW, 2 * WINDOW), 1)
    mine = iota((WINDOW, 2 * WINDOW), 0)
    return (seen > mine) & (seen <= mine + WINDOW), seen >= WINDOW


def window_kernel(wq_ref, wk_ref, v_ref, after_ref, win_ref):
    valid, _ = window_masks()
    windowed(wq_ref.at[pl.ds(WINDOW, win_ref.shape[0])], lambda at: wk_ref[:, at], lambda at: v_ref[:, at], valid, win_ref)


def early_kernel(place_ref, wq_ref, wk_ref, v_ref, halo_ref, after_ref, win_ref):
    valid, own = window_masks()
    valid = valid & (own | ((place_ref[0]) > 0))
    keys = lambda at: jnp.concatenate([halo_ref[:WINDOW, at], wk_ref[:WINDOW, at]])
    values = lambda at: jnp.concatenate([halo_ref[WINDOW:, at], v_ref[:WINDOW, at]])
    windowed(wq_ref.at[pl.ds(0, WINDOW)], keys, values, valid, win_ref)


def block_kernel(q_ref, turned_ref, v_ref, w_ref, cum_ref, after_ref, num_ref, den_ref, token_ref):
    rows, wide = q_ref.shape
    heads = cum_ref.shape[0]
    width = wide // heads
    q = q_ref[...]
    cum_row = cum_ref[...] * LOG2E
    cum_col = cum_row.T
    token_ref[...] = jnp.zeros(token_ref.shape, F32)
    level = iota(turned_ref.shape, 0)
    step, piece = 256, 128
    ones = jnp.ones((rows, 128), BF16)
    causal = iota((piece, piece), 0) >= iota((piece, piece), 1)
    for h in range(heads):
        at = slice(128 * h, 128 * h + 128)
        here = (level >= h * width) & (level < (h + 1) * width)
        k_here = jnp.where(here, turned_ref[...] * width ** (-0.5), 0.0).astype(BF16)
        v = v_ref[:, at].astype(F32)
        w = w_ref[:, at]
        conv = w[0:1] * v + w[1:2] * shifted(v, 1) + w[2:3] * shifted(v, 2)
        right = jnp.concatenate([conv.astype(BF16), ones], axis=1)
        column = jnp.broadcast_to(cum_col[:, h : h + 1], (rows, piece))
        total = None
        for low in range(0, rows, step):
            x = nn(q[low:], k_here[:, low : low + step])
            lines = []
            for i in range(low, rows, piece):
                line = []
                for j in range(low, low + step, piece):
                    if j > i:
                        line.append(jnp.zeros((piece, piece), BF16))
                        continue
                    here = x[i - low : i - low + piece, j - low : j - low + piece]
                    gap = column[i : i + piece] - cum_row[h : h + 1, j : j + piece]
                    if i == j:
                        gap = jnp.where(causal, gap, -jnp.inf)
                    line.append((((0.5 * here + 1.0) * here + 1.0) * jnp.exp2(gap)).astype(BF16))
                lines.append(jnp.concatenate(line, axis=1))
            both = nn(jnp.concatenate(lines), right[low : low + step])
            total = both if total is None else jnp.concatenate([total[:low], total[low:] + both])
        num_ref[:, at] = total[:, :128]
        den_ref[:, at] = total[:, 128:]


def query_kernel(q_ref, k_ref, cum_ref, pick_ref, after_ref, out_ref, token_ref):
    rows, wide = q_ref.shape
    heads = cum_ref.shape[0]
    width = wide // heads
    q = q_ref[...]
    turned = q.astype(F32).T
    token_ref[...] = jnp.zeros(token_ref.shape, F32)
    pick = pick_ref[...]
    keys = k_ref[0:16].astype(F32)[0:8] * width ** (-0.5)
    line = iota((2 * heads, wide), 0)
    lane = iota((2 * heads, wide), 1)
    keys = jnp.where(line < heads, keys[0:1], keys[1:2])
    low = jnp.where(line < heads, line, line - heads) * width
    x = nt(jnp.where((lane >= low) & (lane < low + width), keys, 0.0).astype(BF16), q)
    x = (0.5 * x + 1.0) * x + 1.0
    sub = iota((16, rows), 0)
    at = iota((1, rows), 1)
    for h in range(heads):
        cum = cum_ref[h : h + 1, :]
        enter = jnp.exp(cum)
        score0 = x[h : h + 1] * jnp.exp(cum - cum[:, 0:1])
        score1 = x[heads + h : heads + h + 1] * jnp.exp(jnp.where(at < 1, -jnp.inf, cum - cum[:, 1:2]))
        rest = jnp.where(sub == 0, enter, jnp.where(sub == 1, score0, jnp.where(sub == 2, score1, 0.0)))
        phi = jnp.concatenate(products(turned[h * width : (h + 1) * width], enter) + [rest]).astype(BF16)
        out_ref[h, :, 0:ROWS] = nn(pick, phi).astype(BF16).T


def finish_kernel(place_ref, phi_ref, x0, x1, x2, x3, num_ref, den_ref, win_ref, early_ref, out_far, held, out_ref, sems):
    group = (place_ref[0] & 3)
    heads = phi_ref.shape[0]
    count = x0.shape[0]
    for distance, ref in enumerate((x0, x1, x2, x3)):
        held[group ^ distance] = ref[...]
    tiles = [held[h // count, h % count] for h in range(heads)]
    lines = []
    for tile in tiles:
        tail = tile[ROWS - 16 :].astype(F32)[8:]
        lines.append(jnp.concatenate([tail[1:2] + tail[3:4], tail[2:3] + tail[4:5]], axis=1))
    norms = jnp.concatenate(lines).T
    copies = []
    for h in range(heads):
        at = slice(128 * h, 128 * h + 128)
        norm = jnp.broadcast_to(norms[:ROWS, h : h + 1], (ROWS, 128)).astype(BF16)
        both = nn(phi_ref[h][:, :ROWS], jnp.concatenate([tiles[h], norm], axis=1))
        out = (num_ref[:, at] + both[:, :128]) / (den_ref[:, at] + both[:, 128:])
        out = out + jnp.concatenate([early_ref[:, at], win_ref[:, at]])
        out_ref[h] = out.astype(BF16)
        copies.append(pltpu.make_async_copy(out_ref.at[h], out_far.at[:, pl.ds(128 * h, 128)], sems.at[h]))
        copies[-1].start()
    for copy in copies:
        copy.wait()


def call(kernel, inputs, outs, scratch=(), smem=(), free=(), far=(), name=None, us=1.0, out_space=pltpu.VMEM):
    def space(i):
        return pltpu.SMEM if i in smem else pl.ANY if i in free else pltpu.HBM if i in far else pltpu.VMEM

    return pl.pallas_call(
        kernel,
        out_shape=outs,
        in_specs=[pl.BlockSpec(memory_space=space(i)) for i in range(len(inputs))],
        out_specs=jax.tree.map(lambda _: pl.BlockSpec(memory_space=out_space), outs),
        scratch_shapes=scratch,
        compiler_params=pltpu.CompilerParams(vmem_limit_bytes=VMEM_LIMIT),
        name=name,
        cost_estimate=pl.CostEstimate(flops=int(us * 3e9), bytes_accessed=int(us * 9e6), transcendentals=0),
    )(*inputs)


def local(count, q_feat, k_feat, values, win_query, win_key, log_gates, conv_weight):
    rows = values.shape[0]
    heads = log_gates.shape[1]
    width = q_feat.shape[1] // heads
    quarter = heads // 4
    position = lax.axis_index("seq")
    one = lambda number: jnp.reshape(number, (1,)).astype(jnp.int32)
    place = one(position)
    tables = key_tables(width)
    pick_keys, pick_queries = picks(width)
    shape = jax.ShapeDtypeStruct((quarter, ROWS, 128), BF16)
    wide = lambda *dims: jax.ShapeDtypeStruct(dims, F32)
    held = pltpu.VMEM((4, quarter, ROWS, 128), BF16)

    def swap(x, distance):
        return lax.ppermute(x, "seq", [(i, i ^ distance) for i in range(count)])

    token = call(open_kernel, (place,), wide(8, 128), smem=(0,), name="open", us=6.0)
    cum, turned = call(
        gate_kernel,
        (log_gates.T, k_feat, token),
        [wide(heads, rows), wide(k_feat.shape[1], rows)],
        free=(2,),
        name="gates",
        us=0.01,
    )

    def states(order, after, name, us):
        return call(
            lambda *refs: state_kernel(order, *refs),
            (place, k_feat, turned, values, cum, conv_weight, pick_keys, after),
            [shape] * len(order),
            smem=(0,),
            free=(7,),
            name=name,
            us=us,
        )

    made = {}
    after = cum
    for number, order in enumerate(((3,), (1, 2))):
        made.update(zip(order, states(order, after, f"states{number}", 0.3 + 0.5 * len(order))))
        after = made[order[0]]
    sent = [made[d] for d in (1, 2, 3)]
    others = [swap(x, d) for d, x in zip((1, 2, 3), sent)]
    (own,) = call(
        lambda *refs: state_kernel((0,), *refs),
        (place, k_feat, turned, values, cum, conv_weight, pick_keys, after),
        [shape],
        smem=(0,),
        free=(7,),
        name="own_states",
        us=0.8,
    )
    num, den, token = call(
        block_kernel,
        (q_feat, turned, values, conv_weight, cum, own),
        [wide(*values.shape)] * 2 + [wide(8, 128)],
        free=(5,),
        name="block",
        us=2.7,
    )
    total, before, keys, small = call(
        lambda *refs: group_kernel(width, *refs),
        (place, conv_weight, *tables, own, *others, token),
        [shape, wide(3, quarter, ROWS, 128), wide(2, quarter, ROWS, 128), wide(quarter, 8, 128)],
        [held],
        smem=(0,),
        free=(8,),
        name="merge_group",
        us=2.0,
    )
    base = jnp.zeros_like(total)
    live = position < 0
    distance = 4
    last = total
    while distance < count:
        got = swap(total, distance)
        upper = (position & distance) > 0

        def pair(left, right):
            return call(
                lambda *refs: pair_kernel(width, *refs),
                (place, conv_weight, *tables, left, right),
                shape,
                smem=(0,),
                name="merge_pair",
            )

        if distance == 4:
            base = got
        else:
            base = jnp.where(upper, jnp.where(live, pair(got, base), got), base)
        live = live | upper
        if 2 * distance < count:
            total = pair(jnp.where(upper, got, total), jnp.where(upper, total, got))
        distance *= 2
    edge = call(
        edge_kernel,
        (win_key, values, last),
        jax.ShapeDtypeStruct((2 * WINDOW, values.shape[1]), BF16),
        free=(2,),
        name="edge",
        us=0.2,
    )
    halo = lax.ppermute(edge, "seq", [(i, i + 1) for i in range(count - 1)])

    phi, token = call(
        query_kernel,
        (q_feat, k_feat, cum, pick_queries, edge),
        [jax.ShapeDtypeStruct((heads, rows, 256), BF16), wide(8, 128)],
        free=(4,),
        name="query_features",
        us=1.5,
    )
    here, *sent = call(
        spread_kernel,
        (place, conv_weight, base, before, keys, small, token),
        [shape] * 4,
        [held],
        smem=(0,),
        free=(6,),
        name="spread",
        us=1.0,
    )
    prefixes = [here] + [swap(x, d) for d, x in zip((1, 2, 3), sent)]
    win = call(
        window_kernel,
        (win_query, win_key, values, here),
        wide(rows - WINDOW, values.shape[1]),
        free=(3,),
        name="window",
        us=2.0,
    )
    early = call(
        early_kernel,
        (place, win_query, win_key, values, halo, win),
        wide(WINDOW, values.shape[1]),
        smem=(0,),
        free=(5,),
        name="window_first",
        us=0.4,
    )
    return call(
        finish_kernel,
        (place, phi, *prefixes, num, den, win, early),
        jax.ShapeDtypeStruct(values.shape, BF16),
        [held, pltpu.VMEM((heads, rows, 128), BF16), pltpu.SemaphoreType.DMA((heads,))],
        smem=(0,),
        out_space=pltpu.HBM,
        name="finish",
        us=2.1,
    )


def solution(mesh):
    rows = P(("grp", "seq"), "head")
    count = mesh.shape["seq"]
    return jax.shard_map(
        lambda *args: local(count, *args),
        mesh=mesh,
        in_specs=(rows,) * 6 + (P(None, "head"),),
        out_specs=rows,
        check_vma=False,
    )
```

```python
import numpy as np
import jax
import jax.numpy as jnp
from jax import lax
from jax.experimental import pallas as pl
from jax.experimental.pallas import tpu as pltpu
from jax.sharding import PartitionSpec as P

WINDOW = 64
ROWS = 160
EDGE = 158
LOG2E = float(np.log2(np.e))
F32 = jnp.float32
BF16 = jnp.bfloat16
VMEM_LIMIT = 24 * 1024 * 1024


def feature_tables(width):
    first = -np.ones(ROWS, np.int32)
    second = -np.ones(ROWS, np.int32)
    scale = np.zeros(ROWS, np.float32)
    twice = np.ones(ROWS, np.float32)
    scale[0] = 1.0
    at = 1
    for i in range(width):
        first[at], scale[at] = i, width ** (-0.25)
        at += 1
    for i in range(width):
        for j in range(i, width):
            first[at], second[at], scale[at] = i, j, (2.0 * width) ** (-0.5)
            twice[at] = 1.0 if i == j else 2.0
            at += 1
    one_a = ((first < 0) & (scale > 0)).astype(np.float32)
    one_b = ((second < 0) & (scale > 0)).astype(np.float32)
    return first, second, one_a, one_b, scale, twice


def key_tables(width):
    first, second, one_a, one_b, scale, _ = feature_tables(width)
    pick = np.zeros((2, 2, ROWS, 128), np.float32)
    for token in range(2):
        for factor, index in enumerate((first, second)):
            for row in range(ROWS):
                if index[row] >= 0:
                    pick[token, factor, row, token * width + index[row]] = 1.0
    real = np.stack([np.repeat(x[:, None], 8, axis=1) for x in (one_a, one_b, scale)])
    return jnp.asarray(pick.reshape(4 * ROWS, 128), BF16), jnp.asarray(real, F32)


def wide_rows(width):
    half = width // 2
    pair = lambda i, j: i * width + j if i < half else half * width + (i - half) * half + j - half
    linear = half * width + half * half
    return pair, linear, linear + width


def picks(width):
    first, second, _, _, _, twice = feature_tables(width)
    pair, linear, constant = wide_rows(width)
    keys = np.zeros((ROWS, constant + 16), np.float32)
    keys[0, constant] = 1.0
    for row in range(1, ROWS):
        if second[row] >= 0:
            keys[row, pair(first[row], second[row])] = 1.0
        elif first[row] >= 0:
            keys[row, linear + first[row]] = 1.0
    queries = keys * twice[:, None]
    queries[EDGE, constant + 1] = 1.0
    queries[EDGE + 1, constant + 2] = 1.0
    keys = np.concatenate([keys, np.zeros((256 - ROWS, keys.shape[1]), np.float32)])
    return jnp.asarray(keys, BF16), jnp.asarray(queries, BF16)


def products(x, factor):
    width = x.shape[0]
    half = width // 2
    scaled = x * (factor * (2.0 * width) ** (-0.5))
    blocks = [x * scaled[i : i + 1] for i in range(half)]
    blocks += [x[half:] * scaled[i : i + 1] for i in range(half, width)]
    return blocks + [x * (factor * width ** (-0.25))]


def nt(a, b):
    return lax.dot_general(a, b, (((1,), (1,)), ((), ())), preferred_element_type=F32)


def nn(a, b):
    return lax.dot_general(a, b, (((1,), (0,)), ((), ())), preferred_element_type=F32)


def tn(a, b):
    return lax.dot_general(a, b, (((0,), (0,)), ((), ())), preferred_element_type=F32)


def parts(wide):
    upper = wide.astype(BF16)
    rest = wide - upper.astype(F32)
    middle = rest.astype(BF16)
    lower = (rest - middle.astype(F32)).astype(BF16)
    return upper, middle, lower


def iota(shape, dim):
    return lax.broadcasted_iota(jnp.int32, shape, dim)


def cumulative_rows(gates):
    heads, rows = gates.shape
    upto = (iota((128, 128), 0) <= iota((128, 128), 1)).astype(BF16)
    blocks = [gates[:, i : i + 128] for i in range(0, rows, 128)]
    stacked = jnp.concatenate([piece for block in blocks for piece in parts(block)], axis=0)
    inside = nn(stacked, upto)
    done, before = [], 0.0
    for i in range(len(blocks)):
        three = [inside[(3 * i + p) * heads : (3 * i + p + 1) * heads] for p in range(3)]
        done.append(three[0] + three[1] + three[2] + before)
        before = done[-1][:, 127:]
    return jnp.concatenate(done, axis=1)


def shifted(x, by):
    return jnp.where(iota(x.shape, 0) < by, 0.0, pltpu.roll(x, by, 0))


def quarter_states(quarter, out_ref, k_ref, turned_ref, v_ref, w_ref, cum_ref, pick):
    rows, wide = k_ref.shape
    heads = cum_ref.shape[0]
    width = wide // heads
    count = out_ref.shape[0]
    lane1 = iota((1, 128), 1)
    sub = iota((8, 128), 0)
    keys8 = k_ref[0:16].astype(F32)[0:8]
    wides, norms, values, keeps, lasts = [], [], [], [], []
    for j in range(count):
        head = quarter * count + j
        at = pl.ds(pl.multiple_of(head * 128, 128), 128)
        cum = cum_ref[pl.ds(head, 1), :]
        last = cum[:, rows - 1 :]
        keep = jnp.exp(last - cum)
        k = turned_ref[pl.ds(pl.multiple_of(head * width, width), width), :]
        constant = jnp.where(iota((16, rows), 0) == 0, keep, 0.0)
        phi = jnp.concatenate(products(k, keep) + [constant]).astype(BF16)
        v = v_ref[:, at].astype(F32)
        w = w_ref[:, at]
        conv = (w[0:1] * v + w[1:2] * shifted(v, 1) + w[2:3] * shifted(v, 2)).astype(BF16)
        wides.append(nn(phi, conv).astype(BF16))
        norms.append(nt(jnp.ones((8, rows), BF16), phi))
        values.append(v)
        keeps.append(keep)
        lasts.append(last)
    states = nn(pick[:ROWS], jnp.concatenate(wides, axis=1))
    line = iota(norms[0].shape, 0)
    mixed = jnp.zeros(norms[0].shape, F32)
    for j, norm in enumerate(norms):
        high = norm.astype(BF16).astype(F32)
        mixed = jnp.where(line == 2 * j, high, jnp.where(line == 2 * j + 1, norm - high, mixed))
    norm = nt(mixed.astype(BF16), pick)
    for j in range(count):
        head = quarter * count + j
        high, low = norm[2 * j : 2 * j + 1], norm[2 * j + 1 : 2 * j + 2]
        turned = pltpu.roll(keys8, (wide - head * width) % wide, 1)
        turned2 = pltpu.roll(keys8, (wide - head * width + width) % wide, 1)
        misc = jnp.where(lane1 < width, turned[0:1], 0.0)
        misc = jnp.where((lane1 >= width) & (lane1 < 2 * width), turned2[1:2], misc)
        place = 2 * width
        for value in (keeps[j][:, 0:1], keeps[j][:, 1:2], jnp.exp(lasts[j])):
            for piece in parts(value):
                misc = jnp.where(lane1 == place, piece.astype(F32), misc)
                place += 1
        state = states[:, 128 * j : 128 * j + 128]
        tail = state[ROWS - 8 :]
        for row, text in enumerate((high[:, :128], high[:, 128:], low[:, :128], low[:, 128:], misc)):
            tail = jnp.where(sub == row + 1, text, tail)
        tail = jnp.where(sub >= 6, values[j][rows - 8 :], tail)
        out_ref[j, 0 : ROWS - 16, :] = state[: ROWS - 16].astype(BF16)
        out_ref[j, ROWS - 16 :, :] = jnp.concatenate([state[ROWS - 16 : ROWS - 8], tail]).astype(BF16)


def open_kernel(place_ref, token_ref):
    token_ref[...] = jnp.zeros(token_ref.shape, F32)


def gate_kernel(g_ref, k_ref, after_ref, cum_ref, turned_ref):
    cum_ref[...] = cumulative_rows(g_ref[...])
    turned_ref[...] = k_ref[...].astype(F32).T


def state_kernel(order, place_ref, k_ref, turned_ref, v_ref, cum_ref, w_ref, pick_ref, after_ref, *outs):
    pick = pick_ref[...]
    for out_ref, distance in zip(outs, order):
        quarter = (place_ref[0] & 3) ^ distance
        quarter_states(quarter, out_ref, k_ref, turned_ref, v_ref, w_ref, cum_ref, pick)


def edge_kernel(win_key_ref, v_ref, after_ref, edge_ref):
    edge_ref[:WINDOW] = win_key_ref[win_key_ref.shape[0] - WINDOW :]
    edge_ref[WINDOW:] = v_ref[v_ref.shape[0] - WINDOW :]


def tail_of(tile):
    return tile[ROWS - 8 :]


def value_of(tile, i, width):
    lane1 = iota((1, 128), 1)
    place = 2 * width + 3 * i
    here = (lane1 >= place) & (lane1 < place + 3)
    return jnp.sum(jnp.where(here, tail_of(tile)[5:6], 0.0), axis=1, keepdims=True)


def first_keys(tiles, pick_ref, real_ref):
    lines = [tail_of(tile)[5:6] for tile in tiles]
    rows = jnp.concatenate(lines + [jnp.zeros((8 - len(lines), 128), F32)] if len(lines) < 8 else lines).astype(BF16)
    found = nt(pick_ref[...], rows)
    factors = [found[i * ROWS : (i + 1) * ROWS] for i in range(4)]
    one_a, one_b, scale = (real_ref[i] for i in range(3))
    return [(factors[2 * t] + one_a) * (factors[2 * t + 1] + one_b) * scale for t in range(2)]


def carried(tile, w):
    tail = tail_of(tile)
    return w[1:2] * tail[7:8] + w[2:3] * tail[6:7], w[2:3] * tail[7:8]


def seam(left, columns, enter, w):
    carry0, carry1 = carried(left, w)
    return columns[0] * (enter[0] * carry0) + columns[1] * (enter[1] * carry1)


def merge(left, right, columns, w, width):
    decay = value_of(right, 2, width)
    joined = decay * left + right + seam(left, columns, (value_of(right, 0, width), value_of(right, 1, width)), w)
    sub = iota((8, 128), 0)
    lane1 = iota((1, 128), 1)
    misc = tail_of(left)[5:6]
    misc = jnp.where(lane1 < 2 * width, misc, misc * decay)
    tail = jnp.where(sub == 5, misc, tail_of(joined))
    tail = jnp.where(sub >= 6, tail_of(right), tail)
    return jnp.concatenate([joined[: ROWS - 8], tail])


def packed(tile, width):
    tail = tail_of(tile)
    sub = iota((8, 128), 0)
    lane1 = iota((1, 128), 1)
    misc = tail[5:6]
    fresh = jnp.where(lane1 < 2 * width, misc, 0.0)
    place = 2 * width
    for i in range(3):
        for piece in parts(value_of(tile, i, width)):
            fresh = jnp.where(lane1 == place, piece.astype(F32), fresh)
            place += 1
    tail = jnp.where(sub == 5, fresh, norm_parts(tail))
    return jnp.concatenate([tile[: ROWS - 8], tail]).astype(BF16)


def norm_parts(tail):
    sub = iota((8, 128), 0)
    for row in (1, 2):
        norm = tail[row : row + 1] + tail[row + 2 : row + 3]
        high = norm.astype(BF16).astype(F32)
        tail = jnp.where(sub == row, high, jnp.where(sub == row + 2, norm - high, tail))
    return tail


def head_taps(w_ref, head):
    return w_ref[:, pl.ds(pl.multiple_of(head * 128, 128), 128)]


def group_kernel(width, place_ref, w_ref, pick_ref, real_ref, x0, x1, x2, x3, after_ref, total_ref, before_ref, keys_ref, small_ref, held):
    group = (place_ref[0] & 3)
    count = x0.shape[0]
    for distance, ref in enumerate((x0, x1, x2, x3)):
        held[group ^ distance] = ref[...]
    tiles = [[held[p, j].astype(F32) for j in range(count)] for p in range(4)]
    columns = first_keys([tiles[p][j] for p in range(4) for j in range(count)], pick_ref, real_ref)
    sub = iota((8, 128), 0)
    for j in range(count):
        w = head_taps(w_ref, group * count + j)
        so_far = tiles[0][j]
        for p in range(1, 4):
            before_ref[p - 1, j] = so_far
            pick = p * count + j
            so_far = merge(so_far, tiles[p][j], [c[:, pick : pick + 1] for c in columns], w, width)
        total_ref[j] = packed(so_far, width)
        for token in range(2):
            keys_ref[token, j] = jnp.broadcast_to(columns[token][:, j : j + 1], (ROWS, 128))
        decays = [value_of(tiles[p][j], 2, width) for p in range(3)]
        small = jnp.zeros((8, 128), F32)
        lines = decays[0], value_of(tiles[0][j], 0, width), value_of(tiles[0][j], 1, width), decays[1], decays[1] * decays[2]
        for row, value in enumerate(lines):
            small = jnp.where(sub == row, value, small)
        small_ref[j] = small


def pair_kernel(width, place_ref, w_ref, pick_ref, real_ref, left_ref, right_ref, out_ref):
    count = left_ref.shape[0]
    rights = [right_ref[j].astype(F32) for j in range(count)]
    columns = first_keys(rights, pick_ref, real_ref)
    for j in range(count):
        w = head_taps(w_ref, (place_ref[0] & 3) * count + j)
        left = left_ref[j].astype(F32)
        out_ref[j] = packed(merge(left, rights[j], [c[:, j : j + 1] for c in columns], w, width), width)


def with_edge(tile, source, w):
    carry0, carry1 = carried(source, w)
    sub = iota((8, 128), 0)
    tail = norm_parts(tail_of(tile))
    tail = jnp.where(sub == 6, carry0, jnp.where(sub == 7, carry1, tail))
    return jnp.concatenate([tile[: ROWS - 8], tail]).astype(BF16)


def spread_kernel(place_ref, w_ref, base_ref, before_ref, keys_ref, small_ref, after_ref, o0, o1, o2, o3, held):
    group = (place_ref[0] & 3)
    live = place_ref[0] > 3
    count = base_ref.shape[0]
    for j in range(count):
        w = head_taps(w_ref, group * count + j)
        base = jnp.where(live, base_ref[j].astype(F32), 0.0)
        held[0, j] = with_edge(base, base, w)
        small = small_ref[j]
        through = small[0:1] * base + seam(base, (keys_ref[0, j], keys_ref[1, j]), (small[1:2], small[2:3]), w)
        for p in range(3):
            tile = before_ref[p, j] + (through if p == 0 else small[2 + p : 3 + p] * through)
            held[p + 1, j] = with_edge(tile, before_ref[p, j], w)
    for distance, ref in enumerate((o0, o1, o2, o3)):
        ref[...] = held[group ^ distance]


def windowed(wq_ref, keys, values, valid, out_ref):
    half = WINDOW
    rows = wq_ref.shape[0]
    steps = rows // half
    ones = jnp.ones((rows + half, 128), BF16)
    zeros = jnp.zeros((rows + half, 128), BF16)
    heads = wq_ref.shape[1] // 128
    spans = [slice(i * half, (i + 2) * half) for i in range(steps)]
    for four in range(0, heads, 4):
        scores = []
        for h in range(four, four + 4, 2):
            one, two = slice(128 * h, 128 * h + 128), slice(128 * h + 128, 128 * h + 256)
            upper = jnp.concatenate([keys(one), zeros], axis=1)
            lower = jnp.concatenate([zeros, keys(two)], axis=1)
            queries = wq_ref[:, 128 * h : 128 * h + 256]
            s = [nt(queries[i * half : (i + 1) * half], jnp.concatenate([upper[span], lower[span]])) for i, span in enumerate(spans)]
            scores += [[x[:, :128] for x in s], [x[:, 128:] for x in s]]
        probs = []
        for s in scores:
            s = jnp.concatenate([jnp.where(valid, x * (128 ** (-0.5) * LOG2E), -jnp.inf) for x in s])
            probs.append(jnp.exp2(s - jnp.max(s, axis=1, keepdims=True)).astype(BF16))
        for h, p in zip(range(four, four + 4), probs):
            at = slice(128 * h, 128 * h + 128)
            right = jnp.concatenate([values(at), ones], axis=1)
            both = jnp.concatenate([nn(p[i * half : (i + 1) * half], right[span]) for i, span in enumerate(spans)])
            out_ref[:, at] = both[:, :128] / both[:, 128:]


def window_masks():
    seen = iota((WINDOW, 2 * WINDOW), 1)
    mine = iota((WINDOW, 2 * WINDOW), 0)
    return (seen > mine) & (seen <= mine + WINDOW), seen >= WINDOW


def window_kernel(wq_ref, wk_ref, v_ref, after_ref, win_ref):
    valid, _ = window_masks()
    windowed(wq_ref.at[pl.ds(WINDOW, win_ref.shape[0])], lambda at: wk_ref[:, at], lambda at: v_ref[:, at], valid, win_ref)


def early_kernel(place_ref, wq_ref, wk_ref, v_ref, halo_ref, after_ref, win_ref):
    valid, own = window_masks()
    valid = valid & (own | ((place_ref[0]) > 0))
    keys = lambda at: jnp.concatenate([halo_ref[:WINDOW, at], wk_ref[:WINDOW, at]])
    values = lambda at: jnp.concatenate([halo_ref[WINDOW:, at], v_ref[:WINDOW, at]])
    windowed(wq_ref.at[pl.ds(0, WINDOW)], keys, values, valid, win_ref)


def block_kernel(q_ref, turned_ref, v_ref, w_ref, cum_ref, after_ref, num_ref, den_ref, token_ref):
    rows, wide = q_ref.shape
    heads = cum_ref.shape[0]
    width = wide // heads
    q = q_ref[...]
    cum_row = cum_ref[...] * LOG2E
    cum_col = cum_row.T
    token_ref[...] = jnp.zeros(token_ref.shape, F32)
    step, piece = 256, 128
    ones = jnp.ones((rows, 128), BF16)
    causal = iota((piece, piece), 0) >= iota((piece, piece), 1)
    for h in range(heads):
        at = slice(128 * h, 128 * h + 128)
        mine = (turned_ref[h * width : (h + 1) * width] * width ** (-0.5)).astype(BF16)
        pieces = [jnp.zeros((h * width, rows), BF16), mine, jnp.zeros((wide - (h + 1) * width, rows), BF16)]
        k_here = jnp.concatenate([x for x in pieces if x.shape[0]])
        v = v_ref[:, at].astype(F32)
        w = w_ref[:, at]
        conv = w[0:1] * v + w[1:2] * shifted(v, 1) + w[2:3] * shifted(v, 2)
        right = jnp.concatenate([conv.astype(BF16), ones], axis=1)
        column = jnp.broadcast_to(cum_col[:, h : h + 1] - 1.0, (rows, piece))
        total = None
        for low in range(0, rows, step):
            x = nn(q[low:], k_here[:, low : low + step])
            lines = []
            for i in range(low, rows, piece):
                line = []
                for j in range(low, low + step, piece):
                    if j > i:
                        line.append(jnp.zeros((piece, piece), BF16))
                        continue
                    here = x[i - low : i - low + piece, j - low : j - low + piece]
                    gap = column[i : i + piece] - cum_row[h : h + 1, j : j + piece]
                    if i == j:
                        gap = jnp.where(causal, gap, -jnp.inf)
                    here = here + 1.0
                    line.append(((here * here + 1.0) * jnp.exp2(gap)).astype(BF16))
                lines.append(jnp.concatenate(line, axis=1))
            both = nn(jnp.concatenate(lines), right[low : low + step])
            total = both if total is None else jnp.concatenate([total[:low], total[low:] + both])
        num_ref[:, at] = total[:, :128]
        den_ref[:, at] = total[:, 128:]


def query_kernel(q_ref, k_ref, cum_ref, pick_ref, after_ref, out_ref, token_ref):
    rows, wide = q_ref.shape
    heads = cum_ref.shape[0]
    width = wide // heads
    q = q_ref[...]
    turned = q.astype(F32).T
    token_ref[...] = jnp.zeros(token_ref.shape, F32)
    pick = pick_ref[...]
    keys = k_ref[0:16].astype(F32)[0:8] * width ** (-0.5)
    line = iota((2 * heads, wide), 0)
    lane = iota((2 * heads, wide), 1)
    keys = jnp.where(line < heads, keys[0:1], keys[1:2])
    low = jnp.where(line < heads, line, line - heads) * width
    x = nt(jnp.where((lane >= low) & (lane < low + width), keys, 0.0).astype(BF16), q)
    x = (0.5 * x + 1.0) * x + 1.0
    sub = iota((16, rows), 0)
    at = iota((1, rows), 1)
    for h in range(heads):
        cum = cum_ref[h : h + 1, :]
        enter = jnp.exp(cum)
        score0 = x[h : h + 1] * jnp.exp(cum - cum[:, 0:1])
        score1 = x[heads + h : heads + h + 1] * jnp.exp(jnp.where(at < 1, -jnp.inf, cum - cum[:, 1:2]))
        rest = jnp.where(sub == 0, enter, jnp.where(sub == 1, score0, jnp.where(sub == 2, score1, 0.0)))
        phi = jnp.concatenate(products(turned[h * width : (h + 1) * width], enter) + [rest]).astype(BF16)
        out_ref[h, :, 0:ROWS] = nn(pick, phi).astype(BF16).T


def finish_kernel(place_ref, phi_ref, x0, x1, x2, x3, num_ref, den_ref, win_ref, early_ref, out_far, held, out_ref, sems):
    group = (place_ref[0] & 3)
    heads = phi_ref.shape[0]
    count = x0.shape[0]
    for distance, ref in enumerate((x0, x1, x2, x3)):
        held[group ^ distance] = ref[...]
    tiles = [held[h // count, h % count] for h in range(heads)]
    lines = []
    for tile in tiles:
        tail = tile[ROWS - 16 :].astype(F32)[8:]
        lines.append(jnp.concatenate([tail[1:2] + tail[3:4], tail[2:3] + tail[4:5]], axis=1))
    norms = jnp.concatenate(lines).T
    copies = []
    for h in range(heads):
        at = slice(128 * h, 128 * h + 128)
        norm = jnp.broadcast_to(norms[:ROWS, h : h + 1], (ROWS, 128)).astype(BF16)
        both = nn(phi_ref[h][:, :ROWS], jnp.concatenate([tiles[h], norm], axis=1))
        out = (num_ref[:, at] + both[:, :128]) / (den_ref[:, at] + both[:, 128:])
        out = out + jnp.concatenate([early_ref[:, at], win_ref[:, at]])
        out_ref[h] = out.astype(BF16)
        copies.append(pltpu.make_async_copy(out_ref.at[h], out_far.at[:, pl.ds(128 * h, 128)], sems.at[h]))
        copies[-1].start()
    for copy in copies:
        copy.wait()


def call(kernel, inputs, outs, scratch=(), smem=(), free=(), far=(), name=None, us=1.0, out_space=pltpu.VMEM):
    def space(i):
        return pltpu.SMEM if i in smem else pl.ANY if i in free else pltpu.HBM if i in far else pltpu.VMEM

    return pl.pallas_call(
        kernel,
        out_shape=outs,
        in_specs=[pl.BlockSpec(memory_space=space(i)) for i in range(len(inputs))],
        out_specs=jax.tree.map(lambda _: pl.BlockSpec(memory_space=out_space), outs),
        scratch_shapes=scratch,
        compiler_params=pltpu.CompilerParams(vmem_limit_bytes=VMEM_LIMIT),
        name=name,
        cost_estimate=pl.CostEstimate(flops=int(us * 3e9), bytes_accessed=int(us * 9e6), transcendentals=0),
    )(*inputs)


def local(count, q_feat, k_feat, values, win_query, win_key, log_gates, conv_weight):
    rows = values.shape[0]
    heads = log_gates.shape[1]
    width = q_feat.shape[1] // heads
    quarter = heads // 4
    position = lax.axis_index("seq")
    one = lambda number: jnp.reshape(number, (1,)).astype(jnp.int32)
    place = one(position)
    tables = key_tables(width)
    pick_keys, pick_queries = picks(width)
    shape = jax.ShapeDtypeStruct((quarter, ROWS, 128), BF16)
    wide = lambda *dims: jax.ShapeDtypeStruct(dims, F32)
    held = pltpu.VMEM((4, quarter, ROWS, 128), BF16)

    def swap(x, distance):
        return lax.ppermute(x, "seq", [(i, i ^ distance) for i in range(count)])

    token = call(open_kernel, (place,), wide(8, 128), smem=(0,), name="open", us=6.0)
    cum, turned = call(
        gate_kernel,
        (log_gates.T, k_feat, token),
        [wide(heads, rows), wide(k_feat.shape[1], rows)],
        free=(2,),
        name="gates",
        us=0.01,
    )

    def states(order, after, name, us):
        return call(
            lambda *refs: state_kernel(order, *refs),
            (place, k_feat, turned, values, cum, conv_weight, pick_keys, after),
            [shape] * len(order),
            smem=(0,),
            free=(7,),
            name=name,
            us=us,
        )

    made = {}
    after = cum
    for number, order in enumerate(((3,), (1, 2))):
        made.update(zip(order, states(order, after, f"states{number}", 0.3 + 0.5 * len(order))))
        after = made[order[0]]
    sent = [made[d] for d in (1, 2, 3)]
    others = [swap(x, d) for d, x in zip((1, 2, 3), sent)]
    (own,) = call(
        lambda *refs: state_kernel((0,), *refs),
        (place, k_feat, turned, values, cum, conv_weight, pick_keys, after),
        [shape],
        smem=(0,),
        free=(7,),
        name="own_states",
        us=0.8,
    )
    num, den, token = call(
        block_kernel,
        (q_feat, turned, values, conv_weight, cum, own),
        [wide(*values.shape)] * 2 + [wide(8, 128)],
        free=(5,),
        name="block",
        us=2.7,
    )
    total, before, keys, small = call(
        lambda *refs: group_kernel(width, *refs),
        (place, conv_weight, *tables, own, *others, token),
        [shape, wide(3, quarter, ROWS, 128), wide(2, quarter, ROWS, 128), wide(quarter, 8, 128)],
        [held],
        smem=(0,),
        free=(8,),
        name="merge_group",
        us=2.0,
    )
    base = jnp.zeros_like(total)
    live = position < 0
    distance = 4
    last = total
    while distance < count:
        got = swap(total, distance)
        upper = (position & distance) > 0

        def pair(left, right):
            return call(
                lambda *refs: pair_kernel(width, *refs),
                (place, conv_weight, *tables, left, right),
                shape,
                smem=(0,),
                name="merge_pair",
            )

        if distance == 4:
            base = got
        else:
            base = jnp.where(upper, jnp.where(live, pair(got, base), got), base)
        live = live | upper
        if 2 * distance < count:
            total = pair(jnp.where(upper, got, total), jnp.where(upper, total, got))
        distance *= 2
    edge = call(
        edge_kernel,
        (win_key, values, last),
        jax.ShapeDtypeStruct((2 * WINDOW, values.shape[1]), BF16),
        free=(2,),
        name="edge",
        us=0.2,
    )
    halo = lax.ppermute(edge, "seq", [(i, i + 1) for i in range(count - 1)])

    here, *sent = call(
        spread_kernel,
        (place, conv_weight, base, before, keys, small, edge),
        [shape] * 4,
        [held],
        smem=(0,),
        free=(6,),
        name="spread",
        us=1.0,
    )
    prefixes = [here] + [swap(x, d) for d, x in zip((1, 2, 3), sent)]
    phi, token = call(
        query_kernel,
        (q_feat, k_feat, cum, pick_queries, here),
        [jax.ShapeDtypeStruct((heads, rows, 256), BF16), wide(8, 128)],
        free=(4,),
        name="query_features",
        us=1.5,
    )
    win = call(
        window_kernel,
        (win_query, win_key, values, token),
        wide(rows - WINDOW, values.shape[1]),
        free=(3,),
        name="window",
        us=2.0,
    )
    early = call(
        early_kernel,
        (place, win_query, win_key, values, halo, win),
        wide(WINDOW, values.shape[1]),
        smem=(0,),
        free=(5,),
        name="window_first",
        us=0.4,
    )
    return call(
        finish_kernel,
        (place, phi, *prefixes, num, den, win, early),
        jax.ShapeDtypeStruct(values.shape, BF16),
        [held, pltpu.VMEM((heads, rows, 128), BF16), pltpu.SemaphoreType.DMA((heads,))],
        smem=(0,),
        out_space=pltpu.HBM,
        name="finish",
        us=2.1,
    )


def solution(mesh):
    rows = P(("grp", "seq"), "head")
    count = mesh.shape["seq"]
    return jax.shard_map(
        lambda *args: local(count, *args),
        mesh=mesh,
        in_specs=(rows,) * 6 + (P(None, "head"),),
        out_specs=rows,
        check_vma=False,
    )
```

```python
import numpy as np
import jax
import jax.numpy as jnp
from jax import lax
from jax.experimental import pallas as pl
from jax.experimental.pallas import tpu as pltpu
from jax.sharding import PartitionSpec as P

WINDOW = 64
PARTS = 2
ROWS = 160
EDGE = 158
LOG2E = float(np.log2(np.e))
F32 = jnp.float32
BF16 = jnp.bfloat16
VMEM_LIMIT = 24 * 1024 * 1024


def feature_tables(width):
    first = -np.ones(ROWS, np.int32)
    second = -np.ones(ROWS, np.int32)
    scale = np.zeros(ROWS, np.float32)
    twice = np.ones(ROWS, np.float32)
    scale[0] = 1.0
    at = 1
    for i in range(width):
        first[at], scale[at] = i, width ** (-0.25)
        at += 1
    for i in range(width):
        for j in range(i, width):
            first[at], second[at], scale[at] = i, j, (2.0 * width) ** (-0.5)
            twice[at] = 1.0 if i == j else 2.0
            at += 1
    one_a = ((first < 0) & (scale > 0)).astype(np.float32)
    one_b = ((second < 0) & (scale > 0)).astype(np.float32)
    return first, second, one_a, one_b, scale, twice


def key_tables(width):
    first, second, one_a, one_b, scale, _ = feature_tables(width)
    pick = np.zeros((2, 2, ROWS, 128), np.float32)
    for token in range(2):
        for factor, index in enumerate((first, second)):
            for row in range(ROWS):
                if index[row] >= 0:
                    pick[token, factor, row, token * width + index[row]] = 1.0
    real = np.stack([np.repeat(x[:, None], 8, axis=1) for x in (one_a, one_b, scale)])
    return jnp.asarray(pick.reshape(4 * ROWS, 128), BF16), jnp.asarray(real, F32)


def wide_rows(width):
    half = width // 2
    pair = lambda i, j: i * width + j if i < half else half * width + (i - half) * half + j - half
    linear = half * width + half * half
    return pair, linear, linear + width


def picks(width):
    first, second, _, _, _, twice = feature_tables(width)
    pair, linear, constant = wide_rows(width)
    keys = np.zeros((ROWS, constant + 16), np.float32)
    keys[0, constant] = 1.0
    for row in range(1, ROWS):
        if second[row] >= 0:
            keys[row, pair(first[row], second[row])] = 1.0
        elif first[row] >= 0:
            keys[row, linear + first[row]] = 1.0
    queries = keys * twice[:, None]
    queries[EDGE, constant + 1] = 1.0
    queries[EDGE + 1, constant + 2] = 1.0
    keys = np.concatenate([keys, np.zeros((256 - ROWS, keys.shape[1]), np.float32)])
    return jnp.asarray(keys, BF16), jnp.asarray(queries, BF16)


def products(x, factor):
    width = x.shape[0]
    half = width // 2
    scaled = x * (factor * (2.0 * width) ** (-0.5))
    blocks = [x * scaled[i : i + 1] for i in range(half)]
    blocks += [x[half:] * scaled[i : i + 1] for i in range(half, width)]
    return blocks + [x * (factor * width ** (-0.25))]


def nt(a, b):
    return lax.dot_general(a, b, (((1,), (1,)), ((), ())), preferred_element_type=F32)


def nn(a, b):
    return lax.dot_general(a, b, (((1,), (0,)), ((), ())), preferred_element_type=F32)


def tn(a, b):
    return lax.dot_general(a, b, (((0,), (0,)), ((), ())), preferred_element_type=F32)


def parts(wide):
    upper = wide.astype(BF16)
    rest = wide - upper.astype(F32)
    middle = rest.astype(BF16)
    lower = (rest - middle.astype(F32)).astype(BF16)
    return upper, middle, lower


def iota(shape, dim):
    return lax.broadcasted_iota(jnp.int32, shape, dim)


def cumulative_rows(gates):
    heads, rows = gates.shape
    upto = (iota((128, 128), 0) <= iota((128, 128), 1)).astype(BF16)
    blocks = [gates[:, i : i + 128] for i in range(0, rows, 128)]
    stacked = jnp.concatenate([piece for block in blocks for piece in parts(block)], axis=0)
    inside = nn(stacked, upto)
    done, before = [], 0.0
    for i in range(len(blocks)):
        three = [inside[(3 * i + p) * heads : (3 * i + p + 1) * heads] for p in range(3)]
        done.append(three[0] + three[1] + three[2] + before)
        before = done[-1][:, 127:]
    return jnp.concatenate(done, axis=1)


def shifted(x, by):
    return jnp.where(iota(x.shape, 0) < by, 0.0, pltpu.roll(x, by, 0))


def quarter_states(quarter, out_ref, k_ref, turned_ref, v_ref, w_ref, cum_ref, pick):
    rows, wide = k_ref.shape
    heads = cum_ref.shape[0]
    width = wide // heads
    count = out_ref.shape[0]
    lane1 = iota((1, 128), 1)
    sub = iota((8, 128), 0)
    keys8 = k_ref[0:16].astype(F32)[0:8]
    wides, norms, values, keeps, lasts = [], [], [], [], []
    for j in range(count):
        head = quarter * count + j
        at = pl.ds(pl.multiple_of(head * 128, 128), 128)
        cum = cum_ref[pl.ds(head, 1), :]
        last = cum[:, rows - 1 :]
        keep = jnp.exp(last - cum)
        k = turned_ref[pl.ds(pl.multiple_of(head * width, width), width), :]
        constant = jnp.where(iota((16, rows), 0) == 0, keep, 0.0)
        phi = jnp.concatenate(products(k, keep) + [constant]).astype(BF16)
        v = v_ref[:, at].astype(F32)
        w = w_ref[:, at]
        conv = (w[0:1] * v + w[1:2] * shifted(v, 1) + w[2:3] * shifted(v, 2)).astype(BF16)
        wides.append(nn(phi, conv).astype(BF16))
        norms.append(nt(jnp.ones((8, rows), BF16), phi))
        values.append(v)
        keeps.append(keep)
        lasts.append(last)
    states = nn(pick[:ROWS], jnp.concatenate(wides, axis=1))
    line = iota(norms[0].shape, 0)
    mixed = jnp.zeros(norms[0].shape, F32)
    for j, norm in enumerate(norms):
        high = norm.astype(BF16).astype(F32)
        mixed = jnp.where(line == 2 * j, high, jnp.where(line == 2 * j + 1, norm - high, mixed))
    norm = nt(mixed.astype(BF16), pick)
    for j in range(count):
        head = quarter * count + j
        high, low = norm[2 * j : 2 * j + 1], norm[2 * j + 1 : 2 * j + 2]
        turned = pltpu.roll(keys8, (wide - head * width) % wide, 1)
        turned2 = pltpu.roll(keys8, (wide - head * width + width) % wide, 1)
        misc = jnp.where(lane1 < width, turned[0:1], 0.0)
        misc = jnp.where((lane1 >= width) & (lane1 < 2 * width), turned2[1:2], misc)
        place = 2 * width
        for value in (keeps[j][:, 0:1], keeps[j][:, 1:2], jnp.exp(lasts[j])):
            for piece in parts(value):
                misc = jnp.where(lane1 == place, piece.astype(F32), misc)
                place += 1
        state = states[:, 128 * j : 128 * j + 128]
        tail = state[ROWS - 8 :]
        for row, text in enumerate((high[:, :128], high[:, 128:], low[:, :128], low[:, 128:], misc)):
            tail = jnp.where(sub == row + 1, text, tail)
        tail = jnp.where(sub >= 6, values[j][rows - 8 :], tail)
        out_ref[j, 0 : ROWS - 16, :] = state[: ROWS - 16].astype(BF16)
        out_ref[j, ROWS - 16 :, :] = jnp.concatenate([state[ROWS - 16 : ROWS - 8], tail]).astype(BF16)


def open_kernel(place_ref, token_ref):
    token_ref[...] = jnp.zeros(token_ref.shape, F32)


def gate_kernel(g_ref, k_ref, after_ref, cum_ref, turned_ref):
    cum_ref[...] = cumulative_rows(g_ref[...])
    turned_ref[...] = k_ref[...].astype(F32).T


def state_kernel(order, place_ref, k_ref, turned_ref, v_ref, cum_ref, w_ref, pick_ref, after_ref, *outs):
    pick = pick_ref[...]
    for out_ref, distance in zip(outs, order):
        quarter = (place_ref[0] & 3) ^ distance
        quarter_states(quarter, out_ref, k_ref, turned_ref, v_ref, w_ref, cum_ref, pick)


def edge_kernel(win_key_ref, v_ref, after_ref, edge_ref):
    edge_ref[:WINDOW] = win_key_ref[win_key_ref.shape[0] - WINDOW :]
    edge_ref[WINDOW:] = v_ref[v_ref.shape[0] - WINDOW :]


def tail_of(tile):
    return tile[ROWS - 8 :]


def value_of(tile, i, width):
    lane1 = iota((1, 128), 1)
    place = 2 * width + 3 * i
    here = (lane1 >= place) & (lane1 < place + 3)
    return jnp.sum(jnp.where(here, tail_of(tile)[5:6], 0.0), axis=1, keepdims=True)


def first_keys(tiles, pick_ref, real_ref):
    lines = [tail_of(tile)[5:6] for tile in tiles]
    rows = jnp.concatenate(lines + [jnp.zeros((8 - len(lines), 128), F32)] if len(lines) < 8 else lines).astype(BF16)
    found = nt(pick_ref[...], rows)
    factors = [found[i * ROWS : (i + 1) * ROWS] for i in range(4)]
    one_a, one_b, scale = (real_ref[i] for i in range(3))
    return [(factors[2 * t] + one_a) * (factors[2 * t + 1] + one_b) * scale for t in range(2)]


def carried(tile, w):
    tail = tail_of(tile)
    return w[1:2] * tail[7:8] + w[2:3] * tail[6:7], w[2:3] * tail[7:8]


def seam(left, columns, enter, w):
    carry0, carry1 = carried(left, w)
    return columns[0] * (enter[0] * carry0) + columns[1] * (enter[1] * carry1)


def merge(left, right, columns, w, width):
    decay = value_of(right, 2, width)
    joined = decay * left + right + seam(left, columns, (value_of(right, 0, width), value_of(right, 1, width)), w)
    sub = iota((8, 128), 0)
    lane1 = iota((1, 128), 1)
    misc = tail_of(left)[5:6]
    misc = jnp.where(lane1 < 2 * width, misc, misc * decay)
    tail = jnp.where(sub == 5, misc, tail_of(joined))
    tail = jnp.where(sub >= 6, tail_of(right), tail)
    return jnp.concatenate([joined[: ROWS - 8], tail])


def packed(tile, width):
    tail = tail_of(tile)
    sub = iota((8, 128), 0)
    lane1 = iota((1, 128), 1)
    misc = tail[5:6]
    fresh = jnp.where(lane1 < 2 * width, misc, 0.0)
    place = 2 * width
    for i in range(3):
        for piece in parts(value_of(tile, i, width)):
            fresh = jnp.where(lane1 == place, piece.astype(F32), fresh)
            place += 1
    tail = jnp.where(sub == 5, fresh, norm_parts(tail))
    return jnp.concatenate([tile[: ROWS - 8], tail]).astype(BF16)


def norm_parts(tail):
    sub = iota((8, 128), 0)
    for row in (1, 2):
        norm = tail[row : row + 1] + tail[row + 2 : row + 3]
        high = norm.astype(BF16).astype(F32)
        tail = jnp.where(sub == row, high, jnp.where(sub == row + 2, norm - high, tail))
    return tail


def head_taps(w_ref, head):
    return w_ref[:, pl.ds(pl.multiple_of(head * 128, 128), 128)]


def group_kernel(width, place_ref, w_ref, pick_ref, real_ref, x0, x1, x2, x3, after_ref, total_ref, before_ref, keys_ref, small_ref, held):
    group = (place_ref[0] & 3)
    count = x0.shape[0]
    for distance, ref in enumerate((x0, x1, x2, x3)):
        held[group ^ distance] = ref[...]
    tiles = [[held[p, j].astype(F32) for j in range(count)] for p in range(4)]
    columns = first_keys([tiles[p][j] for p in range(4) for j in range(count)], pick_ref, real_ref)
    sub = iota((8, 128), 0)
    for j in range(count):
        w = head_taps(w_ref, group * count + j)
        so_far = tiles[0][j]
        for p in range(1, 4):
            before_ref[p - 1, j] = so_far
            pick = p * count + j
            so_far = merge(so_far, tiles[p][j], [c[:, pick : pick + 1] for c in columns], w, width)
        total_ref[j] = packed(so_far, width)
        for token in range(2):
            keys_ref[token, j] = jnp.broadcast_to(columns[token][:, j : j + 1], (ROWS, 128))
        decays = [value_of(tiles[p][j], 2, width) for p in range(3)]
        small = jnp.zeros((8, 128), F32)
        lines = decays[0], value_of(tiles[0][j], 0, width), value_of(tiles[0][j], 1, width), decays[1], decays[1] * decays[2]
        for row, value in enumerate(lines):
            small = jnp.where(sub == row, value, small)
        small_ref[j] = small


def pair_kernel(width, place_ref, w_ref, pick_ref, real_ref, left_ref, right_ref, out_ref):
    count = left_ref.shape[0]
    rights = [right_ref[j].astype(F32) for j in range(count)]
    columns = first_keys(rights, pick_ref, real_ref)
    for j in range(count):
        w = head_taps(w_ref, (place_ref[0] & 3) * count + j)
        left = left_ref[j].astype(F32)
        out_ref[j] = packed(merge(left, rights[j], [c[:, j : j + 1] for c in columns], w, width), width)


def with_edge(tile, source, w):
    carry0, carry1 = carried(source, w)
    sub = iota((8, 128), 0)
    tail = norm_parts(tail_of(tile))
    tail = jnp.where(sub == 6, carry0, jnp.where(sub == 7, carry1, tail))
    return jnp.concatenate([tile[: ROWS - 8], tail]).astype(BF16)


def spread_kernel(place_ref, w_ref, base_ref, before_ref, keys_ref, small_ref, after_ref, o0, o1, o2, o3, held):
    group = (place_ref[0] & 3)
    live = place_ref[0] > 3
    count = base_ref.shape[0]
    for j in range(count):
        w = head_taps(w_ref, group * count + j)
        base = jnp.where(live, base_ref[j].astype(F32), 0.0)
        held[0, j] = with_edge(base, base, w)
        small = small_ref[j]
        through = small[0:1] * base + seam(base, (keys_ref[0, j], keys_ref[1, j]), (small[1:2], small[2:3]), w)
        for p in range(3):
            tile = before_ref[p, j] + (through if p == 0 else small[2 + p : 3 + p] * through)
            held[p + 1, j] = with_edge(tile, before_ref[p, j], w)
    for distance, ref in enumerate((o0, o1, o2, o3)):
        ref[...] = held[group ^ distance]


def windowed(wq_ref, keys, values, valid, out_ref):
    half = WINDOW
    rows = wq_ref.shape[0]
    steps = rows // half
    ones = jnp.ones((rows + half, 128), BF16)
    zeros = jnp.zeros((rows + half, 128), BF16)
    heads = wq_ref.shape[1] // 128
    spans = [slice(i * half, (i + 2) * half) for i in range(steps)]
    for four in range(0, heads, 4):
        scores = []
        for h in range(four, four + 4, 2):
            one, two = slice(128 * h, 128 * h + 128), slice(128 * h + 128, 128 * h + 256)
            upper = jnp.concatenate([keys(one), zeros], axis=1)
            lower = jnp.concatenate([zeros, keys(two)], axis=1)
            queries = wq_ref[:, 128 * h : 128 * h + 256]
            s = [nt(queries[i * half : (i + 1) * half], jnp.concatenate([upper[span], lower[span]])) for i, span in enumerate(spans)]
            scores += [[x[:, :128] for x in s], [x[:, 128:] for x in s]]
        probs = []
        for s in scores:
            s = jnp.concatenate([jnp.where(valid, x * (128 ** (-0.5) * LOG2E), -jnp.inf) for x in s])
            probs.append(jnp.exp2(s - jnp.max(s, axis=1, keepdims=True)).astype(BF16))
        for h, p in zip(range(four, four + 4), probs):
            at = slice(128 * h, 128 * h + 128)
            right = jnp.concatenate([values(at), ones], axis=1)
            both = jnp.concatenate([nn(p[i * half : (i + 1) * half], right[span]) for i, span in enumerate(spans)])
            out_ref[:, at] = both[:, :128] / both[:, 128:]


def window_masks():
    seen = iota((WINDOW, 2 * WINDOW), 1)
    mine = iota((WINDOW, 2 * WINDOW), 0)
    return (seen > mine) & (seen <= mine + WINDOW), seen >= WINDOW


def window_kernel(wq_ref, wk_ref, v_ref, after_ref, win_ref):
    valid, _ = window_masks()
    windowed(wq_ref.at[pl.ds(WINDOW, win_ref.shape[0])], lambda at: wk_ref[:, at], lambda at: v_ref[:, at], valid, win_ref)


def early_kernel(place_ref, wq_ref, wk_ref, v_ref, halo_ref, after_ref, win_ref):
    valid, own = window_masks()
    valid = valid & (own | ((place_ref[0]) > 0))
    keys = lambda at: jnp.concatenate([halo_ref[:WINDOW, at], wk_ref[:WINDOW, at]])
    values = lambda at: jnp.concatenate([halo_ref[WINDOW:, at], v_ref[:WINDOW, at]])
    windowed(wq_ref.at[pl.ds(0, WINDOW)], keys, values, valid, win_ref)


def block_kernel(q_ref, turned_ref, v_ref, w_ref, cum_ref, after_ref, num_ref, den_ref, token_ref):
    rows, wide = q_ref.shape
    heads = cum_ref.shape[0]
    width = wide // heads
    q = q_ref[...]
    cum_row = cum_ref[...] * LOG2E
    cum_col = cum_row.T
    token_ref[...] = jnp.zeros(token_ref.shape, F32)
    step, piece = 256, 128
    ones = jnp.ones((rows, 128), BF16)
    causal = iota((piece, piece), 0) >= iota((piece, piece), 1)
    for h in range(heads):
        at = slice(128 * h, 128 * h + 128)
        mine = (turned_ref[h * width : (h + 1) * width] * width ** (-0.5)).astype(BF16)
        pieces = [jnp.zeros((h * width, rows), BF16), mine, jnp.zeros((wide - (h + 1) * width, rows), BF16)]
        k_here = jnp.concatenate([x for x in pieces if x.shape[0]])
        v = v_ref[:, at].astype(F32)
        w = w_ref[:, at]
        conv = w[0:1] * v + w[1:2] * shifted(v, 1) + w[2:3] * shifted(v, 2)
        right = jnp.concatenate([conv.astype(BF16), ones], axis=1)
        column = jnp.broadcast_to(cum_col[:, h : h + 1] - 1.0, (rows, piece))
        total = None
        for low in range(0, rows, step):
            x = nn(q[low:], k_here[:, low : low + step])
            lines = []
            for i in range(low, rows, piece):
                line = []
                for j in range(low, low + step, piece):
                    if j > i:
                        line.append(jnp.zeros((piece, piece), BF16))
                        continue
                    here = x[i - low : i - low + piece, j - low : j - low + piece]
                    gap = column[i : i + piece] - cum_row[h : h + 1, j : j + piece]
                    if i == j:
                        gap = jnp.where(causal, gap, -jnp.inf)
                    here = here + 1.0
                    line.append(((here * here + 1.0) * jnp.exp2(gap)).astype(BF16))
                lines.append(jnp.concatenate(line, axis=1))
            both = nn(jnp.concatenate(lines), right[low : low + step])
            total = both if total is None else jnp.concatenate([total[:low], total[low:] + both])
        num_ref[:, at] = total[:, :128]
        den_ref[:, at] = total[:, 128:]


def query_kernel(q_ref, k_ref, cum_ref, pick_ref, after_ref, out_ref, token_ref):
    rows, wide = q_ref.shape
    heads = cum_ref.shape[0]
    width = wide // heads
    q = q_ref[...]
    turned = q.astype(F32).T
    token_ref[...] = jnp.zeros(token_ref.shape, F32)
    pick = pick_ref[...]
    keys = k_ref[0:16].astype(F32)[0:8] * width ** (-0.5)
    line = iota((2 * heads, wide), 0)
    lane = iota((2 * heads, wide), 1)
    keys = jnp.where(line < heads, keys[0:1], keys[1:2])
    low = jnp.where(line < heads, line, line - heads) * width
    x = nt(jnp.where((lane >= low) & (lane < low + width), keys, 0.0).astype(BF16), q)
    x = (0.5 * x + 1.0) * x + 1.0
    sub = iota((16, rows), 0)
    at = iota((1, rows), 1)
    for h in range(heads):
        cum = cum_ref[h : h + 1, :]
        enter = jnp.exp(cum)
        score0 = x[h : h + 1] * jnp.exp(cum - cum[:, 0:1])
        score1 = x[heads + h : heads + h + 1] * jnp.exp(jnp.where(at < 1, -jnp.inf, cum - cum[:, 1:2]))
        rest = jnp.where(sub == 0, enter, jnp.where(sub == 1, score0, jnp.where(sub == 2, score1, 0.0)))
        phi = jnp.concatenate(products(turned[h * width : (h + 1) * width], enter) + [rest]).astype(BF16)
        out_ref[h, :, 0:ROWS] = nn(pick, phi).astype(BF16).T


def finish_kernel(place_ref, phi_ref, x0, x1, x2, x3, num_ref, den_ref, win_ref, early_ref, out_far, held, out_ref, sems):
    group = (place_ref[0] & 3)
    heads = phi_ref.shape[0]
    count = x0.shape[0]
    for distance, ref in enumerate((x0, x1, x2, x3)):
        held[group ^ distance] = ref[...]
    tiles = [held[h // count, h % count] for h in range(heads)]
    lines = []
    for tile in tiles:
        tail = tile[ROWS - 16 :].astype(F32)[8:]
        lines.append(jnp.concatenate([tail[1:2] + tail[3:4], tail[2:3] + tail[4:5]], axis=1))
    norms = jnp.concatenate(lines).T
    rights = []
    for h in range(heads):
        norm = jnp.broadcast_to(norms[:ROWS, h : h + 1], (ROWS, 128)).astype(BF16)
        rights.append(jnp.concatenate([tiles[h], norm], axis=1))
    copies = []
    rows = phi_ref.shape[1]
    for low in range(0, rows, rows // PARTS):
        here = slice(low, low + rows // PARTS)
        for h in range(heads):
            at = slice(128 * h, 128 * h + 128)
            both = nn(phi_ref[h, here][:, :ROWS], rights[h])
            out = (num_ref[here, at] + both[:, :128]) / (den_ref[here, at] + both[:, 128:])
            if low:
                out = out + win_ref[low - WINDOW : low - WINDOW + rows // PARTS, at]
            else:
                out = out + jnp.concatenate([early_ref[:, at], win_ref[: rows // PARTS - WINDOW, at]])
            out_ref[here, at] = out.astype(BF16)
        copies.append(pltpu.make_async_copy(out_ref.at[pl.ds(low, rows // PARTS)], out_far.at[pl.ds(low, rows // PARTS)], sems.at[len(copies)]))
        copies[-1].start()
    for copy in copies:
        copy.wait()


def call(kernel, inputs, outs, scratch=(), smem=(), free=(), far=(), name=None, us=1.0, out_space=pltpu.VMEM):
    def space(i):
        return pltpu.SMEM if i in smem else pl.ANY if i in free else pltpu.HBM if i in far else pltpu.VMEM

    return pl.pallas_call(
        kernel,
        out_shape=outs,
        in_specs=[pl.BlockSpec(memory_space=space(i)) for i in range(len(inputs))],
        out_specs=jax.tree.map(lambda _: pl.BlockSpec(memory_space=out_space), outs),
        scratch_shapes=scratch,
        compiler_params=pltpu.CompilerParams(vmem_limit_bytes=VMEM_LIMIT),
        name=name,
        cost_estimate=pl.CostEstimate(flops=int(us * 3e9), bytes_accessed=int(us * 9e6), transcendentals=0),
    )(*inputs)


def local(count, q_feat, k_feat, values, win_query, win_key, log_gates, conv_weight):
    rows = values.shape[0]
    heads = log_gates.shape[1]
    width = q_feat.shape[1] // heads
    quarter = heads // 4
    position = lax.axis_index("seq")
    one = lambda number: jnp.reshape(number, (1,)).astype(jnp.int32)
    place = one(position)
    tables = key_tables(width)
    pick_keys, pick_queries = picks(width)
    shape = jax.ShapeDtypeStruct((quarter, ROWS, 128), BF16)
    wide = lambda *dims: jax.ShapeDtypeStruct(dims, F32)
    held = pltpu.VMEM((4, quarter, ROWS, 128), BF16)

    def swap(x, distance):
        return lax.ppermute(x, "seq", [(i, i ^ distance) for i in range(count)])

    token = call(open_kernel, (place,), wide(8, 128), smem=(0,), name="open", us=6.0)
    cum, turned = call(
        gate_kernel,
        (log_gates.T, k_feat, token),
        [wide(heads, rows), wide(k_feat.shape[1], rows)],
        free=(2,),
        name="gates",
        us=0.01,
    )

    def states(order, after, name, us):
        return call(
            lambda *refs: state_kernel(order, *refs),
            (place, k_feat, turned, values, cum, conv_weight, pick_keys, after),
            [shape] * len(order),
            smem=(0,),
            free=(7,),
            name=name,
            us=us,
        )

    made = {}
    after = cum
    for number, order in enumerate(((3,), (1, 2))):
        made.update(zip(order, states(order, after, f"states{number}", 0.3 + 0.5 * len(order))))
        after = made[order[0]]
    sent = [made[d] for d in (1, 2, 3)]
    others = [swap(x, d) for d, x in zip((1, 2, 3), sent)]
    (own,) = call(
        lambda *refs: state_kernel((0,), *refs),
        (place, k_feat, turned, values, cum, conv_weight, pick_keys, after),
        [shape],
        smem=(0,),
        free=(7,),
        name="own_states",
        us=0.8,
    )
    num, den, token = call(
        block_kernel,
        (q_feat, turned, values, conv_weight, cum, own),
        [wide(*values.shape)] * 2 + [wide(8, 128)],
        free=(5,),
        name="block",
        us=2.7,
    )
    total, before, keys, small = call(
        lambda *refs: group_kernel(width, *refs),
        (place, conv_weight, *tables, own, *others, token),
        [shape, wide(3, quarter, ROWS, 128), wide(2, quarter, ROWS, 128), wide(quarter, 8, 128)],
        [held],
        smem=(0,),
        free=(8,),
        name="merge_group",
        us=2.0,
    )
    base = jnp.zeros_like(total)
    live = position < 0
    distance = 4
    last = total
    while distance < count:
        got = swap(total, distance)
        upper = (position & distance) > 0

        def pair(left, right):
            return call(
                lambda *refs: pair_kernel(width, *refs),
                (place, conv_weight, *tables, left, right),
                shape,
                smem=(0,),
                name="merge_pair",
            )

        if distance == 4:
            base = got
        else:
            base = jnp.where(upper, jnp.where(live, pair(got, base), got), base)
        live = live | upper
        if 2 * distance < count:
            total = pair(jnp.where(upper, got, total), jnp.where(upper, total, got))
        distance *= 2
    edge = call(
        edge_kernel,
        (win_key, values, last),
        jax.ShapeDtypeStruct((2 * WINDOW, values.shape[1]), BF16),
        free=(2,),
        name="edge",
        us=0.2,
    )
    halo = lax.ppermute(edge, "seq", [(i, i + 1) for i in range(count - 1)])

    here, *sent = call(
        spread_kernel,
        (place, conv_weight, base, before, keys, small, edge),
        [shape] * 4,
        [held],
        smem=(0,),
        free=(6,),
        name="spread",
        us=1.0,
    )
    prefixes = [here] + [swap(x, d) for d, x in zip((1, 2, 3), sent)]
    phi, token = call(
        query_kernel,
        (q_feat, k_feat, cum, pick_queries, here),
        [jax.ShapeDtypeStruct((heads, rows, 256), BF16), wide(8, 128)],
        free=(4,),
        name="query_features",
        us=1.5,
    )
    win = call(
        window_kernel,
        (win_query, win_key, values, token),
        wide(rows - WINDOW, values.shape[1]),
        free=(3,),
        name="window",
        us=2.0,
    )
    early = call(
        early_kernel,
        (place, win_query, win_key, values, halo, win),
        wide(WINDOW, values.shape[1]),
        smem=(0,),
        free=(5,),
        name="window_first",
        us=0.4,
    )
    return call(
        finish_kernel,
        (place, phi, *prefixes, num, den, win, early),
        jax.ShapeDtypeStruct(values.shape, BF16),
        [held, pltpu.VMEM(values.shape, BF16), pltpu.SemaphoreType.DMA((PARTS,))],
        smem=(0,),
        out_space=pltpu.HBM,
        name="finish",
        us=2.1,
    )


def solution(mesh):
    rows = P(("grp", "seq"), "head")
    count = mesh.shape["seq"]
    return jax.shard_map(
        lambda *args: local(count, *args),
        mesh=mesh,
        in_specs=(rows,) * 6 + (P(None, "head"),),
        out_specs=rows,
        check_vma=False,
    )
```
